256 devices in a mesh: section: 4 (over x_hi, core), seq: 64 (over y, x_lo, z).
Axes of the slice: x: 4 (x_hi: 2, x_lo: 2; x = x_hi * 2 + x_lo), y: 4, z: 8, core: 2. Of those that a mesh axis runs over, the one named last changes fastest.
Arguments:
- hidden: bfloat16 [32768, 4096], P(('seq', 'section')), may hold values from -6 to 6
- norm_gain: float32 [4096], replicated, may hold values from 0.1 to 1.9
- w_query: bfloat16 [4096, 4096], P('seq', 'section'), may hold values from -0.09375 to 0.09375
- w_keyval: bfloat16 [2, 896, 4096], P(None, None, 'section'), may hold values from -120 to 120
- nbr_states: bfloat16 [512, 256, 896], P('seq'), may hold values from -24 to 24
- nbr_lens: int32 [512, 2], replicated, may hold values from 32 to 128
- segment_ids: int32 [32768], replicated, may hold values from 0 to 63, never falling along the last dimension, each value on 1 to 16384 neighbouring positions
Outputs:
- context: bfloat16 [32768, 4096], P('seq', 'section')
The draws below stay inside these ranges and needn't reach their ends.
All inputs are finite; a program needn't handle non-finite values.
Results may differ from the reference program's by a relative error of at most 0.017.
The reference program's roundings to bfloat16 on the way (of `normed`, `query`, `keys` and `weights`) count: a program that leaves them out, or rounds other values in their place, can miss the bound.
Values may be sent and summed in bfloat16 or wider, within the bound.
No kernel may reach another device: no remote copies, remote signals or barrier semaphores. Data moves between devices by JAX's collectives and lax.ppermute only.
A program may use at most 128 MiB of HBM per device.

```python
import math
import jax
import jax.numpy as jnp
import numpy as np
from jax import lax

D = 4096
HEADS = 32
HEAD_DIM = 128
ENC_DIM = 896
SPAN = 64
NBR_LEN = 128
NEIGHBOURS = 2
TOKENS = 32768
SPANS = 512


def draw_w_keyval(key, part):
    key = jax.random.fold_in(key, 23)
    shape = (2, ENC_DIM, HEADS * HEAD_DIM)
    base = jax.random.truncated_normal(key, -6.0, 6.0, shape, jnp.float32) * ENC_DIM ** (-0.5)
    return base.astype(jnp.bfloat16)


def draw_nbr_states(key, part):
    key = jax.random.fold_in(key, 11)
    rows = NEIGHBOURS * NBR_LEN
    shape = (SPANS, rows, ENC_DIM)
    first = jax.random.fold_in(key, 0)
    return jax.random.truncated_normal(first, -6.0, 6.0, shape, jnp.float32).astype(jnp.bfloat16)


def touch_ends(drawn, rng, smallest, top_value):
    index_at = [jax.random.randint(jax.random.fold_in(rng, axis), (), 0, length) for axis, length in enumerate(drawn.shape)]
    main_axis = drawn.shape.index(max(drawn.shape))
    neighbour = index_at[:main_axis] + [(index_at[main_axis] + 1) % drawn.shape[main_axis]] + index_at[main_axis + 1:]
    return drawn.at[tuple(index_at)].set(smallest).at[tuple(neighbour)].set(top_value)


def levels(own_key, extent, cuts, low, largest):
    factor_of, own = 1.0, jax.random.fold_in(own_key, 6)
    for axis_at, blocks in cuts:
        steps = jnp.exp(jax.random.uniform(jax.random.fold_in(own, axis_at), (blocks,), jnp.float32, low / len(cuts), largest / len(cuts)))
        factor_of = factor_of * jnp.repeat(steps, extent[axis_at] // blocks).reshape([-1 if axis == axis_at else 1 for axis in range(len(extent))])
    return factor_of


def profile(count, total, reach, lean):
    loads = [(1 << 20) // math.isqrt(rank ** lean) + 1 for rank in range(2, count + 1)]
    surplus, holding = total - reach - (count - 1), [1] * (count - 1)
    while surplus > 0:
        candidates = [i for i in range(count - 1) if holding[i] < reach]
        pool, remaining = sum([loads[i] for i in candidates]), surplus
        for i in candidates:
            more = min(reach - holding[i], max(1, remaining * loads[i] // pool), surplus)
            holding[i] = holding[i] + more
            surplus = surplus - more
    return np.array([reach] + holding)


def uneven(key, number_of, total, most, slope):
    if number_of == 2:
        one = jax.random.randint(key, (), max(1, total - most), min(most, total - 1) + 1)
        return jnp.stack([one, total - one])
    sizes = jnp.asarray(profile(number_of, total, most, slope), jnp.int32)
    twos = (number_of - 1) // 2
    donor, receiver = sizes[1:1 + 2 * twos:2], sizes[2:2 + 2 * twos:2]
    room = jnp.minimum(donor - 1, most - receiver)
    passed = jax.random.randint(jax.random.fold_in(key, 1), (twos,), 0, 1 << 20) % (room + 1)
    sizes = sizes.at[1:1 + 2 * twos:2].set(donor - passed).at[2:2 + 2 * twos:2].set(receiver + passed)
    return sizes[jax.random.permutation(jax.random.fold_in(key, 2), number_of)]


def bell_draw(own_key, extent, deviation, limit, cuts=(), dtype=jnp.bfloat16):
    gain = levels(own_key, extent, cuts, -0.22, 0.18) if cuts else 1.0
    drawn = jax.random.normal(own_key, extent, jnp.float32) * deviation * gain
    return jnp.minimum(jnp.maximum(drawn, -limit), limit).astype(dtype)


def setup_inputs(seed: int = 0) -> dict:
    splits = jax.random.split(jax.random.key(seed), 8)
    return {
        "hidden": bell_draw(splits[0], (TOKENS, D), 1.0, 6.0, ((0, 256),)),
        "norm_gain": jnp.clip(1.0 + 0.18 * jax.random.normal(splits[1], (D,), jnp.float32), 0.1, 1.9),
        "w_query": bell_draw(splits[2], (D, HEADS * HEAD_DIM), D ** -0.5, 0.09375, ((0, 64), (1, 4))),
        "w_keyval": draw_w_keyval(jax.random.fold_in(splits[7], 71), 0),
        "nbr_states": draw_nbr_states(jax.random.fold_in(splits[7], 71), 0),
        "nbr_lens": touch_ends(jax.random.randint(splits[5], (SPANS, NEIGHBOURS), NBR_LEN // 4, NBR_LEN + 1), jax.random.fold_in(splits[5], 1), NBR_LEN // 4, NBR_LEN).astype(jnp.int32),
        "segment_ids": jnp.searchsorted(jnp.cumsum(uneven(splits[6], max(4, TOKENS // 512), TOKENS, TOKENS // 2, 2)), jnp.arange(TOKENS), side="right").astype(jnp.int32),
    }


def normalize(source, norm_gain):
    values = source.astype(jnp.float32)
    factor = lax.rsqrt(lax.optimization_barrier(jnp.mean(values * values, axis=-1, keepdims=True)) + 1e-06)
    return (values * factor * norm_gain).astype(jnp.bfloat16)

def attend(query_blocks, key_blocks, value_blocks, key_lengths, live_rows):
    scores = jnp.einsum('bqhd,bkhd->bhqk', query_blocks.astype(jnp.float32), key_blocks.astype(jnp.float32))
    keys_total = key_blocks.shape[1]
    position = lax.broadcasted_iota(jnp.int32, (1, keys_total), 1) % NBR_LEN
    limits = jnp.repeat(key_lengths, NBR_LEN, axis=1)
    usable = (position < limits)[:, None, None, :]
    scores = jnp.where(usable, scores, jnp.float32(-1e+30))
    highest = lax.optimization_barrier(jnp.max(scores, axis=-1, keepdims=True))
    weights = jnp.where(usable, jnp.exp(scores - highest), jnp.float32(0.0))
    weights = (weights / lax.optimization_barrier(jnp.sum(weights, axis=-1, keepdims=True))).astype(jnp.bfloat16)
    mixed = jnp.einsum('bhqk,bkhd->bqhd', weights.astype(jnp.float32), value_blocks.astype(jnp.float32))
    mixed = mixed * live_rows[:, :, None, None].astype(jnp.float32)
    return mixed.astype(jnp.bfloat16)

def reference(hidden, norm_gain, w_query, w_keyval, nbr_states, nbr_lens, segment_ids):
    normed = normalize(hidden, norm_gain)
    width = HEADS * HEAD_DIM
    group = math.gcd(SPANS, 8)
    shifted = jnp.concatenate([normed[SPAN - 1:], jnp.zeros((SPAN - 1, D), jnp.bfloat16)], axis=0)
    shifted = shifted.reshape(SPANS // group, group * SPAN, D)
    row_segments = jnp.concatenate([segment_ids[SPAN - 1:], jnp.full((SPAN - 1,), -1, jnp.int32)])
    row_segments = row_segments.reshape(SPANS // group, group, SPAN)
    end_segments = segment_ids.reshape(SPANS, SPAN)[:, SPAN - 1].reshape(SPANS // group, group)
    states_grouped = nbr_states.reshape(SPANS // group, group * NEIGHBOURS * NBR_LEN, ENC_DIM)
    lengths_grouped = nbr_lens.reshape(SPANS // group, group, NEIGHBOURS)

    def one_group(inputs):
        query_rows, states, lengths, segments, ending = inputs
        query = (jnp.dot(query_rows, w_query, preferred_element_type=jnp.float32) * HEAD_DIM ** (-0.5)).astype(jnp.bfloat16)
        keys = jnp.dot(states, w_keyval[0], preferred_element_type=jnp.float32).astype(jnp.bfloat16)
        values = jnp.dot(states, w_keyval[1], preferred_element_type=jnp.float32).astype(jnp.bfloat16)
        mixed = attend(query.reshape(group, SPAN, HEADS, HEAD_DIM), keys.reshape(group, NEIGHBOURS * NBR_LEN, HEADS, HEAD_DIM), values.reshape(group, NEIGHBOURS * NBR_LEN, HEADS, HEAD_DIM), lengths, segments == ending[:, None])
        return mixed.reshape(group * SPAN, width)
    blocks = lax.map(one_group, (shifted, states_grouped, lengths_grouped, row_segments, end_segments))
    flat = blocks.reshape(SPANS * SPAN, width)
    return jnp.concatenate([jnp.zeros((SPAN - 1, width), jnp.bfloat16), flat[:TOKENS - SPAN + 1]], axis=0)
```

```python
import jax
import jax.numpy as jnp
from jax import lax
from jax.sharding import Mesh, PartitionSpec as P

HEAD_DIM = 128
SPAN = 64
NBR_LEN = 128
SIZES = {"xh": 2, "core": 2, "y": 4, "xl": 2, "z": 8}
Z_ORDER = (0, -1, 1, -2, 2, -3, 3, 4)
Y_ORDER = (0, -1, 1, 2)


def hop(x, axis, by):
    n = SIZES[axis]
    return lax.ppermute(x, axis, [(i, (i + by) % n) for i in range(n)])


def halves(x):
    r = x.shape[0] // 2
    return x[:r], x[r:]


def z_ring(x):
    out = [x]
    a = b = x
    for _ in range(3):
        a, b = hop(a, "z", 1), hop(b, "z", -1)
        out += [a, b]
    return out + [hop(halves(a)[0], "z", 1), hop(halves(b)[1], "z", -1)]


def y_ring(x):
    a, b = hop(x, "y", 1), hop(x, "y", -1)
    return [x, a, b, hop(halves(a)[0], "y", 1), hop(halves(b)[1], "y", -1)]


def normalize(source, norm_gain):
    values = source.astype(jnp.float32)
    factor = lax.rsqrt(jnp.mean(values * values, axis=-1, keepdims=True) + 1e-06)
    return (values * factor * norm_gain).astype(jnp.bfloat16)


def rolled(x, axis, start):
    return lax.dynamic_slice_in_dim(jnp.concatenate([x, x], axis=axis), start, x.shape[axis], axis)


def attend(query_blocks, key_blocks, value_blocks, key_lengths, live_rows):
    scores = jnp.einsum(
        "bqhd,bkhd->bhqk", query_blocks, key_blocks, preferred_element_type=jnp.float32
    )
    keys_total = key_blocks.shape[1]
    position = lax.broadcasted_iota(jnp.int32, (1, keys_total), 1) % NBR_LEN
    limits = jnp.repeat(key_lengths, NBR_LEN, axis=1)
    usable = (position < limits)[:, None, None, :]
    scores = jnp.where(usable, scores, jnp.float32(-1e30))
    highest = jnp.max(scores, axis=-1, keepdims=True)
    weights = jnp.where(usable, jnp.exp(scores - highest), jnp.float32(0.0))
    weights = (weights / jnp.sum(weights, axis=-1, keepdims=True)).astype(jnp.bfloat16)
    mixed = jnp.einsum("bhqk,bkhd->bqhd", weights, value_blocks, preferred_element_type=jnp.float32)
    mixed = mixed * live_rows[:, :, None, None].astype(jnp.float32)
    return mixed.astype(jnp.bfloat16)


def local(hidden, norm_gain, w_query, w_keyval, nbr_states, nbr_lens, segment_ids):
    y, xl, z = lax.axis_index("y"), lax.axis_index("xl"), lax.axis_index("z")
    seq = (y * 2 + xl) * 8 + z
    n_seq = 64
    prev_states = lax.ppermute(nbr_states[-1], ("y", "xl", "z"), [(i, i + 1) for i in range(n_seq - 1)])

    normed = normalize(hidden, norm_gain)
    rows = normed.shape[0]
    n5 = normed.reshape(rows, 4, 2, 8, 64)
    n5 = rolled(rolled(rolled(n5, 1, y), 2, xl), 3, z)
    n5 = n5.transpose(0, 1, 3, 2, 4)
    n5 = jnp.stack([n5[:, dy % 4] for dy in Y_ORDER], axis=1)
    n5 = jnp.stack([n5[:, :, dz % 8] for dz in Z_ORDER], axis=2)
    normed = n5.reshape(rows, 4096)
    far = hop(normed, "xh", 1)
    near_core = hop(normed, "core", 1)
    far_core = hop(far, "core", 1)

    width = w_query.shape[1]
    heads_here = width // HEAD_DIM
    pair = jnp.concatenate([w_query, hop(w_query, "xl", 1)], axis=0)
    half = width // 2
    w_a = jnp.concatenate(y_ring(jnp.concatenate(z_ring(pair[:, :half]), axis=0)), axis=0)
    w_b = jnp.concatenate(z_ring(jnp.concatenate(y_ring(pair[:, half:]), axis=0)), axis=0)

    xh, core = lax.axis_index("xh"), lax.axis_index("core")
    mine = jnp.stack([normed, near_core])
    other = jnp.stack([far, far_core])
    mine = rolled(mine, 0, core)
    other = rolled(other, 0, core)
    whole = rolled(jnp.stack([mine, other]), 0, xh).reshape(4 * rows, 4096)
    whole_b = whole.reshape(4 * rows, 4, 8, 128).transpose(0, 2, 1, 3).reshape(4 * rows, 4096)
    tok_rows = 4 * rows
    blocks = tok_rows // SPAN
    totals = jnp.concatenate(
        [
            jnp.dot(whole, w_a, preferred_element_type=jnp.float32),
            jnp.dot(whole_b, w_b, preferred_element_type=jnp.float32),
        ],
        axis=1,
    )
    query = (totals * HEAD_DIM ** (-0.5)).astype(jnp.bfloat16)
    states = jnp.concatenate([prev_states[None], nbr_states], axis=0)
    projected = jnp.einsum(
        "cne,kef->kcnf", states, w_keyval, preferred_element_type=jnp.float32
    ).astype(jnp.bfloat16)
    neighbour_rows = projected.shape[2]
    key_blocks = projected[0].reshape(blocks + 1, neighbour_rows, heads_here, HEAD_DIM)
    value_blocks = projected[1].reshape(blocks + 1, neighbour_rows, heads_here, HEAD_DIM)
    query_padded = jnp.concatenate(
        [jnp.zeros((1, width), jnp.bfloat16), query, jnp.zeros((SPAN - 1, width), jnp.bfloat16)],
        axis=0,
    )
    query_blocks = query_padded.reshape(blocks + 1, SPAN, heads_here, HEAD_DIM)
    first_span = seq * blocks
    padded_lengths = jnp.concatenate(
        [jnp.ones((1, nbr_lens.shape[1]), jnp.int32), nbr_lens], axis=0
    )
    key_lengths = lax.dynamic_slice_in_dim(padded_lengths, first_span, blocks + 1, 0)
    first_token = first_span * SPAN
    own_segments = lax.dynamic_slice_in_dim(segment_ids, first_token, tok_rows, 0)
    row_segments = jnp.concatenate(
        [jnp.full((1,), -1, jnp.int32), own_segments, jnp.full((SPAN - 1,), -1, jnp.int32)]
    ).reshape(blocks + 1, SPAN)
    shifted_ids = jnp.concatenate([jnp.full((1,), -2, jnp.int32), segment_ids])
    end_segments = lax.dynamic_slice_in_dim(shifted_ids, first_token, blocks * SPAN + 1, 0)[::SPAN]
    live_rows = row_segments == end_segments[:, None]
    mixed = attend(query_blocks, key_blocks, value_blocks, key_lengths, live_rows)
    return mixed.reshape((blocks + 1) * SPAN, width)[1 : 1 + tok_rows]


def solution(mesh):
    fine = Mesh(mesh.devices.reshape(tuple(SIZES.values())), tuple(SIZES))
    section, seq = ("xh", "core"), ("y", "xl", "z")
    in_specs = (
        P(seq + section, None),
        P(),
        P(seq, section),
        P(None, None, section),
        P(seq, None, None),
        P(),
        P(),
    )
    out_specs = P(seq, section)
    return jax.shard_map(local, mesh=fine, in_specs=in_specs, out_specs=out_specs, check_vma=False)
```

```python
import jax
import jax.numpy as jnp
from jax import lax
from jax.experimental import pallas as pl
from jax.experimental.pallas import tpu as pltpu
from jax.sharding import Mesh, PartitionSpec as P

HEAD_DIM = 128
SPAN = 64
NBR_LEN = 128
SIZES = {"xh": 2, "core": 2, "y": 4, "xl": 2, "z": 8}
PLANE = ("core", "y", "xl", "z")
VMEM = pl.BlockSpec(memory_space=pltpu.VMEM)
SMEM = pl.BlockSpec(memory_space=pltpu.SMEM)
MIB = 1 << 20


def params(mib):
    return pltpu.CompilerParams(vmem_limit_bytes=mib * MIB)


def cost(flops, moved, exps=0):
    return pl.CostEstimate(flops=flops, bytes_accessed=moved, transcendentals=exps)


def place(w):
    return (w, 0) if w < 4 else (7 - w, 1)


def ring_pairs(by, inner):
    pairs = []
    for core in range(2):
        along_z = (core == 0) == inner
        for w in range(8):
            for z in range(8):
                w2, z2 = (w, (z + by) % 8) if along_z else ((w + by) % 8, z)
                (y, xl), (y2, xl2) = place(w), place(w2)
                pairs.append(
                    (((core * 4 + y) * 2 + xl) * 8 + z, ((core * 4 + y2) * 2 + xl2) * 8 + z2)
                )
    return pairs


def step(x, by, inner):
    return lax.ppermute(x, PLANE, ring_pairs(by, inner))


def hop(x, axis):
    return lax.ppermute(x, axis, [(0, 1), (1, 0)])


def slot_of(inner_axis_z, by):
    if inner_axis_z:
        return lax.rem(lax.axis_index("z") + by + 8, 8)
    y, xl = lax.axis_index("y"), lax.axis_index("xl")
    w = lax.rem(jnp.where(xl == 0, y, 7 - y) + by + 8, 8)
    return jnp.where(w < 4, 2 * w, 2 * (7 - w) + 1)


INNER = (0, -1, 1, -2, 2, -3, 3, -4)


def stack_kernel(*refs):
    outs, rows, half = refs[8:], refs[0].shape[0], refs[8].shape[1]
    on_z = lax.axis_index("core") == 0
    for by, ref in zip(INNER, refs[:8], strict=True):
        slot = jnp.where(on_z, slot_of(True, by), slot_of(False, by))
        for i, out in enumerate(outs):
            out[pl.ds(pl.multiple_of(slot * rows, rows), rows), :] = ref[:, i * half : (i + 1) * half]


def stacked(parts):
    rows, columns = parts[0].shape
    shape = jax.ShapeDtypeStruct((8 * rows, columns // 2), parts[0].dtype)
    return pl.pallas_call(
        stack_kernel,
        out_shape=[shape, shape],
        in_specs=[VMEM] * 8,
        out_specs=[VMEM, VMEM],
        compiler_params=params(8),
        cost_estimate=cost(0, 32 * rows * columns),
        name="stack",
    )(*parts)


def norm_kernel(hidden_ref, gain_ref, out_ref):
    values = hidden_ref[...].astype(jnp.float32)
    factor = lax.rsqrt(jnp.mean(values * values, axis=-1, keepdims=True) + 1e-06)
    out_ref[...] = (values * factor * gain_ref[...]).astype(jnp.bfloat16)


def normalize(hidden, gain):
    rows, width = hidden.shape
    return pl.pallas_call(
        norm_kernel,
        out_shape=jax.ShapeDtypeStruct((rows, width), jnp.bfloat16),
        in_specs=[VMEM, VMEM],
        out_specs=VMEM,
        compiler_params=params(8),
        cost_estimate=cost(6 * rows * width, 4 * rows * width),
        name="norm",
    )(hidden, gain)


def rows_kernel(own_ref, near_ref, far_ref, far_near_ref, out):
    xh, core = lax.axis_index("xh"), lax.axis_index("core")
    slots = [xh * 2 + core, xh * 2 + 1 - core, 2 - 2 * xh + core, 3 - 2 * xh - core]
    refs = [own_ref, near_ref, far_ref, far_near_ref]
    rows = own_ref.shape[0]

    @pl.when(core == 0)
    def _():
        for slot, ref in zip(slots, refs, strict=True):
            out[pl.ds(pl.multiple_of(slot * rows, rows), rows), :] = ref[...]

    @pl.when(core == 1)
    def _():
        for slot, ref in zip(slots, refs, strict=True):
            at = pl.ds(pl.multiple_of(slot * rows, rows), rows)
            for z in range(8):
                for k in range(4):
                    one = ref[:, (16 * k + z) * 64 : (16 * k + z) * 64 + 64]
                    two = ref[:, (16 * k + 8 + z) * 64 : (16 * k + 8 + z) * 64 + 64]
                    to = z * 512 + k * 128
                    out[at, to : to + 128] = jnp.concatenate([one, two], axis=1)


def gather_rows(parts):
    rows, width = parts[0].shape
    return pl.pallas_call(
        rows_kernel,
        out_shape=jax.ShapeDtypeStruct((4 * rows, width), parts[0].dtype),
        in_specs=[VMEM] * 4,
        out_specs=VMEM,
        compiler_params=params(16),
        cost_estimate=cost(0, 16 * rows * width),
        name="rows",
    )(*parts)


def project_kernel(prev_ref, states_ref, w_ref, out_ref):
    for i in range(out_ref.shape[0]):
        block = prev_ref[0] if i == 0 else states_ref[i - 1]
        out_ref[i] = jnp.dot(block, w_ref[0], preferred_element_type=jnp.float32).astype(jnp.bfloat16)


def project(prev, states, w, which, half):
    spans, keys, depth = states.shape
    columns = w.shape[2] // 2
    whole = lambda i: (0, 0, 0)
    return pl.pallas_call(
        project_kernel,
        grid=(1,),
        out_shape=jax.ShapeDtypeStruct((spans + 1, keys, columns), jnp.bfloat16),
        in_specs=[
            pl.BlockSpec(prev.shape, whole, pipeline_mode=pl.Buffered(1)),
            pl.BlockSpec(states.shape, whole, pipeline_mode=pl.Buffered(1)),
            pl.BlockSpec((1, depth, columns), lambda i: (which, 0, half), pipeline_mode=pl.Buffered(1)),
        ],
        out_specs=pl.BlockSpec((spans + 1, keys, columns), whole, pipeline_mode=pl.Buffered(1)),
        compiler_params=params(20),
        cost_estimate=cost(2 * (spans + 1) * keys * depth * columns, 6 * MIB),
        name="project",
    )(prev, states, w)


def outer_slots(steps):
    on_z = lax.axis_index("core") == 1
    return [jnp.where(on_z, slot_of(True, by), slot_of(False, by)) for by in steps]


def products(n_ref, refs, places):
    total = None
    for ref, (slot, start) in zip(refs, places, strict=True):
        depth = ref.shape[0]
        lanes = pl.ds(pl.multiple_of(slot * 512 + start, 256), depth)
        term = jnp.dot(n_ref[:, lanes], ref[...], preferred_element_type=jnp.float32)
        total = term if total is None else total + term
    return total


def partial_product(n, steps, pieces, before=None):
    rows, columns = n.shape[0], pieces[0].shape[1]
    depth = sum(p.shape[0] for p in pieces)
    extra = [] if before is None else [before]

    def body(n_ref, *refs):
        places = [(slot, 0) for slot in outer_slots(steps)]
        total = products(n_ref, refs[: len(pieces)], places)
        if extra:
            total = total + refs[len(pieces)][...]
        refs[-1][...] = total

    return pl.pallas_call(
        body,
        out_shape=jax.ShapeDtypeStruct((rows, columns), jnp.float32),
        in_specs=[VMEM] * (1 + len(pieces) + len(extra)),
        out_specs=VMEM,
        compiler_params=params(20),
        cost_estimate=cost(2 * rows * depth * columns, 2 * depth * (rows + columns)),
        name="partial",
    )(n, *pieces, *extra)


def attend(lens, segments, total, n, steps, pieces, keys, values, other=None):
    rows, columns = total.shape
    blocks = keys.shape[0]
    heads = columns // HEAD_DIM
    extra = [] if other is None else [other]
    count = len(pieces)

    def body(lens_ref, seg_ref, total_ref, n_ref, k_ref, v_ref, *refs):
        piece_refs, (out_ref, q_scr, c_scr, s_scr, w_scr) = refs[:count], refs[-5:]
        if extra:
            out_ref[:, :columns] = refs[count][...]
        seq = (lax.axis_index("y") * 2 + lax.axis_index("xl")) * 8 + lax.axis_index("z")
        slots = outer_slots(steps)
        places = [(slot, 0) for slot in slots[:-1]] + [(slots[-1], 256)]
        acc = total_ref[...] + products(n_ref, piece_refs, places)
        acc = acc * HEAD_DIM ** (-0.5)
        acc = jnp.concatenate([acc, jnp.zeros((SPAN, columns), jnp.float32)], axis=0)
        q_scr[...] = pltpu.roll(acc, 1, 0).astype(jnp.bfloat16)
        lane = lax.broadcasted_iota(jnp.int32, (1, 128), 1)
        wide = lax.broadcasted_iota(jnp.int32, (1, 2 * NBR_LEN), 1)
        row = lax.broadcasted_iota(jnp.int32, (SPAN, HEAD_DIM), 0)
        usable, live = [], []
        for b in range(blocks):
            span = jnp.maximum(seq * (blocks - 1) + b - 1, 0)
            usable.append(
                wide < jnp.where(wide < NBR_LEN, lens_ref[0, span], lens_ref[1, span] + NBR_LEN)
            )
            line = seg_ref[pl.ds(span // 2, 1), :]
            if b % 2:
                same = (line == line[:, 63:64]) & (lane >= 63) & (lane < 127)
                number = jnp.sum(same.astype(jnp.int32), axis=1, keepdims=True)
            else:
                following = seg_ref[pl.ds(jnp.minimum(span // 2 + 1, seg_ref.shape[0] - 1), 1), :]
                same = (following == line[:, 127:128]) & (lane < 63)
                number = jnp.sum(same.astype(jnp.int32), axis=1, keepdims=True) + 1
            if b == 0:
                number = jnp.where(seq == 0, 0, number)
            live.append(row < number)
        for h in range(heads):
            at = slice(h * HEAD_DIM, (h + 1) * HEAD_DIM)
            for b in range(blocks):
                scores = lax.dot_general(
                    q_scr[b * SPAN : (b + 1) * SPAN, at],
                    k_ref[b, :, at],
                    (((1,), (1,)), ((), ())),
                    preferred_element_type=jnp.float32,
                )
                s_scr[h, b * SPAN : (b + 1) * SPAN, :] = jnp.where(usable[b], scores, jnp.float32(-1e30))
        for h in range(heads):
            for c in range(blocks // 3):
                r = slice(c * 3 * SPAN, (c + 1) * 3 * SPAN)
                scores = s_scr[h, r, :]
                weights = jnp.exp(scores - jnp.max(scores, axis=-1, keepdims=True))
                scale = 1.0 / jnp.sum(weights, axis=-1, keepdims=True)
                w_scr[h, r, :] = (weights * scale).astype(jnp.bfloat16)
        for h in range(heads):
            at = slice(h * HEAD_DIM, (h + 1) * HEAD_DIM)
            for b in range(blocks):
                mixed = jnp.dot(
                    w_scr[h, b * SPAN : (b + 1) * SPAN, :],
                    v_ref[b, :, at],
                    preferred_element_type=jnp.float32,
                )
                c_scr[b * SPAN : (b + 1) * SPAN, at] = jnp.where(live[b], mixed, 0.0)
        moved = pltpu.roll(c_scr[...], blocks * SPAN - 1, 0)
        out_ref[:, len(extra) * columns :] = moved[:rows].astype(jnp.bfloat16)

    return pl.pallas_call(
        body,
        out_shape=jax.ShapeDtypeStruct((rows, columns * (1 + len(extra))), jnp.bfloat16),
        in_specs=[SMEM] + [VMEM] * (5 + count + len(extra)),
        out_specs=VMEM,
        scratch_shapes=[
            pltpu.VMEM((blocks * SPAN, columns), jnp.bfloat16),
            pltpu.VMEM((blocks * SPAN, columns), jnp.float32),
            pltpu.VMEM((heads, blocks * SPAN, 2 * NBR_LEN), jnp.float32),
            pltpu.VMEM((heads, blocks * SPAN, 2 * NBR_LEN), jnp.bfloat16),
        ],
        compiler_params=params(28),
        cost_estimate=cost(3 * MIB * 1000, 8 * MIB),
        name="attend",
    )(lens, segments, total, n, keys, values, *pieces, *extra)


def after(value, *others):
    return lax.optimization_barrier((value, *others))[0]


def local(hidden, norm_gain, w_query, w_keyval, nbr_states, nbr_lens, segment_ids):
    a, b = step(w_query, 1, True), step(w_query, -1, True)
    normed = normalize(hidden, norm_gain[None])
    far = hop(normed, "xh")
    near = hop(normed, "core")
    inner = [w_query, a, b]
    a, b = step(after(a, normed), 1, True), step(after(b, normed), -1, True)
    inner += [a, b]
    prev = lax.ppermute(after(nbr_states[-1:], a, b), ("y", "xl", "z"), [(i, i + 1) for i in range(63)])
    a, b = step(after(a, near), 1, True), step(after(b, near), -1, True)
    inner += [a, b]
    inner.append(step(b, -1, True))
    columns = stacked(inner)

    def projected(which, part, *first):
        return project(prev, after(nbr_states, *first), w_keyval, which, part)

    def both(pair, *first):
        a, b = pair
        return step(after(a, *first), 1, False), step(after(b, *first), -1, False)

    one = [(columns[0], columns[0])]
    two = [(columns[1], columns[1])]
    one.append(both(one[0]))
    two.append(both(two[0]))
    far_near = hop(after(far, *columns), "core")
    keys_a = projected(0, 0, *columns)
    values_a = projected(1, 0, keys_a)
    one.append(both(one[1], values_a))
    keys_b = projected(0, 1, *one[1])
    two.append(both(two[1], keys_b))
    values_b = projected(1, 1, *two[1])
    one.append(both(one[2], values_b, far_near))
    whole = gather_rows([after(normed, *one[2]), near, far, far_near])
    total_a = partial_product(whole, [0, -1, 1], [columns[0], *one[1]])
    two.append(both(two[2], total_a))
    total_b = partial_product(whole, [0, -1, 1], [columns[1], *two[1]])
    total_a = partial_product(whole, [-2, 2], one[2], total_a)

    def split(pair, *first):
        a, b = pair
        r = a.shape[0] // 2
        return step(after(a[:r], *first), 1, False), step(after(b[r:], *first), -1, False)

    one.append(split(one[3], total_a, total_b))
    total_b = partial_product(whole, [-2, 2], two[2], after(total_b, *one[3]))
    two.append(split(two[3], total_b))
    total_a = partial_product(whole, [-3, 3], one[3], after(total_a, *two[3]))
    lens, segments = nbr_lens.T, segment_ids.reshape(-1, 128)
    out = attend(lens, segments, total_a, whole, [-4, -4], one[4], keys_a, values_a)
    total_b = partial_product(whole, [-3, 3], two[3], after(total_b, out))
    return attend(lens, segments, total_b, whole, [-4, -4], two[4], keys_b, values_b, out)


def solution(mesh):
    fine = Mesh(mesh.devices.reshape(tuple(SIZES.values())), tuple(SIZES))
    section, seq = ("xh", "core"), ("y", "xl", "z")
    in_specs = (
        P(seq + section, None),
        P(),
        P(seq, section),
        P(None, None, section),
        P(seq, None, None),
        P(),
        P(),
    )
    out_specs = P(seq, section)
    return jax.shard_map(local, mesh=fine, in_specs=in_specs, out_specs=out_specs, check_vma=False)
```

```python
import jax
import jax.numpy as jnp
from jax import lax
from jax.experimental import pallas as pl
from jax.experimental.pallas import tpu as pltpu
from jax.sharding import Mesh, PartitionSpec as P

HEAD_DIM = 128
SPAN = 64
NBR_LEN = 128
SIZES = {"xh": 2, "core": 2, "y": 4, "xl": 2, "z": 8}
PLANE = ("core", "y", "xl", "z")
VMEM = pl.BlockSpec(memory_space=pltpu.VMEM)
SMEM = pl.BlockSpec(memory_space=pltpu.SMEM)
MIB = 1 << 20


def params(mib):
    return pltpu.CompilerParams(vmem_limit_bytes=mib * MIB)


def cost(flops, moved, exps=0):
    return pl.CostEstimate(flops=flops, bytes_accessed=moved, transcendentals=exps)


def moved(move, y, xl, z):
    by, how = move
    if how == "z":
        return y, xl, (z + by) % 8
    return (y + by) % 4, xl ^ how, z


def send(x, first, second):
    pairs = []
    for core, move in enumerate((first, second)):
        for y in range(4):
            for xl in range(2):
                for z in range(8):
                    y2, xl2, z2 = moved(move, y, xl, z)
                    pairs.append(
                        (((core * 4 + y) * 2 + xl) * 8 + z, ((core * 4 + y2) * 2 + xl2) * 8 + z2)
                    )
    return lax.ppermute(x, PLANE, pairs)


def hop(x, axis):
    return lax.ppermute(x, axis, [(0, 1), (1, 0)])


INNER_Z = (0, -1, 1, -2, 2, -3, 3, -4)
INNER_W = ((0, 0), (0, 1), (-1, 0), (1, 0), (2, 0), (-1, 1), (1, 1), (2, 1))
OUTER_Z = (0, -1, 1, -2, 2, -3, 3, -4)
OUTER_W = ((0, 0), (-1, 0), (1, 0), (0, 1), (2, 0), (-1, 1), (1, 1), (2, 1))


def slots(on_z, by_z, by_w):
    y, xl, z = lax.axis_index("y"), lax.axis_index("xl"), lax.axis_index("z")
    out = []
    for dz, (dy, flip) in zip(by_z, by_w, strict=True):
        other = jnp.where(xl == flip, 0, 1)
        out.append(jnp.where(on_z, lax.rem(z + dz + 8, 8), lax.rem(y + dy + 4, 4) * 2 + other))
    return out


def stack_kernel(*refs):
    out, rows = refs[-1], refs[0].shape[0]
    places = slots(lax.axis_index("core") == 0, INNER_Z, INNER_W)
    for slot, ref in zip(places, refs[:-1], strict=True):
        out[pl.ds(pl.multiple_of(slot * rows, rows), rows), :] = ref[...]


def stacked(parts):
    rows, columns = parts[0].shape
    return pl.pallas_call(
        stack_kernel,
        out_shape=jax.ShapeDtypeStruct((8 * rows, columns), parts[0].dtype),
        in_specs=[VMEM] * 8,
        out_specs=VMEM,
        compiler_params=params(8),
        cost_estimate=cost(0, 32 * rows * columns),
        name="stack",
    )(*parts)


def norm_kernel(hidden_ref, gain_ref, out_ref):
    values = hidden_ref[...].astype(jnp.float32)
    factor = lax.rsqrt(jnp.mean(values * values, axis=-1, keepdims=True) + 1e-06)
    out_ref[...] = (values * factor * gain_ref[...]).astype(jnp.bfloat16)


def normalize(hidden, gain):
    rows, width = hidden.shape
    return pl.pallas_call(
        norm_kernel,
        out_shape=jax.ShapeDtypeStruct((rows, width), jnp.bfloat16),
        in_specs=[VMEM, VMEM],
        out_specs=VMEM,
        compiler_params=params(8),
        cost_estimate=cost(6 * rows * width, 4 * rows * width),
        name="norm",
    )(hidden, gain)


def rows_kernel(own_ref, near_ref, far_ref, far_near_ref, out):
    xh, core = lax.axis_index("xh"), lax.axis_index("core")
    slots = [xh * 2 + core, xh * 2 + 1 - core, 2 - 2 * xh + core, 3 - 2 * xh - core]
    refs = [own_ref, near_ref, far_ref, far_near_ref]
    rows = own_ref.shape[0]

    @pl.when(core == 0)
    def _():
        for slot, ref in zip(slots, refs, strict=True):
            out[pl.ds(pl.multiple_of(slot * rows, rows), rows), :] = ref[...]

    @pl.when(core == 1)
    def _():
        for slot, ref in zip(slots, refs, strict=True):
            at = pl.ds(pl.multiple_of(slot * rows, rows), rows)
            for z in range(8):
                for k in range(4):
                    one = ref[:, (16 * k + z) * 64 : (16 * k + z) * 64 + 64]
                    two = ref[:, (16 * k + 8 + z) * 64 : (16 * k + 8 + z) * 64 + 64]
                    to = z * 512 + k * 128
                    out[at, to : to + 128] = jnp.concatenate([one, two], axis=1)


def gather_rows(parts):
    rows, width = parts[0].shape
    return pl.pallas_call(
        rows_kernel,
        out_shape=jax.ShapeDtypeStruct((4 * rows, width), parts[0].dtype),
        in_specs=[VMEM] * 4,
        out_specs=VMEM,
        compiler_params=params(16),
        cost_estimate=cost(0, 16 * rows * width),
        name="rows",
    )(*parts)


def project_kernel(mine_ref, other_ref, states_ref, w_ref, out_ref):
    core, rows = lax.axis_index("core"), mine_ref.shape[0]
    for slot, ref in ((core, mine_ref), (1 - core, other_ref)):
        out_ref[0, pl.ds(pl.multiple_of(slot * rows, rows), rows), :] = jnp.dot(
            ref[...], w_ref[0], preferred_element_type=jnp.float32
        ).astype(jnp.bfloat16)
    for i in range(1, out_ref.shape[0]):
        out_ref[i] = jnp.dot(
            states_ref[i - 1], w_ref[0], preferred_element_type=jnp.float32
        ).astype(jnp.bfloat16)


def project(prev, states, w, which, half):
    spans, keys, depth = states.shape
    columns = w.shape[2] // 2
    whole = lambda i: (0, 0, 0)
    part = pl.BlockSpec(prev[0].shape, lambda i: (0, 0), pipeline_mode=pl.Buffered(1))
    return pl.pallas_call(
        project_kernel,
        grid=(1,),
        out_shape=jax.ShapeDtypeStruct((spans + 1, keys, columns), jnp.bfloat16),
        in_specs=[
            part,
            part,
            pl.BlockSpec(states.shape, whole, pipeline_mode=pl.Buffered(1)),
            pl.BlockSpec((1, depth, columns), lambda i: (which, 0, half), pipeline_mode=pl.Buffered(1)),
        ],
        out_specs=pl.BlockSpec((spans + 1, keys, columns), whole, pipeline_mode=pl.Buffered(1)),
        compiler_params=params(16),
        cost_estimate=cost(2 * (spans + 1) * keys * depth * columns, 6 * MIB),
        name="project",
    )(*prev, states, w)


def outer_slots(which):
    places = slots(lax.axis_index("core") == 1, OUTER_Z, OUTER_W)
    return [places[i] for i in which]


def products(n_ref, refs, places):
    total = None
    for ref, (slot, start) in zip(refs, places, strict=True):
        depth = ref.shape[0]
        lanes = pl.ds(pl.multiple_of(slot * 512 + start, 256), depth)
        term = jnp.dot(n_ref[:, lanes], ref[...], preferred_element_type=jnp.float32)
        total = term if total is None else total + term
    return total


def partial_product(n, which, pieces, before=None):
    rows, columns = n.shape[0], pieces[0].shape[1]
    depth = sum(p.shape[0] for p in pieces)
    extra = [] if before is None else [before]

    def body(n_ref, *refs):
        places = [(slot, 0) for slot in outer_slots(which)]
        total = products(n_ref, refs[: len(pieces)], places)
        if extra:
            total = total + refs[len(pieces)][...]
        refs[-1][...] = total

    return pl.pallas_call(
        body,
        out_shape=jax.ShapeDtypeStruct((rows, columns), jnp.float32),
        in_specs=[VMEM] * (1 + len(pieces) + len(extra)),
        out_specs=VMEM,
        compiler_params=params(16),
        cost_estimate=cost(2 * rows * depth * columns, 2 * depth * (rows + columns)),
        name="partial",
    )(n, *pieces, *extra)


def attend(lens, segments, total, n, pieces, keys, values):
    rows, columns = total.shape
    blocks = keys[0].shape[0]
    heads = columns // HEAD_DIM // 2
    half = columns // 2

    def body(lens_ref, seg_ref, total_ref, n_ref, one_ref, two_ref, *refs):
        k_refs, v_refs, (out_ref, q_scr, c_scr, s_scr, w_scr) = refs[:2], refs[2:4], refs[4:]
        seq = (lax.axis_index("y") * 2 + lax.axis_index("xl")) * 8 + lax.axis_index("z")
        (slot,) = outer_slots([7])
        acc = total_ref[...] + products(n_ref, [one_ref, two_ref], [(slot, 0), (slot, 256)])
        acc = acc * HEAD_DIM ** (-0.5)
        acc = jnp.concatenate([acc, jnp.zeros((SPAN, columns), jnp.float32)], axis=0)
        q_scr[...] = pltpu.roll(acc, 1, 0).astype(jnp.bfloat16)
        lane = lax.broadcasted_iota(jnp.int32, (1, 128), 1)
        wide = lax.broadcasted_iota(jnp.int32, (1, 2 * NBR_LEN), 1)
        row = lax.broadcasted_iota(jnp.int32, (SPAN, HEAD_DIM), 0)
        usable, live = [], []
        for b in range(blocks):
            span = jnp.maximum(seq * (blocks - 1) + b - 1, 0)
            usable.append(
                wide < jnp.where(wide < NBR_LEN, lens_ref[0, span], lens_ref[1, span] + NBR_LEN)
            )
            line = seg_ref[pl.ds(span // 2, 1), :]
            if b % 2:
                same = (line == line[:, 63:64]) & (lane >= 63) & (lane < 127)
                count = jnp.sum(same.astype(jnp.int32), axis=1, keepdims=True)
            else:
                after = seg_ref[pl.ds(jnp.minimum(span // 2 + 1, seg_ref.shape[0] - 1), 1), :]
                same = (after == line[:, 127:128]) & (lane < 63)
                count = jnp.sum(same.astype(jnp.int32), axis=1, keepdims=True) + 1
            if b == 0:
                count = jnp.where(seq == 0, 0, count)
            live.append(row < count)
        for part in range(2):
            for h in range(heads):
                at = slice(h * HEAD_DIM, (h + 1) * HEAD_DIM)
                to = slice(part * half + h * HEAD_DIM, part * half + (h + 1) * HEAD_DIM)
                for b in range(blocks):
                    scores = lax.dot_general(
                        q_scr[b * SPAN : (b + 1) * SPAN, to],
                        k_refs[part][b, :, at],
                        (((1,), (1,)), ((), ())),
                        preferred_element_type=jnp.float32,
                    )
                    s_scr[h, b * SPAN : (b + 1) * SPAN, :] = jnp.where(usable[b], scores, jnp.float32(-1e30))
            for h in range(heads):
                for c in range(blocks // 3):
                    r = slice(c * 3 * SPAN, (c + 1) * 3 * SPAN)
                    scores = s_scr[h, r, :]
                    weights = jnp.exp(scores - jnp.max(scores, axis=-1, keepdims=True))
                    scale = 1.0 / jnp.sum(weights, axis=-1, keepdims=True)
                    w_scr[h, r, :] = (weights * scale).astype(jnp.bfloat16)
            for h in range(heads):
                at = slice(h * HEAD_DIM, (h + 1) * HEAD_DIM)
                to = slice(part * half + h * HEAD_DIM, part * half + (h + 1) * HEAD_DIM)
                for b in range(blocks):
                    mixed = jnp.dot(
                        w_scr[h, b * SPAN : (b + 1) * SPAN, :],
                        v_refs[part][b, :, at],
                        preferred_element_type=jnp.float32,
                    )
                    c_scr[b * SPAN : (b + 1) * SPAN, to] = jnp.where(live[b], mixed, 0.0)
        moved = pltpu.roll(c_scr[...], blocks * SPAN - 1, 0)
        out_ref[...] = moved[:rows].astype(jnp.bfloat16)

    return pl.pallas_call(
        body,
        out_shape=jax.ShapeDtypeStruct((rows, columns), jnp.bfloat16),
        in_specs=[SMEM] + [VMEM] * 9,
        out_specs=VMEM,
        scratch_shapes=[
            pltpu.VMEM((blocks * SPAN, columns), jnp.bfloat16),
            pltpu.VMEM((blocks * SPAN, columns), jnp.float32),
            pltpu.VMEM((heads, blocks * SPAN, 2 * NBR_LEN), jnp.float32),
            pltpu.VMEM((heads, blocks * SPAN, 2 * NBR_LEN), jnp.bfloat16),
        ],
        compiler_params=params(28),
        cost_estimate=cost(6 * MIB * 1000, 16 * MIB),
        name="attend",
    )(lens, segments, total, n, *pieces, *keys, *values)


def after(value, *others):
    return lax.optimization_barrier((value, *others))[0]


def local(hidden, norm_gain, w_query, w_keyval, nbr_states, nbr_lens, segment_ids):
    core = lax.axis_index("core")

    def pick(zero, one):
        return jnp.where(core == 0, zero, one)

    inner = [
        w_query,
        send(w_query, (1, "z"), (0, 1)),
        send(w_query, (-1, "z"), (1, 0)),
        send(w_query, (2, "z"), (-1, 0)),
        send(w_query, (-2, "z"), (2, 0)),
    ]
    normed = normalize(hidden, norm_gain[None])
    near = hop(normed, "core")
    far = hop(normed, "xh")
    a = pick(inner[3], inner[1])
    b = pick(inner[4], inner[1])
    half = nbr_states.shape[1] // 2
    prev = lax.dynamic_slice_in_dim(nbr_states[-1], core * half, half, 0)
    prev = lax.ppermute(after(prev, a, b), ("y", "xl", "z"), [(i, i + 1) for i in range(63)])
    inner += [
        send(a, (1, "z"), (1, 0)),
        send(b, (-1, "z"), (-1, 0)),
        send(a, (2, "z"), (2, 0)),
    ]
    own = stacked([after(inner[0], prev), *inner[1:]])
    prev = [prev, hop(after(prev, own), "core")]

    def projected(which, part, *first):
        return project(prev, after(nbr_states, *first), w_keyval, which, part)

    outer = [own, send(own, (1, 0), (1, "z")), send(own, (-1, 0), (-1, "z"))]
    keys_a = projected(0, 0, own)
    far_near = hop(after(far, keys_a), "core")
    values_a = projected(1, 0, keys_a)
    first = after(outer[1], keys_a, values_a, far)
    outer += [
        send(pick(own, first), (0, 1), (1, "z")),
        send(after(outer[2], keys_a, values_a), (-1, 0), (-1, "z")),
    ]
    keys_b = projected(0, 1, *outer[1:3])
    values_b = projected(1, 1, keys_b)
    whole = gather_rows([after(normed, keys_b), near, far, far_near])
    outer += [
        send(after(outer[3], keys_b, values_b), (1, 0), (1, "z")),
        send(after(pick(outer[3], outer[4]), keys_b, values_b), (-1, 0), (-1, "z")),
    ]
    total = partial_product(after(whole, *outer[3:5]), [0, 1, 2], outer[:3])
    total = partial_product(whole, [3, 4], outer[3:5], total)
    r = own.shape[0] // 2
    last = [
        send(after(outer[5][:r], total), (1, 0), (1, "z")),
        send(after(outer[6][r:], total), (-1, 0), (-1, "z")),
    ]
    total = partial_product(whole, [5, 6], outer[5:7], total)
    return attend(
        nbr_lens.T,
        segment_ids.reshape(-1, 128),
        total,
        whole,
        last,
        [keys_a, keys_b],
        [values_a, values_b],
    )


def solution(mesh):
    fine = Mesh(mesh.devices.reshape(tuple(SIZES.values())), tuple(SIZES))
    section, seq = ("xh", "core"), ("y", "xl", "z")
    in_specs = (
        P(seq + section, None),
        P(),
        P(seq, section),
        P(None, None, section),
        P(seq, None, None),
        P(),
        P(),
    )
    out_specs = P(seq, section)
    return jax.shard_map(local, mesh=fine, in_specs=in_specs, out_specs=out_specs, check_vma=False)
```

```python
import functools

import jax
import jax.numpy as jnp
from jax import lax
from jax.experimental import pallas as pl
from jax.experimental.pallas import tpu as pltpu
from jax.sharding import Mesh, PartitionSpec as P

HEAD_DIM = 128
SPAN = 64
NBR_LEN = 128
SIZES = {"xh": 2, "core": 2, "y": 4, "xl": 2, "z": 8}
PLANE = ("core", "y", "xl", "z")
VMEM = pl.BlockSpec(memory_space=pltpu.VMEM)
SMEM = pl.BlockSpec(memory_space=pltpu.SMEM)
MIB = 1 << 20


def params(mib):
    return pltpu.CompilerParams(vmem_limit_bytes=mib * MIB)


def cost(flops, moved, exps=0):
    return pl.CostEstimate(flops=flops, bytes_accessed=moved, transcendentals=exps)


def moved(move, y, xl, z):
    by, how = move
    if how == "z":
        return y, xl, (z + by) % 8
    return (y + by) % 4, xl ^ how, z


def send(x, first, second):
    pairs = []
    for core, move in enumerate((first, second)):
        for y in range(4):
            for xl in range(2):
                for z in range(8):
                    y2, xl2, z2 = moved(move, y, xl, z)
                    pairs.append(
                        (((core * 4 + y) * 2 + xl) * 8 + z, ((core * 4 + y2) * 2 + xl2) * 8 + z2)
                    )
    return lax.ppermute(x, PLANE, pairs)


def hop(x, axis):
    return lax.ppermute(x, axis, [(0, 1), (1, 0)])


OUTER_Z = (0, -1, 1, -2, 2, -3, 3, -4)
OUTER_W = ((0, 0), (-1, 0), (1, 0), (0, 1), (2, 0), (-1, 1), (1, 1), (2, 1))


def outer_slots(which):
    y, xl, z = lax.axis_index("y"), lax.axis_index("xl"), lax.axis_index("z")
    out = []
    for i in which:
        dz, (dy, flip) = OUTER_Z[i], OUTER_W[i]
        other = jnp.where(xl == flip, 0, 1)
        along_w = lax.rem(y + dy + 4, 4) * 2 + other
        out.append(jnp.where(lax.axis_index("core") == 1, lax.rem(z + dz + 8, 8), along_w))
    return out


def stack_kernel(orders, *refs):
    out, rows = refs[-1], refs[0].shape[0]
    for core, order in enumerate(orders):

        @pl.when(lax.axis_index("core") == core)
        def _(order=order):
            for i, which in enumerate(order):
                out[i * rows : (i + 1) * rows, :] = refs[which][...]


def stacked(parts, orders):
    rows, columns = parts[0].shape
    return pl.pallas_call(
        functools.partial(stack_kernel, orders),
        out_shape=jax.ShapeDtypeStruct((4 * rows, columns), parts[0].dtype),
        in_specs=[VMEM] * len(parts),
        out_specs=VMEM,
        compiler_params=params(8),
        cost_estimate=cost(0, 16 * rows * columns),
        name="stack",
    )(*parts)


def norm_kernel(hidden_ref, gain_ref, out_ref):
    values = hidden_ref[...].astype(jnp.float32)
    factor = lax.rsqrt(jnp.mean(values * values, axis=-1, keepdims=True) + 1e-06)
    out_ref[...] = (values * factor * gain_ref[...]).astype(jnp.bfloat16)


def normalize(hidden, gain):
    rows, width = hidden.shape
    return pl.pallas_call(
        norm_kernel,
        out_shape=jax.ShapeDtypeStruct((rows, width), jnp.bfloat16),
        in_specs=[VMEM, VMEM],
        out_specs=VMEM,
        compiler_params=params(8),
        cost_estimate=cost(6 * rows * width, 4 * rows * width),
        name="norm",
    )(hidden, gain)


def rows_kernel(own_ref, near_ref, far_ref, far_near_ref, out):
    xh, core = lax.axis_index("xh"), lax.axis_index("core")
    y, xl, z = lax.axis_index("y"), lax.axis_index("xl"), lax.axis_index("z")
    slots = [xh * 2 + core, xh * 2 + 1 - core, 2 - 2 * xh + core, 3 - 2 * xh - core]
    refs = [own_ref, near_ref, far_ref, far_near_ref]
    rows = own_ref.shape[0]
    tile = lambda ref, at: ref[:, pl.ds(pl.multiple_of(at, 128), 128)]
    start = lax.rem(z + 6, 8) // 2

    for slot, ref in zip(slots, refs, strict=True):
        at = pl.ds(pl.multiple_of(slot * rows, rows), rows)

        @pl.when((core == 0) & (lax.rem(z, 2) == 0))
        def _(at=at, ref=ref):
            for w in range(8):
                for k in range(4):
                    to = w * 512 + k * 128
                    out[at, to : to + 128] = tile(ref, w * 512 + lax.rem(start + k, 4) * 128)

        @pl.when((core == 0) & (lax.rem(z, 2) == 1))
        def _(at=at, ref=ref):
            for w in range(8):
                for k in range(4):
                    one = tile(ref, w * 512 + lax.rem(start + k, 4) * 128)[:, 64:]
                    two = tile(ref, w * 512 + lax.rem(start + k + 1, 4) * 128)[:, :64]
                    to = w * 512 + k * 128
                    out[at, to : to + 128] = jnp.concatenate([one, two], axis=1)

        @pl.when(core == 1)
        def _(at=at, ref=ref):
            for k in range(4):
                side = xl if k < 2 else 1 - xl
                base = [(lax.rem(y + 2 * (k % 2) + i, 4) * 2 + side) * 512 for i in range(2)]
                for z_at in range(8):
                    half = slice(64 * (z_at % 2), 64 * (z_at % 2) + 64)
                    one, two = [tile(ref, b + z_at // 2 * 128)[:, half] for b in base]
                    to = z_at * 512 + k * 128
                    out[at, to : to + 128] = jnp.concatenate([one, two], axis=1)


def gather_rows(parts):
    rows, width = parts[0].shape
    return pl.pallas_call(
        rows_kernel,
        out_shape=jax.ShapeDtypeStruct((4 * rows, width), parts[0].dtype),
        in_specs=[VMEM] * 4,
        out_specs=VMEM,
        compiler_params=params(16),
        cost_estimate=cost(0, 16 * rows * width),
        name="rows",
    )(*parts)


def project_kernel(states_ref, w_ref, out_ref):
    for i in range(out_ref.shape[0]):
        out_ref[i] = jnp.dot(
            states_ref[i], w_ref[0], preferred_element_type=jnp.float32
        ).astype(jnp.bfloat16)


def project(states, w, which, half):
    spans, keys, depth = states.shape
    columns = w.shape[2] // 2
    whole = lambda i: (0, 0, 0)
    return pl.pallas_call(
        project_kernel,
        grid=(1,),
        out_shape=jax.ShapeDtypeStruct((spans, keys, columns), jnp.bfloat16),
        in_specs=[
            pl.BlockSpec(states.shape, whole, pipeline_mode=pl.Buffered(1)),
            pl.BlockSpec((1, depth, columns), lambda i: (which, 0, half), pipeline_mode=pl.Buffered(1)),
        ],
        out_specs=pl.BlockSpec((spans, keys, columns), whole, pipeline_mode=pl.Buffered(1)),
        compiler_params=params(16),
        cost_estimate=cost(2 * spans * keys * depth * columns, 6 * MIB),
        name="project",
    )(states, w)


def project_prev_kernel(mine_ref, other_ref, w_ref, out_ref):
    core, rows = lax.axis_index("core"), mine_ref.shape[0]
    for which in range(2):
        for slot, ref in ((core, mine_ref), (1 - core, other_ref)):
            out_ref[which, pl.ds(pl.multiple_of(slot * rows, rows), rows), :] = jnp.dot(
                ref[...], w_ref[which], preferred_element_type=jnp.float32
            ).astype(jnp.bfloat16)


def project_prev(mine, other, w):
    rows, depth = mine.shape
    columns = w.shape[2]
    return pl.pallas_call(
        project_prev_kernel,
        out_shape=jax.ShapeDtypeStruct((2, 2 * rows, columns), jnp.bfloat16),
        in_specs=[VMEM] * 3,
        out_specs=VMEM,
        compiler_params=params(12),
        cost_estimate=cost(8 * rows * depth * columns, 6 * MIB),
        name="project_prev",
    )(mine, other, w)


def products(n_ref, refs, places):
    total = None
    for ref, place in zip(refs, places, strict=True):
        lanes = pl.ds(pl.multiple_of(place, 128), ref.shape[0])
        term = jnp.dot(n_ref[:, lanes], ref[...], preferred_element_type=jnp.float32)
        total = term if total is None else total + term
    return total


def partial_product(n, start, which, pieces, before=None):
    rows, columns = n.shape[0], pieces[0].shape[1]
    depth = sum(p.shape[0] for p in pieces)
    extra = [] if before is None else [before]

    def body(n_ref, *refs):
        places = [slot * 512 + start for slot in outer_slots(which)]
        total = products(n_ref, refs[: len(pieces)], places)
        if extra:
            total = total + refs[len(pieces)][...]
        refs[-1][...] = total

    return pl.pallas_call(
        body,
        out_shape=jax.ShapeDtypeStruct((rows, columns), jnp.float32),
        in_specs=[VMEM] * (1 + len(pieces) + len(extra)),
        out_specs=VMEM,
        compiler_params=params(16),
        cost_estimate=cost(2 * rows * depth * columns, 2 * depth * (rows + columns)),
        name="partial",
    )(n, *pieces, *extra)


def attend(lens, segments, total, n, pieces, prev, keys, values):
    rows, columns = total.shape
    blocks = keys[0].shape[0] + 1
    heads = columns // HEAD_DIM // 2
    half = columns // 2

    def body(lens_ref, seg_ref, total_ref, n_ref, *refs):
        piece_refs, prev_ref, k_refs, v_refs = refs[:4], refs[4], refs[5:7], refs[7:9]
        out_ref, q_scr, c_scr, s_scr, w_scr = refs[9:]
        seq = (lax.axis_index("y") * 2 + lax.axis_index("xl")) * 8 + lax.axis_index("z")
        (slot,) = outer_slots([7])
        places = [slot * 512 + i * 128 for i in range(4)]
        acc = total_ref[...] + products(n_ref, piece_refs, places)
        acc = acc * HEAD_DIM ** (-0.5)
        acc = jnp.concatenate([acc, jnp.zeros((SPAN, columns), jnp.float32)], axis=0)
        q_scr[...] = pltpu.roll(acc, 1, 0).astype(jnp.bfloat16)
        lane = lax.broadcasted_iota(jnp.int32, (1, 128), 1)
        wide = lax.broadcasted_iota(jnp.int32, (1, 2 * NBR_LEN), 1)
        row = lax.broadcasted_iota(jnp.int32, (SPAN, HEAD_DIM), 0)
        usable, live = [], []
        for b in range(blocks):
            span = jnp.maximum(seq * (blocks - 1) + b - 1, 0)
            usable.append(
                wide < jnp.where(wide < NBR_LEN, lens_ref[0, span], lens_ref[1, span] + NBR_LEN)
            )
            line = seg_ref[pl.ds(span // 2, 1), :]
            if b % 2:
                same = (line == line[:, 63:64]) & (lane >= 63) & (lane < 127)
                count = jnp.sum(same.astype(jnp.int32), axis=1, keepdims=True)
            else:
                after = seg_ref[pl.ds(jnp.minimum(span // 2 + 1, seg_ref.shape[0] - 1), 1), :]
                same = (after == line[:, 127:128]) & (lane < 63)
                count = jnp.sum(same.astype(jnp.int32), axis=1, keepdims=True) + 1
            if b == 0:
                count = jnp.where(seq == 0, 0, count)
            live.append(row < count)
        for part in range(2):
            for h in range(heads):
                at = slice(h * HEAD_DIM, (h + 1) * HEAD_DIM)
                to = slice(part * half + h * HEAD_DIM, part * half + (h + 1) * HEAD_DIM)
                for b in range(blocks):
                    scores = lax.dot_general(
                        q_scr[b * SPAN : (b + 1) * SPAN, to],
                        k_refs[part][b - 1, :, at] if b else prev_ref[0, :, to],
                        (((1,), (1,)), ((), ())),
                        preferred_element_type=jnp.float32,
                    )
                    s_scr[h, b * SPAN : (b + 1) * SPAN, :] = jnp.where(usable[b], scores, jnp.float32(-1e30))
            for h in range(heads):
                for c in range(blocks // 3):
                    r = slice(c * 3 * SPAN, (c + 1) * 3 * SPAN)
                    scores = s_scr[h, r, :]
                    weights = jnp.exp(scores - jnp.max(scores, axis=-1, keepdims=True))
                    scale = 1.0 / jnp.sum(weights, axis=-1, keepdims=True)
                    w_scr[h, r, :] = (weights * scale).astype(jnp.bfloat16)
            for h in range(heads):
                at = slice(h * HEAD_DIM, (h + 1) * HEAD_DIM)
                to = slice(part * half + h * HEAD_DIM, part * half + (h + 1) * HEAD_DIM)
                for b in range(blocks):
                    mixed = jnp.dot(
                        w_scr[h, b * SPAN : (b + 1) * SPAN, :],
                        v_refs[part][b - 1, :, at] if b else prev_ref[1, :, to],
                        preferred_element_type=jnp.float32,
                    )
                    c_scr[b * SPAN : (b + 1) * SPAN, to] = jnp.where(live[b], mixed, 0.0)
        moved = pltpu.roll(c_scr[...], blocks * SPAN - 1, 0)
        out_ref[...] = moved[:rows].astype(jnp.bfloat16)

    return pl.pallas_call(
        body,
        out_shape=jax.ShapeDtypeStruct((rows, columns), jnp.bfloat16),
        in_specs=[SMEM] + [VMEM] * 12,
        out_specs=VMEM,
        scratch_shapes=[
            pltpu.VMEM((blocks * SPAN, columns), jnp.bfloat16),
            pltpu.VMEM((blocks * SPAN, columns), jnp.float32),
            pltpu.VMEM((heads, blocks * SPAN, 2 * NBR_LEN), jnp.float32),
            pltpu.VMEM((heads, blocks * SPAN, 2 * NBR_LEN), jnp.bfloat16),
        ],
        compiler_params=params(28),
        cost_estimate=cost(6 * MIB * 1000, 16 * MIB),
        name="attend",
    )(lens, segments, total, n, *pieces, prev, *keys, *values)


def after(value, *others):
    return lax.optimization_barrier((value, *others))[0]


def local(hidden, norm_gain, w_query, w_keyval, nbr_states, nbr_lens, segment_ids):
    core = lax.axis_index("core")

    def pick(zero, one):
        return jnp.where(core == 0, zero, one)

    def outer_first(column):
        return [send(column, (1, 0), (1, "z")), send(column, (-1, 0), (-1, "z"))]

    def outer_second(column, one, two, *first):
        return [
            send(after(pick(column, one), *first), (0, 1), (1, "z")),
            send(after(two, *first), (-1, 0), (-1, "z")),
        ]

    def outer_third(three, four, *first):
        return [
            send(after(three, *first), (1, 0), (1, "z")),
            send(after(pick(three, four), *first), (-1, 0), (-1, "z")),
        ]

    def outer_last(five, six, *first):
        r = five.shape[0] // 2
        return [
            send(after(five[:r], *first), (1, 0), (1, "z")),
            send(after(six[r:], *first), (-1, 0), (-1, "z")),
        ]

    def projected(which, part, *first):
        return project(after(nbr_states, *first), w_keyval, which, part)

    round_one = [
        send(w_query, (1, "z"), (0, 1)),
        send(w_query, (-1, "z"), (1, 0)),
        send(w_query, (2, "z"), (-1, 0)),
        send(w_query, (-2, "z"), (2, 0)),
    ]
    normed = normalize(hidden, norm_gain[None])
    near = hop(normed, "core")
    far = hop(normed, "xh")
    column_a = stacked([w_query, *round_one], ((3, 1, 0, 2), (0, 3, 4, 2)))
    head = after(pick(round_one[3], round_one[0]), normed)
    round_two = [
        send(head, (-1, "z"), (-1, 0)),
        send(head, (-2, "z"), (2, 0)),
        send(pick(round_one[2], round_one[0]), (1, "z"), (1, 0)),
    ]
    column_b = stacked([head, *round_two], ((0, 1, 2, 3), (0, 1, 2, 3)))

    a = [column_a, *outer_first(column_a)]
    half = nbr_states.shape[1] // 2
    prev = lax.dynamic_slice_in_dim(nbr_states[-1], core * half, half, 0)
    prev = lax.ppermute(after(prev, column_a), ("y", "xl", "z"), [(i, i + 1) for i in range(63)])
    keys_a = projected(0, 0, column_a)
    b = [column_b, *outer_first(column_b)]
    a += outer_second(*a, keys_a)
    values_a = projected(1, 0, *a[1:3])
    b += outer_second(*b, values_a)
    far_near = hop(after(far, values_a), "core")
    keys_b = projected(0, 1, *b[1:3])
    a += outer_third(*a[3:5], keys_b)
    values_b = projected(1, 1, *a[3:5], prev)
    b += outer_third(*b[3:5], values_b)
    prev_near = hop(after(prev, values_b), "core")
    whole = gather_rows([after(normed, *b[3:5]), near, far, far_near])
    total = partial_product(whole, 0, [0, 1, 2], a[:3])
    a += outer_last(*a[5:7], total)
    total = partial_product(whole, 256, [0, 1, 2], b[:3], total)
    total = partial_product(whole, 0, [3, 4], a[3:5], total)
    b += outer_last(*b[5:7], total)
    total = partial_product(whole, 256, [3, 4], b[3:5], total)
    prev = project_prev(after(prev, total), prev_near, w_keyval)
    total = partial_product(whole, 0, [5, 6], a[5:7], total)
    total = partial_product(whole, 256, [5, 6], b[5:7], total)
    return attend(
        nbr_lens.T,
        segment_ids.reshape(-1, 128),
        total,
        whole,
        [*a[7:], *b[7:]],
        prev,
        [keys_a, keys_b],
        [values_a, values_b],
    )


def solution(mesh):
    fine = Mesh(mesh.devices.reshape(tuple(SIZES.values())), tuple(SIZES))
    section, seq = ("xh", "core"), ("y", "xl", "z")
    in_specs = (
        P(seq + section, None),
        P(),
        P(seq, section),
        P(None, None, section),
        P(seq, None, None),
        P(),
        P(),
    )
    out_specs = P(seq, section)
    return jax.shard_map(local, mesh=fine, in_specs=in_specs, out_specs=out_specs, check_vma=False)
```

```python
import functools

import jax
import jax.numpy as jnp
from jax import lax
from jax.experimental import pallas as pl
from jax.experimental.pallas import tpu as pltpu
from jax.sharding import Mesh, PartitionSpec as P

HEAD_DIM = 128
SPAN = 64
NBR_LEN = 128
SIZES = {"xh": 2, "core": 2, "y": 4, "xl": 2, "z": 8}
PLANE = ("core", "y", "xl", "z")
VMEM = pl.BlockSpec(memory_space=pltpu.VMEM)
SMEM = pl.BlockSpec(memory_space=pltpu.SMEM)
MIB = 1 << 20


def params(mib):
    return pltpu.CompilerParams(vmem_limit_bytes=mib * MIB)


def cost(flops, moved, exps=0):
    return pl.CostEstimate(flops=flops, bytes_accessed=moved, transcendentals=exps)


def moved(move, y, xl, z):
    by, how = move
    if how == "z":
        return y, xl, (z + by) % 8
    return (y + by) % 4, xl ^ how, z


def send(x, first, second):
    pairs = []
    for core, move in enumerate((first, second)):
        for y in range(4):
            for xl in range(2):
                for z in range(8):
                    y2, xl2, z2 = moved(move, y, xl, z)
                    pairs.append(
                        (((core * 4 + y) * 2 + xl) * 8 + z, ((core * 4 + y2) * 2 + xl2) * 8 + z2)
                    )
    return lax.ppermute(x, PLANE, pairs)


def hop(x, axis):
    return lax.ppermute(x, axis, [(0, 1), (1, 0)])


OUTER_Z = (0, -1, 1, -2, 2, -3, 3, -4)
OUTER_W = ((0, 0), (-1, 0), (1, 0), (0, 1), (2, 0), (-1, 1), (1, 1), (2, 1))


def outer_slots(which):
    y, xl, z = lax.axis_index("y"), lax.axis_index("xl"), lax.axis_index("z")
    out = []
    for i in which:
        dz, (dy, flip) = OUTER_Z[i], OUTER_W[i]
        other = jnp.where(xl == flip, 0, 1)
        along_w = lax.rem(y + dy + 4, 4) * 2 + other
        out.append(jnp.where(lax.axis_index("core") == 1, lax.rem(z + dz + 8, 8), along_w))
    return out


def stack_kernel(orders, *refs):
    out, rows = refs[-1], refs[0].shape[0]
    for core, order in enumerate(orders):

        @pl.when(lax.axis_index("core") == core)
        def _(order=order):
            for i, which in enumerate(order):
                out[i * rows : (i + 1) * rows, :] = refs[which][...]


def stacked(parts, orders):
    rows, columns = parts[0].shape
    return pl.pallas_call(
        functools.partial(stack_kernel, orders),
        out_shape=jax.ShapeDtypeStruct((4 * rows, columns), parts[0].dtype),
        in_specs=[VMEM] * len(parts),
        out_specs=VMEM,
        compiler_params=params(8),
        cost_estimate=cost(0, 16 * rows * columns),
        name="stack",
    )(*parts)


def norm_kernel(hidden_ref, gain_ref, out_ref):
    values = hidden_ref[...].astype(jnp.float32)
    factor = lax.rsqrt(jnp.mean(values * values, axis=-1, keepdims=True) + 1e-06)
    out_ref[...] = (values * factor * gain_ref[...]).astype(jnp.bfloat16)


def normalize(hidden, gain):
    rows, width = hidden.shape
    return pl.pallas_call(
        norm_kernel,
        out_shape=jax.ShapeDtypeStruct((rows, width), jnp.bfloat16),
        in_specs=[VMEM, VMEM],
        out_specs=VMEM,
        compiler_params=params(8),
        cost_estimate=cost(6 * rows * width, 4 * rows * width),
        name="norm",
    )(hidden, gain)


def rows_kernel(own_ref, near_ref, far_ref, far_near_ref, out):
    xh, core = lax.axis_index("xh"), lax.axis_index("core")
    y, xl, z = lax.axis_index("y"), lax.axis_index("xl"), lax.axis_index("z")
    slots = [xh * 2 + core, xh * 2 + 1 - core, 2 - 2 * xh + core, 3 - 2 * xh - core]
    refs = [own_ref, near_ref, far_ref, far_near_ref]
    rows = own_ref.shape[0]
    tile = lambda ref, at: ref[:, pl.ds(pl.multiple_of(at, 128), 128)]
    start = lax.rem(z + 6, 8) // 2

    for slot, ref in zip(slots, refs, strict=True):
        at = pl.ds(pl.multiple_of(slot * rows, rows), rows)

        @pl.when((core == 0) & (lax.rem(z, 2) == 0))
        def _(at=at, ref=ref):
            for w in range(8):
                for k in range(4):
                    to = w * 512 + k * 128
                    out[at, to : to + 128] = tile(ref, w * 512 + lax.rem(start + k, 4) * 128)

        @pl.when((core == 0) & (lax.rem(z, 2) == 1))
        def _(at=at, ref=ref):
            for w in range(8):
                for k in range(4):
                    one = tile(ref, w * 512 + lax.rem(start + k, 4) * 128)[:, 64:]
                    two = tile(ref, w * 512 + lax.rem(start + k + 1, 4) * 128)[:, :64]
                    to = w * 512 + k * 128
                    out[at, to : to + 128] = jnp.concatenate([one, two], axis=1)

        @pl.when(core == 1)
        def _(at=at, ref=ref):
            for k in range(4):
                side = xl if k < 2 else 1 - xl
                base = [(lax.rem(y + 2 * (k % 2) + i, 4) * 2 + side) * 512 for i in range(2)]
                for z_at in range(8):
                    half = slice(64 * (z_at % 2), 64 * (z_at % 2) + 64)
                    one, two = [tile(ref, b + z_at // 2 * 128)[:, half] for b in base]
                    to = z_at * 512 + k * 128
                    out[at, to : to + 128] = jnp.concatenate([one, two], axis=1)


def gather_rows(parts):
    rows, width = parts[0].shape
    return pl.pallas_call(
        rows_kernel,
        out_shape=jax.ShapeDtypeStruct((4 * rows, width), parts[0].dtype),
        in_specs=[VMEM] * 4,
        out_specs=VMEM,
        compiler_params=params(16),
        cost_estimate=cost(0, 16 * rows * width),
        name="rows",
    )(*parts)


def project_kernel(states_ref, w_ref, out_ref):
    for i in range(out_ref.shape[0]):
        out_ref[i] = jnp.dot(
            states_ref[i], w_ref[0], preferred_element_type=jnp.float32
        ).astype(jnp.bfloat16)


def project(states, w, which, half):
    spans, keys, depth = states.shape
    columns = w.shape[2] // 2
    whole = lambda i: (0, 0, 0)
    return pl.pallas_call(
        project_kernel,
        grid=(1,),
        out_shape=jax.ShapeDtypeStruct((spans, keys, columns), jnp.bfloat16),
        in_specs=[
            pl.BlockSpec(states.shape, whole, pipeline_mode=pl.Buffered(1)),
            pl.BlockSpec((1, depth, columns), lambda i: (which, 0, half), pipeline_mode=pl.Buffered(1)),
        ],
        out_specs=pl.BlockSpec((spans, keys, columns), whole, pipeline_mode=pl.Buffered(1)),
        compiler_params=params(16),
        cost_estimate=cost(2 * spans * keys * depth * columns, 6 * MIB),
        name="project",
    )(states, w)


def project_prev_kernel(mine_ref, other_ref, w_ref, out_ref):
    core, rows = lax.axis_index("core"), mine_ref.shape[0]
    for which in range(2):
        for slot, ref in ((core, mine_ref), (1 - core, other_ref)):
            out_ref[which, pl.ds(pl.multiple_of(slot * rows, rows), rows), :] = jnp.dot(
                ref[...], w_ref[which], preferred_element_type=jnp.float32
            ).astype(jnp.bfloat16)


def project_prev(mine, other, w):
    rows, depth = mine.shape
    columns = w.shape[2]
    return pl.pallas_call(
        project_prev_kernel,
        out_shape=jax.ShapeDtypeStruct((2, 2 * rows, columns), jnp.bfloat16),
        in_specs=[VMEM] * 3,
        out_specs=VMEM,
        compiler_params=params(12),
        cost_estimate=cost(8 * rows * depth * columns, 6 * MIB),
        name="project_prev",
    )(mine, other, w)


def products(n_ref, refs, places):
    total = None
    for ref, place in zip(refs, places, strict=True):
        lanes = pl.ds(pl.multiple_of(place, 128), ref.shape[0])
        term = jnp.dot(n_ref[:, lanes], ref[...], preferred_element_type=jnp.float32)
        total = term if total is None else total + term
    return total


def partial_product(n, terms, before=None):
    pieces = [piece for _, _, some in terms for piece in some]
    rows, columns = n.shape[0], pieces[0].shape[1]
    depth = sum(p.shape[0] for p in pieces)
    extra = [] if before is None else [before]

    def body(n_ref, *refs):
        places = [slot * 512 + start for start, which, _ in terms for slot in outer_slots(which)]
        total = products(n_ref, refs[: len(pieces)], places)
        if extra:
            total = total + refs[len(pieces)][...]
        refs[-1][...] = total

    return pl.pallas_call(
        body,
        out_shape=jax.ShapeDtypeStruct((rows, columns), jnp.float32),
        in_specs=[VMEM] * (1 + len(pieces) + len(extra)),
        out_specs=VMEM,
        compiler_params=params(20),
        cost_estimate=cost(2 * rows * depth * columns, 2 * depth * (rows + columns)),
        name="partial",
    )(n, *pieces, *extra)


def attend(lens, segments, total, n, pieces, prev, keys, values):
    rows, columns = total.shape
    blocks = keys[0].shape[0] + 1
    heads = columns // HEAD_DIM // 2
    half = columns // 2

    def body(lens_ref, seg_ref, total_ref, n_ref, *refs):
        piece_refs, prev_ref, k_refs, v_refs = refs[:4], refs[4], refs[5:7], refs[7:9]
        out_ref, q_scr, c_scr, s_scr, w_scr = refs[9:]
        seq = (lax.axis_index("y") * 2 + lax.axis_index("xl")) * 8 + lax.axis_index("z")
        (slot,) = outer_slots([7])
        places = [slot * 512 + i * 128 for i in range(4)]
        acc = total_ref[...] + products(n_ref, piece_refs, places)
        acc = acc * HEAD_DIM ** (-0.5)
        acc = jnp.concatenate([acc, jnp.zeros((SPAN, columns), jnp.float32)], axis=0)
        q_scr[...] = pltpu.roll(acc, 1, 0).astype(jnp.bfloat16)
        lane = lax.broadcasted_iota(jnp.int32, (1, 128), 1)
        wide = lax.broadcasted_iota(jnp.int32, (1, 2 * NBR_LEN), 1)
        row = lax.broadcasted_iota(jnp.int32, (SPAN, HEAD_DIM), 0)
        usable, live = [], []
        for b in range(blocks):
            span = jnp.maximum(seq * (blocks - 1) + b - 1, 0)
            usable.append(
                wide < jnp.where(wide < NBR_LEN, lens_ref[0, span], lens_ref[1, span] + NBR_LEN)
            )
            line = seg_ref[pl.ds(span // 2, 1), :]
            if b % 2:
                same = (line == line[:, 63:64]) & (lane >= 63) & (lane < 127)
                count = jnp.sum(same.astype(jnp.int32), axis=1, keepdims=True)
            else:
                after = seg_ref[pl.ds(jnp.minimum(span // 2 + 1, seg_ref.shape[0] - 1), 1), :]
                same = (after == line[:, 127:128]) & (lane < 63)
                count = jnp.sum(same.astype(jnp.int32), axis=1, keepdims=True) + 1
            if b == 0:
                count = jnp.where(seq == 0, 0, count)
            live.append(row < count)
        for part in range(2):
            for h in range(heads):
                at = slice(h * HEAD_DIM, (h + 1) * HEAD_DIM)
                to = slice(part * half + h * HEAD_DIM, part * half + (h + 1) * HEAD_DIM)
                for b in range(blocks):
                    scores = lax.dot_general(
                        q_scr[b * SPAN : (b + 1) * SPAN, to],
                        k_refs[part][b - 1, :, at] if b else prev_ref[0, :, to],
                        (((1,), (1,)), ((), ())),
                        preferred_element_type=jnp.float32,
                    )
                    s_scr[h, b * SPAN : (b + 1) * SPAN, :] = jnp.where(usable[b], scores, jnp.float32(-1e30))
            for h in range(heads):
                for c in range(blocks // 3):
                    r = slice(c * 3 * SPAN, (c + 1) * 3 * SPAN)
                    scores = s_scr[h, r, :]
                    weights = jnp.exp(scores - jnp.max(scores, axis=-1, keepdims=True))
                    scale = 1.0 / jnp.sum(weights, axis=-1, keepdims=True)
                    w_scr[h, r, :] = (weights * scale).astype(jnp.bfloat16)
            for h in range(heads):
                at = slice(h * HEAD_DIM, (h + 1) * HEAD_DIM)
                to = slice(part * half + h * HEAD_DIM, part * half + (h + 1) * HEAD_DIM)
                for b in range(blocks):
                    mixed = jnp.dot(
                        w_scr[h, b * SPAN : (b + 1) * SPAN, :],
                        v_refs[part][b - 1, :, at] if b else prev_ref[1, :, to],
                        preferred_element_type=jnp.float32,
                    )
                    c_scr[b * SPAN : (b + 1) * SPAN, to] = jnp.where(live[b], mixed, 0.0)
        moved = pltpu.roll(c_scr[...], blocks * SPAN - 1, 0)
        out_ref[...] = moved[:rows].astype(jnp.bfloat16)

    return pl.pallas_call(
        body,
        out_shape=jax.ShapeDtypeStruct((rows, columns), jnp.bfloat16),
        in_specs=[SMEM] + [VMEM] * 12,
        out_specs=VMEM,
        scratch_shapes=[
            pltpu.VMEM((blocks * SPAN, columns), jnp.bfloat16),
            pltpu.VMEM((blocks * SPAN, columns), jnp.float32),
            pltpu.VMEM((heads, blocks * SPAN, 2 * NBR_LEN), jnp.float32),
            pltpu.VMEM((heads, blocks * SPAN, 2 * NBR_LEN), jnp.bfloat16),
        ],
        compiler_params=params(28),
        cost_estimate=cost(6 * MIB * 1000, 16 * MIB),
        name="attend",
    )(lens, segments, total, n, *pieces, prev, *keys, *values)


def after(value, *others):
    return lax.optimization_barrier((value, *others))[0]


def local(hidden, norm_gain, w_query, w_keyval, nbr_states, nbr_lens, segment_ids):
    core = lax.axis_index("core")

    def pick(zero, one):
        return jnp.where(core == 0, zero, one)

    def outer_first(column):
        return [send(column, (1, 0), (1, "z")), send(column, (-1, 0), (-1, "z"))]

    def outer_second(column, one, two, *first):
        one, two = after(one, *first), after(two, *first)
        return [send(pick(column, one), (0, 1), (1, "z")), send(two, (-1, 0), (-1, "z"))]

    def outer_third(three, four, *first):
        three, four = after(three, *first), after(four, *first)
        return [send(three, (1, 0), (1, "z")), send(pick(three, four), (-1, 0), (-1, "z"))]

    def outer_last(five, six, *first):
        r = five.shape[0] // 2
        five, six = after(five, *first), after(six, *first)
        return [send(five[:r], (1, 0), (1, "z")), send(six[r:], (-1, 0), (-1, "z"))]

    def projected(which, part, *first):
        return project(after(nbr_states, *first), w_keyval, which, part)

    round_one = [
        send(w_query, (1, "z"), (0, 1)),
        send(w_query, (-1, "z"), (1, 0)),
        send(w_query, (2, "z"), (-1, 0)),
        send(w_query, (-2, "z"), (2, 0)),
    ]
    normed = normalize(hidden, norm_gain[None])
    near = hop(normed, "core")
    far = hop(normed, "xh")
    column_a = stacked([w_query, *round_one], ((3, 1, 0, 2), (0, 3, 4, 2)))
    head = after(pick(round_one[3], round_one[0]), normed)
    round_two = [
        send(head, (-1, "z"), (-1, 0)),
        send(head, (-2, "z"), (2, 0)),
        send(pick(round_one[2], round_one[0]), (1, "z"), (1, 0)),
    ]
    column_b = stacked([head, *round_two], ((0, 1, 2, 3), (0, 1, 2, 3)))

    a = [column_a, *outer_first(column_a)]
    half = nbr_states.shape[1] // 2
    prev = lax.dynamic_slice_in_dim(nbr_states[-1], core * half, half, 0)
    prev = lax.ppermute(after(prev, column_a), ("y", "xl", "z"), [(i, i + 1) for i in range(63)])
    keys_a = projected(0, 0, column_a)
    b = [column_b, *outer_first(column_b)]
    a += outer_second(*a, keys_a)
    values_a = projected(1, 0, *a[1:3])
    b += outer_second(*b, values_a, prev)
    prev_near = hop(prev, "core")
    keys_b = projected(0, 1, *b[1:3])
    far_near = hop(after(far, keys_b), "core")
    a += outer_third(*a[3:5], keys_b)
    values_b = projected(1, 1, *a[3:5])
    prev = project_prev(after(prev, values_b), prev_near, w_keyval)
    whole = gather_rows([after(normed, prev), near, far, far_near])
    b += outer_third(*b[3:5], whole)
    total = partial_product(after(whole, *b[3:5]), [(0, [0, 1, 2], a[:3])])
    a += outer_last(*a[5:7], total)
    total = partial_product(
        after(whole, *a[5:7]), [(256, [0, 1, 2], b[:3]), (0, [3, 4], a[3:5])], total
    )
    b += outer_last(*b[5:7], total)
    total = partial_product(
        after(whole, *b[5:7]),
        [(256, [3, 4], b[3:5]), (0, [5, 6], a[5:7]), (256, [5, 6], b[5:7])],
        total,
    )
    return attend(
        nbr_lens.T,
        segment_ids.reshape(-1, 128),
        total,
        whole,
        [*a[7:], *b[7:]],
        prev,
        [keys_a, keys_b],
        [values_a, values_b],
    )


def solution(mesh):
    fine = Mesh(mesh.devices.reshape(tuple(SIZES.values())), tuple(SIZES))
    section, seq = ("xh", "core"), ("y", "xl", "z")
    in_specs = (
        P(seq + section, None),
        P(),
        P(seq, section),
        P(None, None, section),
        P(seq, None, None),
        P(),
        P(),
    )
    out_specs = P(seq, section)
    return jax.shard_map(local, mesh=fine, in_specs=in_specs, out_specs=out_specs, check_vma=False)
```

```python
import functools

import jax
import jax.numpy as jnp
from jax import lax
from jax.experimental import pallas as pl
from jax.experimental.pallas import tpu as pltpu
from jax.sharding import Mesh, PartitionSpec as P

HEAD_DIM = 128
SPAN = 64
NBR_LEN = 128
SIZES = {"xh": 2, "core": 2, "y": 4, "xl": 2, "z": 8}
PLANE = ("core", "y", "xl", "z")
VMEM = pl.BlockSpec(memory_space=pltpu.VMEM)
SMEM = pl.BlockSpec(memory_space=pltpu.SMEM)
MIB = 1 << 20


def params(mib):
    return pltpu.CompilerParams(vmem_limit_bytes=mib * MIB)


def cost(flops, moved):
    return pl.CostEstimate(flops=flops // 100, bytes_accessed=moved // 100, transcendentals=0)


def moved(move, y, xl, z):
    by, how = move
    if how == "z":
        return y, xl, (z + by) % 8
    return (y + by) % 4, xl ^ how, z


def send(x, first, second):
    pairs = []
    for core, move in enumerate((first, second)):
        for y in range(4):
            for xl in range(2):
                for z in range(8):
                    y2, xl2, z2 = moved(move, y, xl, z)
                    pairs.append(
                        (((core * 4 + y) * 2 + xl) * 8 + z, ((core * 4 + y2) * 2 + xl2) * 8 + z2)
                    )
    return lax.ppermute(x, PLANE, pairs)


def hop(x, axis):
    return lax.ppermute(x, axis, [(0, 1), (1, 0)])


OUTER_Z = (0, -1, 1, -2, 2, -3, 3, -4)
OUTER_W = ((0, 0), (-1, 0), (1, 0), (0, 1), (2, 0), (-1, 1), (1, 1), (2, 1))


def outer_slots(which):
    y, xl, z = lax.axis_index("y"), lax.axis_index("xl"), lax.axis_index("z")
    out = []
    for i in which:
        dz, (dy, flip) = OUTER_Z[i], OUTER_W[i]
        other = jnp.where(xl == flip, 0, 1)
        along_w = lax.rem(y + dy + 4, 4) * 2 + other
        out.append(jnp.where(lax.axis_index("core") == 1, lax.rem(z + dz + 8, 8), along_w))
    return out


def stack_kernel(orders, *refs):
    out, rows = refs[-1], refs[0].shape[0]
    for core, order in enumerate(orders):

        @pl.when(lax.axis_index("core") == core)
        def _(order=order):
            for i, which in enumerate(order):
                out[i * rows : (i + 1) * rows, :] = refs[which][...]


def stacked(parts, orders):
    rows, columns = parts[0].shape
    return pl.pallas_call(
        functools.partial(stack_kernel, orders),
        out_shape=jax.ShapeDtypeStruct((4 * rows, columns), parts[0].dtype),
        in_specs=[VMEM] * len(parts),
        out_specs=VMEM,
        compiler_params=params(8),
        cost_estimate=cost(0, 16 * rows * columns),
        name="stack",
    )(*parts)


def norm_kernel(hidden_ref, gain_ref, out_ref):
    values = hidden_ref[...].astype(jnp.float32)
    factor = lax.rsqrt(jnp.mean(values * values, axis=-1, keepdims=True) + 1e-06)
    out_ref[...] = (values * factor * gain_ref[...]).astype(jnp.bfloat16)


def normalize(hidden, gain):
    rows, width = hidden.shape
    return pl.pallas_call(
        norm_kernel,
        out_shape=jax.ShapeDtypeStruct((rows, width), jnp.bfloat16),
        in_specs=[VMEM, VMEM],
        out_specs=VMEM,
        compiler_params=params(8),
        cost_estimate=cost(6 * rows * width, 4 * rows * width),
        name="norm",
    )(hidden, gain)


def rows_kernel(own_ref, near_ref, far_ref, far_near_ref, out):
    xh, core = lax.axis_index("xh"), lax.axis_index("core")
    y, xl, z = lax.axis_index("y"), lax.axis_index("xl"), lax.axis_index("z")
    slots = [xh * 2 + core, xh * 2 + 1 - core, 2 - 2 * xh + core, 3 - 2 * xh - core]
    refs = [own_ref, near_ref, far_ref, far_near_ref]
    rows = own_ref.shape[0]
    part = 32
    start = lax.rem(z + 6, 8) // 2

    for slot, ref in zip(slots, refs, strict=True):

        def one(i, _, slot=slot, ref=ref):
            here = pl.ds(pl.multiple_of(i * part, part), part)
            at = pl.ds(pl.multiple_of(slot * rows + i * part, part), part)

            def tile(lane):
                return ref[here, pl.ds(pl.multiple_of(lane, 128), 128)]

            @pl.when((core == 0) & (lax.rem(z, 2) == 0))
            def _():
                for w in range(8):
                    for k in range(4):
                        to = w * 512 + k * 128
                        out[at, to : to + 128] = tile(w * 512 + lax.rem(start + k, 4) * 128)

            @pl.when((core == 0) & (lax.rem(z, 2) == 1))
            def _():
                for w in range(8):
                    for k in range(4):
                        one = tile(w * 512 + lax.rem(start + k, 4) * 128)[:, 64:]
                        two = tile(w * 512 + lax.rem(start + k + 1, 4) * 128)[:, :64]
                        to = w * 512 + k * 128
                        out[at, to : to + 128] = jnp.concatenate([one, two], axis=1)

            @pl.when(core == 1)
            def _():
                for k in range(4):
                    side = xl if k < 2 else 1 - xl
                    base = [(lax.rem(y + 2 * (k % 2) + j, 4) * 2 + side) * 512 for j in range(2)]
                    for z_at in range(8):
                        half = slice(64 * (z_at % 2), 64 * (z_at % 2) + 64)
                        one, two = [tile(b + z_at // 2 * 128)[:, half] for b in base]
                        to = z_at * 512 + k * 128
                        out[at, to : to + 128] = jnp.concatenate([one, two], axis=1)

        lax.fori_loop(0, rows // part, one, None)


def gather_rows(parts):
    rows, width = parts[0].shape
    return pl.pallas_call(
        rows_kernel,
        out_shape=jax.ShapeDtypeStruct((4 * rows, width), parts[0].dtype),
        in_specs=[VMEM] * 4,
        out_specs=VMEM,
        compiler_params=params(16),
        cost_estimate=cost(0, 16 * rows * width),
        name="rows",
    )(*parts)


def project_kernel(states_ref, w_ref, out_ref):
    def one(i, _):
        out_ref[i] = jnp.dot(
            states_ref[i], w_ref[0], preferred_element_type=jnp.float32
        ).astype(jnp.bfloat16)

    lax.fori_loop(0, out_ref.shape[0], one, None)


def project(states, w, which, half):
    spans, keys, depth = states.shape
    columns = w.shape[2] // 2
    whole = lambda i: (0, 0, 0)
    return pl.pallas_call(
        project_kernel,
        grid=(1,),
        out_shape=jax.ShapeDtypeStruct((spans, keys, columns), jnp.bfloat16),
        in_specs=[
            pl.BlockSpec(states.shape, whole, pipeline_mode=pl.Buffered(1)),
            pl.BlockSpec((1, depth, columns), lambda i: (which, 0, half), pipeline_mode=pl.Buffered(1)),
        ],
        out_specs=pl.BlockSpec((spans, keys, columns), whole, pipeline_mode=pl.Buffered(1)),
        compiler_params=params(16),
        cost_estimate=cost(2 * spans * keys * depth * columns, 6 * MIB),
        name="project",
    )(states, w)


def project_prev_kernel(mine_ref, other_ref, w_ref, out_ref):
    core, rows = lax.axis_index("core"), mine_ref.shape[0]
    for which in range(2):
        for slot, ref in ((core, mine_ref), (1 - core, other_ref)):
            out_ref[which, pl.ds(pl.multiple_of(slot * rows, rows), rows), :] = jnp.dot(
                ref[...], w_ref[which], preferred_element_type=jnp.float32
            ).astype(jnp.bfloat16)


def project_prev(mine, other, w):
    rows, depth = mine.shape
    columns = w.shape[2]
    return pl.pallas_call(
        project_prev_kernel,
        out_shape=jax.ShapeDtypeStruct((2, 2 * rows, columns), jnp.bfloat16),
        in_specs=[VMEM] * 3,
        out_specs=VMEM,
        compiler_params=params(12),
        cost_estimate=cost(8 * rows * depth * columns, 6 * MIB),
        name="project_prev",
    )(mine, other, w)


def products(n_ref, refs, places):
    total = None
    for ref, place in zip(refs, places, strict=True):
        lanes = pl.ds(pl.multiple_of(place, 128), ref.shape[0])
        term = jnp.dot(n_ref[:, lanes], ref[...], preferred_element_type=jnp.float32)
        total = term if total is None else total + term
    return total


def partial_product(n, terms, before=None):
    pieces = [piece for _, _, some in terms for piece in some]
    rows, columns = n.shape[0], pieces[0].shape[1]
    depth = sum(p.shape[0] for p in pieces)
    extra = [] if before is None else [before]

    def body(n_ref, *refs):
        places = [slot * 512 + start for start, which, _ in terms for slot in outer_slots(which)]
        total = products(n_ref, refs[: len(pieces)], places)
        if extra:
            total = total + refs[len(pieces)][...]
        refs[-1][...] = total

    return pl.pallas_call(
        body,
        out_shape=jax.ShapeDtypeStruct((rows, columns), jnp.float32),
        in_specs=[VMEM] * (1 + len(pieces) + len(extra)),
        out_specs=VMEM,
        compiler_params=params(20),
        cost_estimate=cost(2 * rows * depth * columns, 2 * depth * (rows + columns)),
        name="partial",
    )(n, *pieces, *extra)


def attend(lens, segments, total, n, pieces, prev, keys, values):
    rows, columns = total.shape
    blocks = keys[0].shape[0] + 1
    heads = columns // HEAD_DIM // 2
    half = columns // 2

    def body(lens_ref, seg_ref, total_ref, n_ref, *refs):
        piece_refs, prev_ref, k_refs, v_refs = refs[:4], refs[4], refs[5:7], refs[7:9]
        out_ref, q_scr, c_scr, s_scr, w_scr = refs[9:]
        seq = (lax.axis_index("y") * 2 + lax.axis_index("xl")) * 8 + lax.axis_index("z")
        (slot,) = outer_slots([7])
        places = [slot * 512 + i * 128 for i in range(4)]
        acc = total_ref[...] + products(n_ref, piece_refs, places)
        acc = acc * HEAD_DIM ** (-0.5)
        acc = jnp.concatenate([acc, jnp.zeros((SPAN, columns), jnp.float32)], axis=0)
        q_scr[...] = pltpu.roll(acc, 1, 0).astype(jnp.bfloat16)
        lane = lax.broadcasted_iota(jnp.int32, (1, 128), 1)
        wide = lax.broadcasted_iota(jnp.int32, (1, 2 * NBR_LEN), 1)
        row = lax.broadcasted_iota(jnp.int32, (SPAN, HEAD_DIM), 0)
        usable, live = [], []
        for b in range(blocks):
            span = jnp.maximum(seq * (blocks - 1) + b - 1, 0)
            usable.append(
                wide < jnp.where(wide < NBR_LEN, lens_ref[0, span], lens_ref[1, span] + NBR_LEN)
            )
            line = seg_ref[pl.ds(span // 2, 1), :]
            if b % 2:
                same = (line == line[:, 63:64]) & (lane >= 63) & (lane < 127)
                count = jnp.sum(same.astype(jnp.int32), axis=1, keepdims=True)
            else:
                after = seg_ref[pl.ds(jnp.minimum(span // 2 + 1, seg_ref.shape[0] - 1), 1), :]
                same = (after == line[:, 127:128]) & (lane < 63)
                count = jnp.sum(same.astype(jnp.int32), axis=1, keepdims=True) + 1
            if b == 0:
                count = jnp.where(seq == 0, 0, count)
            live.append(row < count)
        for part in range(2):
            for h in range(heads):
                at = slice(h * HEAD_DIM, (h + 1) * HEAD_DIM)
                to = slice(part * half + h * HEAD_DIM, part * half + (h + 1) * HEAD_DIM)
                for b in range(blocks):
                    scores = lax.dot_general(
                        q_scr[b * SPAN : (b + 1) * SPAN, to],
                        k_refs[part][b - 1, :, at] if b else prev_ref[0, :, to],
                        (((1,), (1,)), ((), ())),
                        preferred_element_type=jnp.float32,
                    )
                    s_scr[h, b * SPAN : (b + 1) * SPAN, :] = jnp.where(usable[b], scores, jnp.float32(-1e30))
            for h in range(heads):
                for c in range(blocks // 3):
                    r = slice(c * 3 * SPAN, (c + 1) * 3 * SPAN)
                    scores = s_scr[h, r, :]
                    weights = jnp.exp(scores - jnp.max(scores, axis=-1, keepdims=True))
                    scale = 1.0 / jnp.sum(weights, axis=-1, keepdims=True)
                    w_scr[h, r, :] = (weights * scale).astype(jnp.bfloat16)
            for h in range(heads):
                at = slice(h * HEAD_DIM, (h + 1) * HEAD_DIM)
                to = slice(part * half + h * HEAD_DIM, part * half + (h + 1) * HEAD_DIM)
                for b in range(blocks):
                    mixed = jnp.dot(
                        w_scr[h, b * SPAN : (b + 1) * SPAN, :],
                        v_refs[part][b - 1, :, at] if b else prev_ref[1, :, to],
                        preferred_element_type=jnp.float32,
                    )
                    c_scr[b * SPAN : (b + 1) * SPAN, to] = jnp.where(live[b], mixed, 0.0)
        moved = pltpu.roll(c_scr[...], blocks * SPAN - 1, 0)
        out_ref[...] = moved[:rows].astype(jnp.bfloat16)

    return pl.pallas_call(
        body,
        out_shape=jax.ShapeDtypeStruct((rows, columns), jnp.bfloat16),
        in_specs=[SMEM] + [VMEM] * 12,
        out_specs=VMEM,
        scratch_shapes=[
            pltpu.VMEM((blocks * SPAN, columns), jnp.bfloat16),
            pltpu.VMEM((blocks * SPAN, columns), jnp.float32),
            pltpu.VMEM((heads, blocks * SPAN, 2 * NBR_LEN), jnp.float32),
            pltpu.VMEM((heads, blocks * SPAN, 2 * NBR_LEN), jnp.bfloat16),
        ],
        compiler_params=params(28),
        cost_estimate=cost(6 * MIB * 1000, 16 * MIB),
        name="attend",
    )(lens, segments, total, n, *pieces, prev, *keys, *values)


def after(value, *others):
    return lax.optimization_barrier((value, *others))[0]


def local(hidden, norm_gain, w_query, w_keyval, nbr_states, nbr_lens, segment_ids):
    core = lax.axis_index("core")

    def pick(zero, one):
        return jnp.where(core == 0, zero, one)

    def outer_first(column):
        return [send(column, (1, 0), (1, "z")), send(column, (-1, 0), (-1, "z"))]

    def outer_second(column, one, two, *first):
        one, two = after(one, *first), after(two, *first)
        return [send(pick(column, one), (0, 1), (1, "z")), send(two, (-1, 0), (-1, "z"))]

    def outer_third(three, four, *first):
        three, four = after(three, *first), after(four, *first)
        return [send(three, (1, 0), (1, "z")), send(pick(three, four), (-1, 0), (-1, "z"))]

    def outer_last(five, six, *first):
        r = five.shape[0] // 2
        five, six = after(five, *first), after(six, *first)
        return [send(five[:r], (1, 0), (1, "z")), send(six[r:], (-1, 0), (-1, "z"))]

    def projected(which, part, *first):
        return project(after(nbr_states, *first), w_keyval, which, part)

    round_one = [
        send(w_query, (1, "z"), (0, 1)),
        send(w_query, (-1, "z"), (1, 0)),
        send(w_query, (2, "z"), (-1, 0)),
        send(w_query, (-2, "z"), (2, 0)),
    ]
    normed = normalize(hidden, norm_gain[None])
    near = hop(after(normed, *round_one), "core")
    far = hop(normed, "xh")
    column_a = stacked([w_query, *round_one], ((3, 1, 0, 2), (0, 3, 4, 2)))
    head = after(pick(round_one[3], round_one[0]), normed)
    round_two = [
        send(head, (-1, "z"), (-1, 0)),
        send(head, (-2, "z"), (2, 0)),
        send(pick(round_one[2], round_one[0]), (1, "z"), (1, 0)),
    ]
    a = [column_a, *outer_first(column_a)]
    keys_a = projected(0, 0, column_a)
    column_b = stacked([after(head, keys_a), *round_two], ((0, 1, 2, 3), (0, 1, 2, 3)))
    half = nbr_states.shape[1] // 2
    prev = lax.dynamic_slice_in_dim(nbr_states[-1], core * half, half, 0)
    prev = lax.ppermute(after(prev, column_b), ("y", "xl", "z"), [(i, i + 1) for i in range(63)])
    b = [column_b, *outer_first(after(column_b, near))]
    a += outer_second(*a)
    values_a = projected(1, 0, *a[1:3])
    b += outer_second(*b, values_a)
    keys_b = projected(0, 1, *b[1:3])
    far_near = hop(after(far, *a[3:5]), "core")
    a += outer_third(*a[3:5], keys_b)
    values_b = projected(1, 1, *a[3:5])
    prev_near = hop(after(prev, values_b), "core")
    b += outer_third(*b[3:5], values_b, prev)
    whole = gather_rows([after(normed, values_b), near, far, far_near])
    total = partial_product(whole, [(0, [0, 1, 2], a[:3])])
    a += outer_last(*a[5:7])
    prev = project_prev(after(prev, total), prev_near, w_keyval)
    total = partial_product(
        after(whole, *a[5:7]), [(256, [0, 1, 2], b[:3]), (0, [3, 4], a[3:5])], total
    )
    b += outer_last(*b[5:7], total)
    total = partial_product(
        after(whole, *b[5:7]),
        [(256, [3, 4], b[3:5]), (0, [5, 6], a[5:7]), (256, [5, 6], b[5:7])],
        total,
    )
    return attend(
        nbr_lens.T,
        segment_ids.reshape(-1, 128),
        total,
        whole,
        [*a[7:], *b[7:]],
        prev,
        [keys_a, keys_b],
        [values_a, values_b],
    )


def solution(mesh):
    fine = Mesh(mesh.devices.reshape(tuple(SIZES.values())), tuple(SIZES))
    section, seq = ("xh", "core"), ("y", "xl", "z")
    in_specs = (
        P(seq + section, None),
        P(),
        P(seq, section),
        P(None, None, section),
        P(seq, None, None),
        P(),
        P(),
    )
    out_specs = P(seq, section)
    return jax.shard_map(local, mesh=fine, in_specs=in_specs, out_specs=out_specs, check_vma=False)
```

```python
import functools

import jax
import jax.numpy as jnp
from jax import lax
from jax.experimental import pallas as pl
from jax.experimental.pallas import tpu as pltpu
from jax.sharding import Mesh, PartitionSpec as P

HEAD_DIM = 128
SPAN = 64
NBR_LEN = 128
SIZES = {"xh": 2, "core": 2, "y": 4, "xl": 2, "z": 8}
PLANE = ("core", "y", "xl", "z")
VMEM = pl.BlockSpec(memory_space=pltpu.VMEM)
SMEM = pl.BlockSpec(memory_space=pltpu.SMEM)
MIB = 1 << 20


def params(mib):
    return pltpu.CompilerParams(vmem_limit_bytes=mib * MIB)


def cost(flops, moved, exps=0):
    return pl.CostEstimate(flops=flops, bytes_accessed=moved, transcendentals=exps)


def moved(move, y, xl, z):
    by, how = move
    if how == "z":
        return y, xl, (z + by) % 8
    return (y + by) % 4, xl ^ how, z


def send(x, first, second):
    pairs = []
    for core, move in enumerate((first, second)):
        for y in range(4):
            for xl in range(2):
                for z in range(8):
                    y2, xl2, z2 = moved(move, y, xl, z)
                    pairs.append(
                        (((core * 4 + y) * 2 + xl) * 8 + z, ((core * 4 + y2) * 2 + xl2) * 8 + z2)
                    )
    return lax.ppermute(x, PLANE, pairs)


def hop(x, axis):
    return lax.ppermute(x, axis, [(0, 1), (1, 0)])


OUTER_Z = (0, -1, 1, -2, 2, -3, 3, -4)
OUTER_W = ((0, 0), (-1, 0), (1, 0), (0, 1), (2, 0), (-1, 1), (1, 1), (2, 1))


def outer_slots(which):
    y, xl, z = lax.axis_index("y"), lax.axis_index("xl"), lax.axis_index("z")
    out = []
    for i in which:
        dz, (dy, flip) = OUTER_Z[i], OUTER_W[i]
        other = jnp.where(xl == flip, 0, 1)
        along_w = lax.rem(y + dy + 4, 4) * 2 + other
        out.append(jnp.where(lax.axis_index("core") == 1, lax.rem(z + dz + 8, 8), along_w))
    return out


def stack_kernel(orders, *refs):
    out, rows = refs[-1], refs[0].shape[0]
    for core, order in enumerate(orders):

        @pl.when(lax.axis_index("core") == core)
        def _(order=order):
            for i, which in enumerate(order):
                out[i * rows : (i + 1) * rows, :] = refs[which][...]


def stacked(parts, orders):
    rows, columns = parts[0].shape
    return pl.pallas_call(
        functools.partial(stack_kernel, orders),
        out_shape=jax.ShapeDtypeStruct((4 * rows, columns), parts[0].dtype),
        in_specs=[VMEM] * len(parts),
        out_specs=VMEM,
        compiler_params=params(8),
        cost_estimate=cost(0, 16 * rows * columns),
        name="stack",
    )(*parts)


def norm_kernel(hidden_ref, gain_ref, out_ref):
    values = hidden_ref[...].astype(jnp.float32)
    factor = lax.rsqrt(jnp.mean(values * values, axis=-1, keepdims=True) + 1e-06)
    out_ref[...] = (values * factor * gain_ref[...]).astype(jnp.bfloat16)


def normalize(hidden, gain):
    rows, width = hidden.shape
    return pl.pallas_call(
        norm_kernel,
        out_shape=jax.ShapeDtypeStruct((rows, width), jnp.bfloat16),
        in_specs=[VMEM, VMEM],
        out_specs=VMEM,
        compiler_params=params(8),
        cost_estimate=cost(6 * rows * width, 4 * rows * width),
        name="norm",
    )(hidden, gain)


def rows_kernel(own_ref, near_ref, far_ref, far_near_ref, out):
    xh, core = lax.axis_index("xh"), lax.axis_index("core")
    y, xl, z = lax.axis_index("y"), lax.axis_index("xl"), lax.axis_index("z")
    slots = [xh * 2 + core, xh * 2 + 1 - core, 2 - 2 * xh + core, 3 - 2 * xh - core]
    refs = [own_ref, near_ref, far_ref, far_near_ref]
    rows = own_ref.shape[0]
    part = 32
    start = lax.rem(z + 6, 8) // 2

    for slot, ref in zip(slots, refs, strict=True):

        def one(i, _, slot=slot, ref=ref):
            here = pl.ds(pl.multiple_of(i * part, part), part)
            at = pl.ds(pl.multiple_of(slot * rows + i * part, part), part)

            def tile(lane):
                return ref[here, pl.ds(pl.multiple_of(lane, 128), 128)]

            @pl.when((core == 0) & (lax.rem(z, 2) == 0))
            def _():
                for w in range(8):
                    for k in range(4):
                        to = w * 512 + k * 128
                        out[at, to : to + 128] = tile(w * 512 + lax.rem(start + k, 4) * 128)

            @pl.when((core == 0) & (lax.rem(z, 2) == 1))
            def _():
                for w in range(8):
                    for k in range(4):
                        one = tile(w * 512 + lax.rem(start + k, 4) * 128)[:, 64:]
                        two = tile(w * 512 + lax.rem(start + k + 1, 4) * 128)[:, :64]
                        to = w * 512 + k * 128
                        out[at, to : to + 128] = jnp.concatenate([one, two], axis=1)

            @pl.when(core == 1)
            def _():
                for k in range(4):
                    side = xl if k < 2 else 1 - xl
                    base = [(lax.rem(y + 2 * (k % 2) + j, 4) * 2 + side) * 512 for j in range(2)]
                    for z_at in range(8):
                        half = slice(64 * (z_at % 2), 64 * (z_at % 2) + 64)
                        one, two = [tile(b + z_at // 2 * 128)[:, half] for b in base]
                        to = z_at * 512 + k * 128
                        out[at, to : to + 128] = jnp.concatenate([one, two], axis=1)

        lax.fori_loop(0, rows // part, one, None)


def gather_rows(parts):
    rows, width = parts[0].shape
    return pl.pallas_call(
        rows_kernel,
        out_shape=jax.ShapeDtypeStruct((4 * rows, width), parts[0].dtype),
        in_specs=[VMEM] * 4,
        out_specs=VMEM,
        compiler_params=params(16),
        cost_estimate=cost(0, 16 * rows * width),
        name="rows",
    )(*parts)


def project_kernel(states_ref, w_ref, out_ref):
    def one(i, _):
        out_ref[i] = jnp.dot(
            states_ref[i], w_ref[0], preferred_element_type=jnp.float32
        ).astype(jnp.bfloat16)

    lax.fori_loop(0, out_ref.shape[0], one, None)


def project(states, w, which, half):
    spans, keys, depth = states.shape
    columns = w.shape[2] // 2
    whole = lambda i: (0, 0, 0)
    return pl.pallas_call(
        project_kernel,
        grid=(1,),
        out_shape=jax.ShapeDtypeStruct((spans, keys, columns), jnp.bfloat16),
        in_specs=[
            pl.BlockSpec(states.shape, whole, pipeline_mode=pl.Buffered(1)),
            pl.BlockSpec((1, depth, columns), lambda i: (which, 0, half), pipeline_mode=pl.Buffered(1)),
        ],
        out_specs=pl.BlockSpec((spans, keys, columns), whole, pipeline_mode=pl.Buffered(1)),
        compiler_params=params(16),
        cost_estimate=cost(2 * spans * keys * depth * columns, 6 * MIB),
        name="project",
    )(states, w)


def project_prev_kernel(mine_ref, other_ref, w_ref, out_ref):
    core, rows = lax.axis_index("core"), mine_ref.shape[0]
    for which in range(2):
        for slot, ref in ((core, mine_ref), (1 - core, other_ref)):
            out_ref[which, pl.ds(pl.multiple_of(slot * rows, rows), rows), :] = jnp.dot(
                ref[...], w_ref[which], preferred_element_type=jnp.float32
            ).astype(jnp.bfloat16)


def project_prev(mine, other, w):
    rows, depth = mine.shape
    columns = w.shape[2]
    return pl.pallas_call(
        project_prev_kernel,
        out_shape=jax.ShapeDtypeStruct((2, 2 * rows, columns), jnp.bfloat16),
        in_specs=[VMEM] * 3,
        out_specs=VMEM,
        compiler_params=params(12),
        cost_estimate=cost(8 * rows * depth * columns, 6 * MIB),
        name="project_prev",
    )(mine, other, w)


def products(n_ref, refs, places):
    total = None
    for ref, place in zip(refs, places, strict=True):
        lanes = pl.ds(pl.multiple_of(place, 128), ref.shape[0])
        term = jnp.dot(n_ref[:, lanes], ref[...], preferred_element_type=jnp.float32)
        total = term if total is None else total + term
    return total


def partial_product(n, terms, before=None):
    pieces = [piece for _, _, some in terms for piece in some]
    rows, columns = n.shape[0], pieces[0].shape[1]
    depth = sum(p.shape[0] for p in pieces)
    extra = [] if before is None else [before]

    def body(n_ref, *refs):
        places = [slot * 512 + start for start, which, _ in terms for slot in outer_slots(which)]
        total = products(n_ref, refs[: len(pieces)], places)
        if extra:
            total = total + refs[len(pieces)][...]
        refs[-1][...] = total

    return pl.pallas_call(
        body,
        out_shape=jax.ShapeDtypeStruct((rows, columns), jnp.float32),
        in_specs=[VMEM] * (1 + len(pieces) + len(extra)),
        out_specs=VMEM,
        compiler_params=params(20),
        cost_estimate=cost(2 * rows * depth * columns, 2 * depth * (rows + columns)),
        name="partial",
    )(n, *pieces, *extra)


def attend(lens, segments, total, n, pieces, prev, keys, values):
    rows, columns = total.shape
    blocks = keys[0].shape[0] + 1
    heads = columns // HEAD_DIM // 2
    half = columns // 2

    def body(lens_ref, seg_ref, total_ref, n_ref, *refs):
        piece_refs, prev_ref, k_refs, v_refs = refs[:4], refs[4], refs[5:7], refs[7:9]
        out_ref, q_scr, c_scr, s_scr, w_scr = refs[9:]
        seq = (lax.axis_index("y") * 2 + lax.axis_index("xl")) * 8 + lax.axis_index("z")
        (slot,) = outer_slots([7])
        places = [slot * 512 + i * 128 for i in range(4)]
        acc = total_ref[...] + products(n_ref, piece_refs, places)
        acc = acc * HEAD_DIM ** (-0.5)
        acc = jnp.concatenate([acc, jnp.zeros((SPAN, columns), jnp.float32)], axis=0)
        q_scr[...] = pltpu.roll(acc, 1, 0).astype(jnp.bfloat16)
        lane = lax.broadcasted_iota(jnp.int32, (1, 128), 1)
        wide = lax.broadcasted_iota(jnp.int32, (1, 2 * NBR_LEN), 1)
        row = lax.broadcasted_iota(jnp.int32, (SPAN, HEAD_DIM), 0)
        usable, live = [], []
        for b in range(blocks):
            span = jnp.maximum(seq * (blocks - 1) + b - 1, 0)
            usable.append(
                wide < jnp.where(wide < NBR_LEN, lens_ref[0, span], lens_ref[1, span] + NBR_LEN)
            )
            line = seg_ref[pl.ds(span // 2, 1), :]
            if b % 2:
                same = (line == line[:, 63:64]) & (lane >= 63) & (lane < 127)
                count = jnp.sum(same.astype(jnp.int32), axis=1, keepdims=True)
            else:
                after = seg_ref[pl.ds(jnp.minimum(span // 2 + 1, seg_ref.shape[0] - 1), 1), :]
                same = (after == line[:, 127:128]) & (lane < 63)
                count = jnp.sum(same.astype(jnp.int32), axis=1, keepdims=True) + 1
            if b == 0:
                count = jnp.where(seq == 0, 0, count)
            live.append(row < count)
        for part in range(2):
            for h in range(heads):
                at = slice(h * HEAD_DIM, (h + 1) * HEAD_DIM)
                to = slice(part * half + h * HEAD_DIM, part * half + (h + 1) * HEAD_DIM)
                for b in range(blocks):
                    scores = lax.dot_general(
                        q_scr[b * SPAN : (b + 1) * SPAN, to],
                        k_refs[part][b - 1, :, at] if b else prev_ref[0, :, to],
                        (((1,), (1,)), ((), ())),
                        preferred_element_type=jnp.float32,
                    )
                    s_scr[h, b * SPAN : (b + 1) * SPAN, :] = jnp.where(usable[b], scores, jnp.float32(-1e30))
            for h in range(heads):
                for c in range(blocks // 3):
                    r = slice(c * 3 * SPAN, (c + 1) * 3 * SPAN)
                    scores = s_scr[h, r, :]
                    weights = jnp.exp(scores - jnp.max(scores, axis=-1, keepdims=True))
                    scale = 1.0 / jnp.sum(weights, axis=-1, keepdims=True)
                    w_scr[h, r, :] = (weights * scale).astype(jnp.bfloat16)
            for h in range(heads):
                at = slice(h * HEAD_DIM, (h + 1) * HEAD_DIM)
                to = slice(part * half + h * HEAD_DIM, part * half + (h + 1) * HEAD_DIM)
                for b in range(blocks):
                    mixed = jnp.dot(
                        w_scr[h, b * SPAN : (b + 1) * SPAN, :],
                        v_refs[part][b - 1, :, at] if b else prev_ref[1, :, to],
                        preferred_element_type=jnp.float32,
                    )
                    c_scr[b * SPAN : (b + 1) * SPAN, to] = jnp.where(live[b], mixed, 0.0)
        moved = pltpu.roll(c_scr[...], blocks * SPAN - 1, 0)
        out_ref[...] = moved[:rows].astype(jnp.bfloat16)

    return pl.pallas_call(
        body,
        out_shape=jax.ShapeDtypeStruct((rows, columns), jnp.bfloat16),
        in_specs=[SMEM] + [VMEM] * 12,
        out_specs=VMEM,
        scratch_shapes=[
            pltpu.VMEM((blocks * SPAN, columns), jnp.bfloat16),
            pltpu.VMEM((blocks * SPAN, columns), jnp.float32),
            pltpu.VMEM((heads, blocks * SPAN, 2 * NBR_LEN), jnp.float32),
            pltpu.VMEM((heads, blocks * SPAN, 2 * NBR_LEN), jnp.bfloat16),
        ],
        compiler_params=params(28),
        cost_estimate=cost(6 * MIB * 1000, 16 * MIB),
        name="attend",
    )(lens, segments, total, n, *pieces, prev, *keys, *values)


def after(value, *others):
    return lax.optimization_barrier((value, *others))[0]


def local(hidden, norm_gain, w_query, w_keyval, nbr_states, nbr_lens, segment_ids):
    core = lax.axis_index("core")

    def pick(zero, one):
        return jnp.where(core == 0, zero, one)

    def outer_first(column):
        return [send(column, (1, 0), (1, "z")), send(column, (-1, 0), (-1, "z"))]

    def outer_second(column, one, two, *first):
        one, two = after(one, *first), after(two, *first)
        return [send(pick(column, one), (0, 1), (1, "z")), send(two, (-1, 0), (-1, "z"))]

    def outer_third(three, four, *first):
        three, four = after(three, *first), after(four, *first)
        return [send(three, (1, 0), (1, "z")), send(pick(three, four), (-1, 0), (-1, "z"))]

    def outer_last(five, six, *first):
        r = five.shape[0] // 2
        five, six = after(five, *first), after(six, *first)
        return [send(five[:r], (1, 0), (1, "z")), send(six[r:], (-1, 0), (-1, "z"))]

    def projected(which, part, *first):
        return project(after(nbr_states, *first), w_keyval, which, part)

    round_one = [
        send(w_query, (1, "z"), (0, 1)),
        send(w_query, (-1, "z"), (1, 0)),
        send(w_query, (2, "z"), (-1, 0)),
        send(w_query, (-2, "z"), (2, 0)),
    ]
    normed = normalize(hidden, norm_gain[None])
    near = hop(after(normed, *round_one), "core")
    far = hop(normed, "xh")
    column_a = stacked([w_query, *round_one], ((3, 1, 0, 2), (0, 3, 4, 2)))
    head = after(pick(round_one[3], round_one[0]), normed)
    round_two = [
        send(head, (-1, "z"), (-1, 0)),
        send(head, (-2, "z"), (2, 0)),
        send(pick(round_one[2], round_one[0]), (1, "z"), (1, 0)),
    ]
    a = [column_a, *outer_first(column_a)]
    column_b = stacked([head, *round_two], ((0, 1, 2, 3), (0, 1, 2, 3)))
    half = nbr_states.shape[1] // 2
    prev = lax.dynamic_slice_in_dim(nbr_states[-1], core * half, half, 0)
    prev = lax.ppermute(after(prev, column_b), ("y", "xl", "z"), [(i, i + 1) for i in range(63)])
    b = [column_b, *outer_first(after(column_b, near))]
    a += outer_second(*a, *round_two)
    keys_a = projected(0, 0, column_b)
    values_a = projected(1, 0, keys_a, *a[1:3])
    b += outer_second(*b, values_a)
    keys_b = projected(0, 1, *b[1:3])
    far_near = hop(after(far, *a[3:5]), "core")
    a += outer_third(*a[3:5], keys_b)
    values_b = projected(1, 1, *a[3:5])
    prev_near = hop(after(prev, values_b), "core")
    b += outer_third(*b[3:5], values_b, prev)
    whole = gather_rows([after(normed, values_b), near, far, far_near])
    total = partial_product(whole, [(0, [0, 1, 2], a[:3])])
    a += outer_last(*a[5:7])
    prev = project_prev(after(prev, total), prev_near, w_keyval)
    total = partial_product(
        after(whole, *a[5:7]), [(256, [0, 1, 2], b[:3]), (0, [3, 4], a[3:5])], total
    )
    b += outer_last(*b[5:7], total)
    total = partial_product(
        after(whole, *b[5:7]),
        [(256, [3, 4], b[3:5]), (0, [5, 6], a[5:7]), (256, [5, 6], b[5:7])],
        total,
    )
    return attend(
        nbr_lens.T,
        segment_ids.reshape(-1, 128),
        total,
        whole,
        [*a[7:], *b[7:]],
        prev,
        [keys_a, keys_b],
        [values_a, values_b],
    )


def solution(mesh):
    fine = Mesh(mesh.devices.reshape(tuple(SIZES.values())), tuple(SIZES))
    section, seq = ("xh", "core"), ("y", "xl", "z")
    in_specs = (
        P(seq + section, None),
        P(),
        P(seq, section),
        P(None, None, section),
        P(seq, None, None),
        P(),
        P(),
    )
    out_specs = P(seq, section)
    return jax.shard_map(local, mesh=fine, in_specs=in_specs, out_specs=out_specs, check_vma=False)
```

```python
import functools

import jax
import jax.numpy as jnp
from jax import lax
from jax.experimental import pallas as pl
from jax.experimental.pallas import tpu as pltpu
from jax.sharding import Mesh, PartitionSpec as P

HEAD_DIM = 128
SPAN = 64
NBR_LEN = 128
SIZES = {"xh": 2, "core": 2, "y": 4, "xl": 2, "z": 8}
PLANE = ("core", "y", "xl", "z")
VMEM = pl.BlockSpec(memory_space=pltpu.VMEM)
SMEM = pl.BlockSpec(memory_space=pltpu.SMEM)
MIB = 1 << 20


def params(mib):
    return pltpu.CompilerParams(vmem_limit_bytes=mib * MIB)


def cost(flops, moved, exps=0):
    return pl.CostEstimate(flops=flops, bytes_accessed=moved, transcendentals=exps)


def moved(move, y, xl, z):
    by, how = move
    if how == "z":
        return y, xl, (z + by) % 8
    return (y + by) % 4, xl ^ how, z


def send(x, first, second):
    pairs = []
    for core, move in enumerate((first, second)):
        for y in range(4):
            for xl in range(2):
                for z in range(8):
                    y2, xl2, z2 = moved(move, y, xl, z)
                    pairs.append(
                        (((core * 4 + y) * 2 + xl) * 8 + z, ((core * 4 + y2) * 2 + xl2) * 8 + z2)
                    )
    return lax.ppermute(x, PLANE, pairs)


def hop(x, axis):
    return lax.ppermute(x, axis, [(0, 1), (1, 0)])


OUTER_Z = (0, -1, 1, -2, 2, -3, 3, -4)
OUTER_W = ((0, 0), (-1, 0), (1, 0), (0, 1), (2, 0), (-1, 1), (1, 1), (2, 1))


def outer_slots(which):
    y, xl, z = lax.axis_index("y"), lax.axis_index("xl"), lax.axis_index("z")
    out = []
    for i in which:
        dz, (dy, flip) = OUTER_Z[i], OUTER_W[i]
        other = jnp.where(xl == flip, 0, 1)
        along_w = lax.rem(y + dy + 4, 4) * 2 + other
        out.append(jnp.where(lax.axis_index("core") == 1, lax.rem(z + dz + 8, 8), along_w))
    return out


def stack_kernel(orders, *refs):
    out, rows = refs[-1], refs[0].shape[0]
    for core, order in enumerate(orders):

        @pl.when(lax.axis_index("core") == core)
        def _(order=order):
            for i, which in enumerate(order):
                out[i * rows : (i + 1) * rows, :] = refs[which][...]


def stacked(parts, orders):
    rows, columns = parts[0].shape
    return pl.pallas_call(
        functools.partial(stack_kernel, orders),
        out_shape=jax.ShapeDtypeStruct((4 * rows, columns), parts[0].dtype),
        in_specs=[VMEM] * len(parts),
        out_specs=VMEM,
        compiler_params=params(4),
        cost_estimate=cost(0, 16 * rows * columns),
        name="stack",
    )(*parts)


def norm_kernel(hidden_ref, gain_ref, out_ref):
    values = hidden_ref[...].astype(jnp.float32)
    factor = lax.rsqrt(jnp.mean(values * values, axis=-1, keepdims=True) + 1e-06)
    out_ref[...] = (values * factor * gain_ref[...]).astype(jnp.bfloat16)


def normalize(hidden, gain):
    rows, width = hidden.shape
    return pl.pallas_call(
        norm_kernel,
        out_shape=jax.ShapeDtypeStruct((rows, width), jnp.bfloat16),
        in_specs=[VMEM, VMEM],
        out_specs=VMEM,
        compiler_params=params(8),
        cost_estimate=cost(6 * rows * width, 4 * rows * width),
        name="norm",
    )(hidden, gain)


def rows_kernel(own_ref, near_ref, far_ref, far_near_ref, out):
    xh, core = lax.axis_index("xh"), lax.axis_index("core")
    y, xl, z = lax.axis_index("y"), lax.axis_index("xl"), lax.axis_index("z")
    slots = [xh * 2 + core, xh * 2 + 1 - core, 2 - 2 * xh + core, 3 - 2 * xh - core]
    refs = [own_ref, near_ref, far_ref, far_near_ref]
    rows = own_ref.shape[0]
    part = 32
    start = lax.rem(z + 6, 8) // 2

    for slot, ref in zip(slots, refs, strict=True):

        def one(i, _, slot=slot, ref=ref):
            here = pl.ds(pl.multiple_of(i * part, part), part)
            at = pl.ds(pl.multiple_of(slot * rows + i * part, part), part)

            def tile(lane):
                return ref[here, pl.ds(pl.multiple_of(lane, 128), 128)]

            @pl.when((core == 0) & (lax.rem(z, 2) == 0))
            def _():
                for w in range(8):
                    for k in range(4):
                        to = w * 512 + k * 128
                        out[at, to : to + 128] = tile(w * 512 + lax.rem(start + k, 4) * 128)

            @pl.when((core == 0) & (lax.rem(z, 2) == 1))
            def _():
                for w in range(8):
                    for k in range(4):
                        one = tile(w * 512 + lax.rem(start + k, 4) * 128)[:, 64:]
                        two = tile(w * 512 + lax.rem(start + k + 1, 4) * 128)[:, :64]
                        to = w * 512 + k * 128
                        out[at, to : to + 128] = jnp.concatenate([one, two], axis=1)

            @pl.when(core == 1)
            def _():
                for k in range(4):
                    side = xl if k < 2 else 1 - xl
                    base = [(lax.rem(y + 2 * (k % 2) + j, 4) * 2 + side) * 512 for j in range(2)]
                    for z_at in range(8):
                        half = slice(64 * (z_at % 2), 64 * (z_at % 2) + 64)
                        one, two = [tile(b + z_at // 2 * 128)[:, half] for b in base]
                        to = z_at * 512 + k * 128
                        out[at, to : to + 128] = jnp.concatenate([one, two], axis=1)

        lax.fori_loop(0, rows // part, one, None)


def gather_rows(parts):
    rows, width = parts[0].shape
    return pl.pallas_call(
        rows_kernel,
        out_shape=jax.ShapeDtypeStruct((4 * rows, width), parts[0].dtype),
        in_specs=[VMEM] * 4,
        out_specs=VMEM,
        compiler_params=params(10),
        cost_estimate=cost(0, 16 * rows * width),
        name="rows",
    )(*parts)


def project_kernel(states_ref, w_ref, out_ref):
    for i in range(out_ref.shape[0]):
        out_ref[i] = jnp.dot(
            states_ref[i], w_ref[0], preferred_element_type=jnp.float32
        ).astype(jnp.bfloat16)


def project(states, w, which, half):
    spans, keys, depth = states.shape
    columns = w.shape[2] // 2
    whole = lambda i: (0, 0, 0)
    return pl.pallas_call(
        project_kernel,
        grid=(1,),
        out_shape=jax.ShapeDtypeStruct((spans, keys, columns), jnp.bfloat16),
        in_specs=[
            pl.BlockSpec(states.shape, whole, pipeline_mode=pl.Buffered(1)),
            pl.BlockSpec((1, depth, columns), lambda i: (which, 0, half), pipeline_mode=pl.Buffered(1)),
        ],
        out_specs=pl.BlockSpec((spans, keys, columns), whole, pipeline_mode=pl.Buffered(1)),
        compiler_params=params(10),
        cost_estimate=cost(2 * spans * keys * depth * columns, 6 * MIB),
        name="project",
    )(states, w)


def project_prev_kernel(mine_ref, other_ref, w_ref, out_ref):
    core, rows = lax.axis_index("core"), mine_ref.shape[0]
    for which in range(2):
        for slot, ref in ((core, mine_ref), (1 - core, other_ref)):
            out_ref[which, pl.ds(pl.multiple_of(slot * rows, rows), rows), :] = jnp.dot(
                ref[...], w_ref[which], preferred_element_type=jnp.float32
            ).astype(jnp.bfloat16)


def project_prev(mine, other, w):
    rows, depth = mine.shape
    columns = w.shape[2]
    return pl.pallas_call(
        project_prev_kernel,
        out_shape=jax.ShapeDtypeStruct((2, 2 * rows, columns), jnp.bfloat16),
        in_specs=[VMEM] * 3,
        out_specs=VMEM,
        compiler_params=params(8),
        cost_estimate=cost(8 * rows * depth * columns, 6 * MIB),
        name="project_prev",
    )(mine, other, w)


def products(n_ref, refs, places):
    total = None
    for ref, place in zip(refs, places, strict=True):
        lanes = pl.ds(pl.multiple_of(place, 128), ref.shape[0])
        term = jnp.dot(n_ref[:, lanes], ref[...], preferred_element_type=jnp.float32)
        total = term if total is None else total + term
    return total


def partial_product(n, terms, before=None):
    pieces = [piece for _, _, some in terms for piece in some]
    rows, columns = n.shape[0], pieces[0].shape[1]
    depth = sum(p.shape[0] for p in pieces)
    extra = [] if before is None else [before]

    def body(n_ref, *refs):
        places = [slot * 512 + start for start, which, _ in terms for slot in outer_slots(which)]
        tile = columns // 2

        def one(i, _):
            at = pl.ds(pl.multiple_of(i * tile, tile), tile)
            total = products(n_ref, [ref.at[:, at] for ref in refs[: len(pieces)]], places)
            if extra:
                total = total + refs[len(pieces)][:, at]
            refs[-1][:, at] = total

        lax.fori_loop(0, columns // tile, one, None)

    return pl.pallas_call(
        body,
        out_shape=jax.ShapeDtypeStruct((rows, columns), jnp.float32),
        in_specs=[VMEM] * (1 + len(pieces) + len(extra)),
        out_specs=VMEM,
        compiler_params=params(14),
        cost_estimate=cost(2 * rows * depth * columns, 2 * depth * (rows + columns)),
        name="partial",
    )(n, *pieces, *extra)


def attend(lens, segments, total, n, pieces, prev, keys, values):
    rows, columns = total.shape
    blocks = keys[0].shape[0] + 1
    heads = columns // HEAD_DIM // 2
    half = columns // 2

    def body(lens_ref, seg_ref, total_ref, n_ref, *refs):
        piece_refs, prev_ref, k_refs, v_refs = refs[:4], refs[4], refs[5:7], refs[7:9]
        out_ref, q_scr, c_scr, s_scr, w_scr = refs[9:]
        seq = (lax.axis_index("y") * 2 + lax.axis_index("xl")) * 8 + lax.axis_index("z")
        (slot,) = outer_slots([7])
        places = [slot * 512 + i * 128 for i in range(4)]
        acc = total_ref[...] + products(n_ref, piece_refs, places)
        acc = acc * HEAD_DIM ** (-0.5)
        acc = jnp.concatenate([acc, jnp.zeros((SPAN, columns), jnp.float32)], axis=0)
        q_scr[...] = pltpu.roll(acc, 1, 0).astype(jnp.bfloat16)
        lane = lax.broadcasted_iota(jnp.int32, (1, 128), 1)
        wide = lax.broadcasted_iota(jnp.int32, (1, 2 * NBR_LEN), 1)
        row = lax.broadcasted_iota(jnp.int32, (SPAN, HEAD_DIM), 0)
        usable, live = [], []
        for b in range(blocks):
            span = jnp.maximum(seq * (blocks - 1) + b - 1, 0)
            usable.append(
                wide < jnp.where(wide < NBR_LEN, lens_ref[0, span], lens_ref[1, span] + NBR_LEN)
            )
            line = seg_ref[pl.ds(span // 2, 1), :]
            if b % 2:
                same = (line == line[:, 63:64]) & (lane >= 63) & (lane < 127)
                count = jnp.sum(same.astype(jnp.int32), axis=1, keepdims=True)
            else:
                after = seg_ref[pl.ds(jnp.minimum(span // 2 + 1, seg_ref.shape[0] - 1), 1), :]
                same = (after == line[:, 127:128]) & (lane < 63)
                count = jnp.sum(same.astype(jnp.int32), axis=1, keepdims=True) + 1
            if b == 0:
                count = jnp.where(seq == 0, 0, count)
            live.append(row < count)
        for part in range(2):
            for h in range(heads):
                at = slice(h * HEAD_DIM, (h + 1) * HEAD_DIM)
                to = slice(part * half + h * HEAD_DIM, part * half + (h + 1) * HEAD_DIM)
                for b in range(blocks):
                    scores = lax.dot_general(
                        q_scr[b * SPAN : (b + 1) * SPAN, to],
                        k_refs[part][b - 1, :, at] if b else prev_ref[0, :, to],
                        (((1,), (1,)), ((), ())),
                        preferred_element_type=jnp.float32,
                    )
                    s_scr[h, b * SPAN : (b + 1) * SPAN, :] = jnp.where(usable[b], scores, jnp.float32(-1e30))

            def soften(h, _):
                for c in range(blocks // 3):
                    r = slice(c * 3 * SPAN, (c + 1) * 3 * SPAN)
                    scores = s_scr[h, r, :]
                    weights = jnp.exp(scores - jnp.max(scores, axis=-1, keepdims=True))
                    scale = 1.0 / jnp.sum(weights, axis=-1, keepdims=True)
                    w_scr[h, r, :] = (weights * scale).astype(jnp.bfloat16)

            lax.fori_loop(0, heads, soften, None)
            for h in range(heads):
                at = slice(h * HEAD_DIM, (h + 1) * HEAD_DIM)
                to = slice(part * half + h * HEAD_DIM, part * half + (h + 1) * HEAD_DIM)
                for b in range(blocks):
                    mixed = jnp.dot(
                        w_scr[h, b * SPAN : (b + 1) * SPAN, :],
                        v_refs[part][b - 1, :, at] if b else prev_ref[1, :, to],
                        preferred_element_type=jnp.float32,
                    )
                    c_scr[b * SPAN : (b + 1) * SPAN, to] = jnp.where(live[b], mixed, 0.0)
        moved = pltpu.roll(c_scr[...], blocks * SPAN - 1, 0)
        out_ref[...] = moved[:rows].astype(jnp.bfloat16)

    return pl.pallas_call(
        body,
        out_shape=jax.ShapeDtypeStruct((rows, columns), jnp.bfloat16),
        in_specs=[SMEM] + [VMEM] * 12,
        out_specs=VMEM,
        scratch_shapes=[
            pltpu.VMEM((blocks * SPAN, columns), jnp.bfloat16),
            pltpu.VMEM((blocks * SPAN, columns), jnp.float32),
            pltpu.VMEM((heads, blocks * SPAN, 2 * NBR_LEN), jnp.float32),
            pltpu.VMEM((heads, blocks * SPAN, 2 * NBR_LEN), jnp.bfloat16),
        ],
        compiler_params=params(27),
        cost_estimate=cost(6 * MIB * 1000, 16 * MIB),
        name="attend",
    )(lens, segments, total, n, *pieces, prev, *keys, *values)


def after(value, *others):
    return lax.optimization_barrier((value, *others))[0]


def local(hidden, norm_gain, w_query, w_keyval, nbr_states, nbr_lens, segment_ids):
    core = lax.axis_index("core")

    def pick(zero, one):
        return jnp.where(core == 0, zero, one)

    def outer_first(column):
        return [send(column, (1, 0), (1, "z")), send(column, (-1, 0), (-1, "z"))]

    def outer_second(column, one, two, *first):
        one, two = after(one, *first), after(two, *first)
        return [send(pick(column, one), (0, 1), (1, "z")), send(two, (-1, 0), (-1, "z"))]

    def outer_third(three, four, *first):
        three, four = after(three, *first), after(four, *first)
        return [send(three, (1, 0), (1, "z")), send(pick(three, four), (-1, 0), (-1, "z"))]

    def outer_last(five, six, *first):
        r = five.shape[0] // 2
        five, six = after(five, *first), after(six, *first)
        return [send(five[:r], (1, 0), (1, "z")), send(six[r:], (-1, 0), (-1, "z"))]

    def projected(which, part, *first):
        return project(after(nbr_states, *first), w_keyval, which, part)

    round_one = [
        send(w_query, (1, "z"), (0, 1)),
        send(w_query, (-1, "z"), (1, 0)),
        send(w_query, (2, "z"), (-1, 0)),
        send(w_query, (-2, "z"), (2, 0)),
    ]
    normed = normalize(hidden, norm_gain[None])
    near = hop(after(normed, *round_one), "core")
    far = hop(normed, "xh")
    column_a = stacked([w_query, *round_one], ((3, 1, 0, 2), (0, 3, 4, 2)))
    head = after(pick(round_one[3], round_one[0]), normed)
    round_two = [
        send(head, (-1, "z"), (-1, 0)),
        send(head, (-2, "z"), (2, 0)),
        send(pick(round_one[2], round_one[0]), (1, "z"), (1, 0)),
    ]
    a = [column_a, *outer_first(column_a)]
    column_b = stacked([head, *round_two], ((0, 1, 2, 3), (0, 1, 2, 3)))
    half = nbr_states.shape[1] // 2
    prev = lax.dynamic_slice_in_dim(nbr_states[-1], core * half, half, 0)
    prev = lax.ppermute(after(prev, column_b), ("y", "xl", "z"), [(i, i + 1) for i in range(63)])
    b = [column_b, *outer_first(after(column_b, near))]
    a += outer_second(*a, *round_two)
    keys_a = projected(0, 0, column_b)
    values_a = projected(1, 0, keys_a, *a[1:3])
    b += outer_second(*b, values_a)
    keys_b = projected(0, 1, *b[1:3])
    far_near = hop(after(far, *a[3:5]), "core")
    a += outer_third(*a[3:5], keys_b)
    values_b = projected(1, 1, *a[3:5])
    prev_near = hop(after(prev, values_b), "core")
    b += outer_third(*b[3:5], values_b, prev)
    whole = gather_rows([after(normed, values_b), near, far, far_near])
    total = partial_product(whole, [(0, [0, 1, 2], a[:3])])
    a += outer_last(*a[5:7])
    prev = project_prev(after(prev, total), prev_near, w_keyval)
    total = partial_product(
        after(whole, *a[5:7]), [(256, [0, 1, 2], b[:3]), (0, [3, 4], a[3:5])], total
    )
    b += outer_last(*b[5:7], total)
    total = partial_product(
        after(whole, *b[5:7]),
        [(256, [3, 4], b[3:5]), (0, [5, 6], a[5:7]), (256, [5, 6], b[5:7])],
        total,
    )
    return attend(
        nbr_lens.T,
        segment_ids.reshape(-1, 128),
        total,
        whole,
        [*a[7:], *b[7:]],
        prev,
        [keys_a, keys_b],
        [values_a, values_b],
    )


def solution(mesh):
    fine = Mesh(mesh.devices.reshape(tuple(SIZES.values())), tuple(SIZES))
    section, seq = ("xh", "core"), ("y", "xl", "z")
    in_specs = (
        P(seq + section, None),
        P(),
        P(seq, section),
        P(None, None, section),
        P(seq, None, None),
        P(),
        P(),
    )
    out_specs = P(seq, section)
    return jax.shard_map(local, mesh=fine, in_specs=in_specs, out_specs=out_specs, check_vma=False)
```

```python
import functools

import jax
import jax.numpy as jnp
from jax import lax
from jax.experimental import pallas as pl
from jax.experimental.pallas import tpu as pltpu
from jax.sharding import Mesh, PartitionSpec as P

HEAD_DIM = 128
SPAN = 64
NBR_LEN = 128
SIZES = {"xh": 2, "core": 2, "y": 4, "xl": 2, "z": 8}
PLANE = ("core", "y", "xl", "z")
VMEM = pl.BlockSpec(memory_space=pltpu.VMEM)
SMEM = pl.BlockSpec(memory_space=pltpu.SMEM)
MIB = 1 << 20


def params(mib):
    return pltpu.CompilerParams(vmem_limit_bytes=mib * MIB)


def cost(flops, moved, exps=0):
    return pl.CostEstimate(flops=flops, bytes_accessed=moved, transcendentals=exps)


def moved(move, y, xl, z):
    by, how = move
    if how == "z":
        return y, xl, (z + by) % 8
    return (y + by) % 4, xl ^ how, z


def send(x, first, second):
    pairs = []
    for core, move in enumerate((first, second)):
        for y in range(4):
            for xl in range(2):
                for z in range(8):
                    y2, xl2, z2 = moved(move, y, xl, z)
                    pairs.append(
                        (((core * 4 + y) * 2 + xl) * 8 + z, ((core * 4 + y2) * 2 + xl2) * 8 + z2)
                    )
    return lax.ppermute(x, PLANE, pairs)


def hop(x, axis):
    return lax.ppermute(x, axis, [(0, 1), (1, 0)])


OUTER_Z = (0, -1, 1, -2, 2, -3, 3, -4)
OUTER_W = ((0, 0), (-1, 0), (1, 0), (0, 1), (2, 0), (-1, 1), (1, 1), (2, 1))


def outer_slots(which):
    y, xl, z = lax.axis_index("y"), lax.axis_index("xl"), lax.axis_index("z")
    out = []
    for i in which:
        dz, (dy, flip) = OUTER_Z[i], OUTER_W[i]
        other = jnp.where(xl == flip, 0, 1)
        along_w = lax.rem(y + dy + 4, 4) * 2 + other
        out.append(jnp.where(lax.axis_index("core") == 1, lax.rem(z + dz + 8, 8), along_w))
    return out


def stack_kernel(orders, *refs):
    out, rows = refs[-1], refs[0].shape[0]
    for core, order in enumerate(orders):

        @pl.when(lax.axis_index("core") == core)
        def _(order=order):
            for i, which in enumerate(order):
                out[i * rows : (i + 1) * rows, :] = refs[which][...]


def stacked(parts, orders):
    rows, columns = parts[0].shape
    return pl.pallas_call(
        functools.partial(stack_kernel, orders),
        out_shape=jax.ShapeDtypeStruct((4 * rows, columns), parts[0].dtype),
        in_specs=[VMEM] * len(parts),
        out_specs=VMEM,
        compiler_params=params(4),
        cost_estimate=cost(0, 16 * rows * columns),
        name="stack",
    )(*parts)


def norm_kernel(hidden_ref, gain_ref, out_ref):
    values = hidden_ref[...].astype(jnp.float32)
    factor = lax.rsqrt(jnp.mean(values * values, axis=-1, keepdims=True) + 1e-06)
    out_ref[...] = (values * factor * gain_ref[...]).astype(jnp.bfloat16)


def normalize(hidden, gain):
    rows, width = hidden.shape
    return pl.pallas_call(
        norm_kernel,
        out_shape=jax.ShapeDtypeStruct((rows, width), jnp.bfloat16),
        in_specs=[VMEM, VMEM],
        out_specs=VMEM,
        compiler_params=params(8),
        cost_estimate=cost(6 * rows * width, 4 * rows * width),
        name="norm",
    )(hidden, gain)


def rows_kernel(own_ref, near_ref, far_ref, far_near_ref, out):
    xh, core = lax.axis_index("xh"), lax.axis_index("core")
    y, xl, z = lax.axis_index("y"), lax.axis_index("xl"), lax.axis_index("z")
    slots = [xh * 2 + core, xh * 2 + 1 - core, 2 - 2 * xh + core, 3 - 2 * xh - core]
    refs = [own_ref, near_ref, far_ref, far_near_ref]
    rows = own_ref.shape[0]
    part = 32
    start = lax.rem(z + 6, 8) // 2

    for slot, ref in zip(slots, refs, strict=True):

        def one(i, _, slot=slot, ref=ref):
            here = pl.ds(pl.multiple_of(i * part, part), part)
            at = pl.ds(pl.multiple_of(slot * rows + i * part, part), part)

            def tile(lane):
                return ref[here, pl.ds(pl.multiple_of(lane, 128), 128)]

            @pl.when((core == 0) & (lax.rem(z, 2) == 0))
            def _():
                for w in range(8):
                    for k in range(4):
                        to = w * 512 + k * 128
                        out[at, to : to + 128] = tile(w * 512 + lax.rem(start + k, 4) * 128)

            @pl.when((core == 0) & (lax.rem(z, 2) == 1))
            def _():
                for w in range(8):
                    for k in range(4):
                        one = tile(w * 512 + lax.rem(start + k, 4) * 128)[:, 64:]
                        two = tile(w * 512 + lax.rem(start + k + 1, 4) * 128)[:, :64]
                        to = w * 512 + k * 128
                        out[at, to : to + 128] = jnp.concatenate([one, two], axis=1)

            @pl.when(core == 1)
            def _():
                for k in range(4):
                    side = xl if k < 2 else 1 - xl
                    base = [(lax.rem(y + 2 * (k % 2) + j, 4) * 2 + side) * 512 for j in range(2)]
                    for z_at in range(8):
                        half = slice(64 * (z_at % 2), 64 * (z_at % 2) + 64)
                        one, two = [tile(b + z_at // 2 * 128)[:, half] for b in base]
                        to = z_at * 512 + k * 128
                        out[at, to : to + 128] = jnp.concatenate([one, two], axis=1)

        lax.fori_loop(0, rows // part, one, None)


def gather_rows(parts):
    rows, width = parts[0].shape
    return pl.pallas_call(
        rows_kernel,
        out_shape=jax.ShapeDtypeStruct((4 * rows, width), parts[0].dtype),
        in_specs=[VMEM] * 4,
        out_specs=VMEM,
        compiler_params=params(10),
        cost_estimate=cost(0, 16 * rows * width),
        name="rows",
    )(*parts)


def project_kernel(states_ref, w_ref, out_ref):
    for i in range(out_ref.shape[0]):
        out_ref[i] = jnp.dot(
            states_ref[i], w_ref[0], preferred_element_type=jnp.float32
        ).astype(jnp.bfloat16)


def project(states, w, which, half):
    spans, keys, depth = states.shape
    columns = w.shape[2] // 2
    whole = lambda i: (0, 0, 0)
    return pl.pallas_call(
        project_kernel,
        grid=(1,),
        out_shape=jax.ShapeDtypeStruct((spans, keys, columns), jnp.bfloat16),
        in_specs=[
            pl.BlockSpec(states.shape, whole, pipeline_mode=pl.Buffered(1)),
            pl.BlockSpec((1, depth, columns), lambda i: (which, 0, half), pipeline_mode=pl.Buffered(1)),
        ],
        out_specs=pl.BlockSpec((spans, keys, columns), whole, pipeline_mode=pl.Buffered(1)),
        compiler_params=params(10),
        cost_estimate=cost(2 * spans * keys * depth * columns, 6 * MIB),
        name="project",
    )(states, w)


def project_prev_kernel(mine_ref, other_ref, w_ref, out_ref):
    core, rows = lax.axis_index("core"), mine_ref.shape[0]
    for which in range(2):
        for slot, ref in ((core, mine_ref), (1 - core, other_ref)):
            out_ref[which, pl.ds(pl.multiple_of(slot * rows, rows), rows), :] = jnp.dot(
                ref[...], w_ref[which], preferred_element_type=jnp.float32
            ).astype(jnp.bfloat16)


def project_prev(mine, other, w):
    rows, depth = mine.shape
    columns = w.shape[2]
    return pl.pallas_call(
        project_prev_kernel,
        out_shape=jax.ShapeDtypeStruct((2, 2 * rows, columns), jnp.bfloat16),
        in_specs=[VMEM] * 3,
        out_specs=VMEM,
        compiler_params=params(8),
        cost_estimate=cost(8 * rows * depth * columns, 6 * MIB),
        name="project_prev",
    )(mine, other, w)


def products(n_ref, refs, places):
    total = None
    for ref, place in zip(refs, places, strict=True):
        lanes = pl.ds(pl.multiple_of(place, 128), ref.shape[0])
        term = jnp.dot(n_ref[:, lanes], ref[...], preferred_element_type=jnp.float32)
        total = term if total is None else total + term
    return total


def partial_product(n, terms, before=None):
    pieces = [piece for _, _, some in terms for piece in some]
    rows, columns = n.shape[0], pieces[0].shape[1]
    depth = sum(p.shape[0] for p in pieces)
    extra = [] if before is None else [before]

    def body(n_ref, *refs):
        places = [slot * 512 + start for start, which, _ in terms for slot in outer_slots(which)]
        tile = columns // 2

        def one(i, _):
            at = pl.ds(pl.multiple_of(i * tile, tile), tile)
            total = products(n_ref, [ref.at[:, at] for ref in refs[: len(pieces)]], places)
            if extra:
                total = total + refs[len(pieces)][:, at]
            refs[-1][:, at] = total

        lax.fori_loop(0, columns // tile, one, None)

    return pl.pallas_call(
        body,
        out_shape=jax.ShapeDtypeStruct((rows, columns), jnp.float32),
        in_specs=[VMEM] * (1 + len(pieces) + len(extra)),
        out_specs=VMEM,
        compiler_params=params(14),
        cost_estimate=cost(2 * rows * depth * columns, 2 * depth * (rows + columns)),
        name="partial",
    )(n, *pieces, *extra)


def attend(lens, segments, total, n, pieces, prev, keys, values):
    rows, columns = total.shape
    blocks = keys[0].shape[0] + 1
    heads = columns // HEAD_DIM // 2
    half = columns // 2

    def body(lens_ref, seg_ref, total_ref, n_ref, *refs):
        piece_refs, prev_ref, k_refs, v_refs = refs[:4], refs[4], refs[5:7], refs[7:9]
        out_ref, q_scr, c_scr, s_scr, w_scr = refs[9:]
        seq = (lax.axis_index("y") * 2 + lax.axis_index("xl")) * 8 + lax.axis_index("z")
        (slot,) = outer_slots([7])
        places = [slot * 512 + i * 128 for i in range(4)]
        acc = total_ref[...] + products(n_ref, piece_refs, places)
        acc = acc * HEAD_DIM ** (-0.5)
        acc = jnp.concatenate([acc, jnp.zeros((SPAN, columns), jnp.float32)], axis=0)
        q_scr[...] = pltpu.roll(acc, 1, 0).astype(jnp.bfloat16)
        lane = lax.broadcasted_iota(jnp.int32, (1, 128), 1)
        wide = lax.broadcasted_iota(jnp.int32, (1, 2 * NBR_LEN), 1)
        row = lax.broadcasted_iota(jnp.int32, (SPAN, HEAD_DIM), 0)
        usable, live = [], []
        for b in range(blocks):
            span = jnp.maximum(seq * (blocks - 1) + b - 1, 0)
            usable.append(
                wide < jnp.where(wide < NBR_LEN, lens_ref[0, span], lens_ref[1, span] + NBR_LEN)
            )
            line = seg_ref[pl.ds(span // 2, 1), :]
            if b % 2:
                same = (line == line[:, 63:64]) & (lane >= 63) & (lane < 127)
                count = jnp.sum(same.astype(jnp.int32), axis=1, keepdims=True)
            else:
                after = seg_ref[pl.ds(jnp.minimum(span // 2 + 1, seg_ref.shape[0] - 1), 1), :]
                same = (after == line[:, 127:128]) & (lane < 63)
                count = jnp.sum(same.astype(jnp.int32), axis=1, keepdims=True) + 1
            if b == 0:
                count = jnp.where(seq == 0, 0, count)
            live.append(row < count)
        for part in range(2):
            for h in range(heads):
                at = slice(h * HEAD_DIM, (h + 1) * HEAD_DIM)
                to = slice(part * half + h * HEAD_DIM, part * half + (h + 1) * HEAD_DIM)
                for b in range(blocks):
                    scores = lax.dot_general(
                        q_scr[b * SPAN : (b + 1) * SPAN, to],
                        k_refs[part][b - 1, :, at] if b else prev_ref[0, :, to],
                        (((1,), (1,)), ((), ())),
                        preferred_element_type=jnp.float32,
                    )
                    s_scr[h, b * SPAN : (b + 1) * SPAN, :] = jnp.where(usable[b], scores, jnp.float32(-1e30))
            for h in range(heads):
                for c in range(blocks // 3):
                    r = slice(c * 3 * SPAN, (c + 1) * 3 * SPAN)
                    scores = s_scr[h, r, :]
                    weights = jnp.exp(scores - jnp.max(scores, axis=-1, keepdims=True))
                    scale = 1.0 / jnp.sum(weights, axis=-1, keepdims=True)
                    w_scr[h, r, :] = (weights * scale).astype(jnp.bfloat16)
            for h in range(heads):
                at = slice(h * HEAD_DIM, (h + 1) * HEAD_DIM)
                to = slice(part * half + h * HEAD_DIM, part * half + (h + 1) * HEAD_DIM)
                for b in range(blocks):
                    mixed = jnp.dot(
                        w_scr[h, b * SPAN : (b + 1) * SPAN, :],
                        v_refs[part][b - 1, :, at] if b else prev_ref[1, :, to],
                        preferred_element_type=jnp.float32,
                    )
                    c_scr[b * SPAN : (b + 1) * SPAN, to] = jnp.where(live[b], mixed, 0.0)
        moved = pltpu.roll(c_scr[...], blocks * SPAN - 1, 0)
        out_ref[...] = moved[:rows].astype(jnp.bfloat16)

    return pl.pallas_call(
        body,
        out_shape=jax.ShapeDtypeStruct((rows, columns), jnp.bfloat16),
        in_specs=[SMEM] + [VMEM] * 12,
        out_specs=VMEM,
        scratch_shapes=[
            pltpu.VMEM((blocks * SPAN, columns), jnp.bfloat16),
            pltpu.VMEM((blocks * SPAN, columns), jnp.float32),
            pltpu.VMEM((heads, blocks * SPAN, 2 * NBR_LEN), jnp.float32),
            pltpu.VMEM((heads, blocks * SPAN, 2 * NBR_LEN), jnp.bfloat16),
        ],
        compiler_params=params(27),
        cost_estimate=cost(6 * MIB * 1000, 16 * MIB),
        name="attend",
    )(lens, segments, total, n, *pieces, prev, *keys, *values)


def after(value, *others):
    return lax.optimization_barrier((value, *others))[0]


def local(hidden, norm_gain, w_query, w_keyval, nbr_states, nbr_lens, segment_ids):
    core = lax.axis_index("core")

    def pick(zero, one):
        return jnp.where(core == 0, zero, one)

    def outer_first(column):
        return [send(column, (1, 0), (1, "z")), send(column, (-1, 0), (-1, "z"))]

    def outer_second(column, one, two, *first):
        one, two = after(one, *first), after(two, *first)
        return [send(pick(column, one), (0, 1), (1, "z")), send(two, (-1, 0), (-1, "z"))]

    def outer_third(three, four, *first):
        three, four = after(three, *first), after(four, *first)
        return [send(three, (1, 0), (1, "z")), send(pick(three, four), (-1, 0), (-1, "z"))]

    def outer_last(five, six, *first):
        r = five.shape[0] // 2
        five, six = after(five, *first), after(six, *first)
        return [send(five[:r], (1, 0), (1, "z")), send(six[r:], (-1, 0), (-1, "z"))]

    def projected(which, part, *first):
        return project(after(nbr_states, *first), w_keyval, which, part)

    round_one = [
        send(w_query, (1, "z"), (0, 1)),
        send(w_query, (-1, "z"), (1, 0)),
        send(w_query, (2, "z"), (-1, 0)),
        send(w_query, (-2, "z"), (2, 0)),
    ]
    normed = normalize(hidden, norm_gain[None])
    near = hop(after(normed, *round_one), "core")
    far = hop(normed, "xh")
    column_a = stacked([w_query, *round_one], ((3, 1, 0, 2), (0, 3, 4, 2)))
    head = after(pick(round_one[3], round_one[0]), normed)
    round_two = [
        send(head, (-1, "z"), (-1, 0)),
        send(head, (-2, "z"), (2, 0)),
        send(pick(round_one[2], round_one[0]), (1, "z"), (1, 0)),
    ]
    a = [column_a, *outer_first(column_a)]
    column_b = stacked([head, *round_two], ((0, 1, 2, 3), (0, 1, 2, 3)))
    half = nbr_states.shape[1] // 2
    prev = lax.dynamic_slice_in_dim(nbr_states[-1], core * half, half, 0)
    prev = lax.ppermute(after(prev, column_b), ("y", "xl", "z"), [(i, i + 1) for i in range(63)])
    b = [column_b, *outer_first(after(column_b, near))]
    a += outer_second(*a, *round_two)
    far_near = hop(after(far, column_b), "core")
    keys_a = projected(0, 0, column_b, far)
    values_a = projected(1, 0, keys_a)
    b += outer_second(*b, values_a)
    a += outer_third(*a[3:5], values_a)
    whole = gather_rows([after(normed, values_a), near, far, far_near])
    total = partial_product(whole, [(0, [0, 1, 2], a[:3]), (256, [0, 1, 2], b[:3])])
    b += outer_third(*b[3:5], total)
    keys_b = projected(0, 1, total)
    prev_near = hop(after(prev, keys_b), "core")
    a += outer_last(*a[5:7], keys_b)
    values_b = projected(1, 1, keys_b, *b[3:5])
    total = partial_product(
        after(whole, values_b), [(0, [3, 4], a[3:5]), (256, [3, 4], b[3:5])], total
    )
    b += outer_last(*b[5:7], total)
    prev = project_prev(after(prev, total), prev_near, w_keyval)
    total = partial_product(
        after(whole, prev), [(0, [5, 6], a[5:7]), (256, [5, 6], b[5:7])], total
    )
    return attend(
        nbr_lens.T,
        segment_ids.reshape(-1, 128),
        total,
        whole,
        [*a[7:], *b[7:]],
        prev,
        [keys_a, keys_b],
        [values_a, values_b],
    )


def solution(mesh):
    fine = Mesh(mesh.devices.reshape(tuple(SIZES.values())), tuple(SIZES))
    section, seq = ("xh", "core"), ("y", "xl", "z")
    in_specs = (
        P(seq + section, None),
        P(),
        P(seq, section),
        P(None, None, section),
        P(seq, None, None),
        P(),
        P(),
    )
    out_specs = P(seq, section)
    return jax.shard_map(local, mesh=fine, in_specs=in_specs, out_specs=out_specs, check_vma=False)
```

```python
import functools

import jax
import jax.numpy as jnp
from jax import lax
from jax.experimental import pallas as pl
from jax.experimental.pallas import tpu as pltpu
from jax.sharding import Mesh, PartitionSpec as P

HEAD_DIM = 128
SPAN = 64
NBR_LEN = 128
SIZES = {"xh": 2, "core": 2, "y": 4, "xl": 2, "z": 8}
PLANE = ("core", "y", "xl", "z")
VMEM = pl.BlockSpec(memory_space=pltpu.VMEM)
SMEM = pl.BlockSpec(memory_space=pltpu.SMEM)
MIB = 1 << 20


def params(mib):
    return pltpu.CompilerParams(vmem_limit_bytes=mib * MIB)


def cost(flops, moved, exps=0):
    return pl.CostEstimate(flops=flops, bytes_accessed=moved, transcendentals=exps)


def moved(move, y, xl, z):
    by, how = move
    if how == "z":
        return y, xl, (z + by) % 8
    return (y + by) % 4, xl ^ how, z


def send(x, first, second):
    pairs = []
    for core, move in enumerate((first, second)):
        for y in range(4):
            for xl in range(2):
                for z in range(8):
                    y2, xl2, z2 = moved(move, y, xl, z)
                    pairs.append(
                        (((core * 4 + y) * 2 + xl) * 8 + z, ((core * 4 + y2) * 2 + xl2) * 8 + z2)
                    )
    return lax.ppermute(x, PLANE, pairs)


def hop(x, axis):
    return lax.ppermute(x, axis, [(0, 1), (1, 0)])


OUTER_Z = (0, -1, 1, -2, 2, -3, 3, -4)
OUTER_W = ((0, 0), (-1, 0), (1, 0), (0, 1), (2, 0), (-1, 1), (1, 1), (2, 1))


def outer_slots(which):
    y, xl, z = lax.axis_index("y"), lax.axis_index("xl"), lax.axis_index("z")
    out = []
    for i in which:
        dz, (dy, flip) = OUTER_Z[i], OUTER_W[i]
        other = jnp.where(xl == flip, 0, 1)
        along_w = lax.rem(y + dy + 4, 4) * 2 + other
        out.append(jnp.where(lax.axis_index("core") == 1, lax.rem(z + dz + 8, 8), along_w))
    return out


def stack_kernel(orders, *refs):
    out, rows = refs[-1], refs[0].shape[0]
    for core, order in enumerate(orders):

        @pl.when(lax.axis_index("core") == core)
        def _(order=order):
            for i, which in enumerate(order):
                out[i * rows : (i + 1) * rows, :] = refs[which][...]


def stacked(parts, orders):
    rows, columns = parts[0].shape
    return pl.pallas_call(
        functools.partial(stack_kernel, orders),
        out_shape=jax.ShapeDtypeStruct((4 * rows, columns), parts[0].dtype),
        in_specs=[VMEM] * len(parts),
        out_specs=VMEM,
        compiler_params=params(8),
        cost_estimate=cost(0, 16 * rows * columns),
        name="stack",
    )(*parts)


def norm_kernel(hidden_ref, gain_ref, out_ref):
    values = hidden_ref[...].astype(jnp.float32)
    factor = lax.rsqrt(jnp.mean(values * values, axis=-1, keepdims=True) + 1e-06)
    out_ref[...] = (values * factor * gain_ref[...]).astype(jnp.bfloat16)


def normalize(hidden, gain):
    rows, width = hidden.shape
    return pl.pallas_call(
        norm_kernel,
        out_shape=jax.ShapeDtypeStruct((rows, width), jnp.bfloat16),
        in_specs=[VMEM, VMEM],
        out_specs=VMEM,
        compiler_params=params(8),
        cost_estimate=cost(6 * rows * width, 4 * rows * width),
        name="norm",
    )(hidden, gain)


def rows_kernel(own_ref, near_ref, far_ref, far_near_ref, out):
    xh, core = lax.axis_index("xh"), lax.axis_index("core")
    y, xl, z = lax.axis_index("y"), lax.axis_index("xl"), lax.axis_index("z")
    slots = [xh * 2 + core, xh * 2 + 1 - core, 2 - 2 * xh + core, 3 - 2 * xh - core]
    refs = [own_ref, near_ref, far_ref, far_near_ref]
    rows = own_ref.shape[0]
    part = 32
    start = lax.rem(z + 6, 8) // 2

    for slot, ref in zip(slots, refs, strict=True):

        def one(i, _, slot=slot, ref=ref):
            here = pl.ds(pl.multiple_of(i * part, part), part)
            at = pl.ds(pl.multiple_of(slot * rows + i * part, part), part)

            def tile(lane):
                return ref[here, pl.ds(pl.multiple_of(lane, 128), 128)]

            @pl.when((core == 0) & (lax.rem(z, 2) == 0))
            def _():
                for w in range(8):
                    for k in range(4):
                        to = w * 512 + k * 128
                        out[at, to : to + 128] = tile(w * 512 + lax.rem(start + k, 4) * 128)

            @pl.when((core == 0) & (lax.rem(z, 2) == 1))
            def _():
                for w in range(8):
                    for k in range(4):
                        one = tile(w * 512 + lax.rem(start + k, 4) * 128)[:, 64:]
                        two = tile(w * 512 + lax.rem(start + k + 1, 4) * 128)[:, :64]
                        to = w * 512 + k * 128
                        out[at, to : to + 128] = jnp.concatenate([one, two], axis=1)

            @pl.when(core == 1)
            def _():
                for k in range(4):
                    side = xl if k < 2 else 1 - xl
                    base = [(lax.rem(y + 2 * (k % 2) + j, 4) * 2 + side) * 512 for j in range(2)]
                    for z_at in range(8):
                        half = slice(64 * (z_at % 2), 64 * (z_at % 2) + 64)
                        one, two = [tile(b + z_at // 2 * 128)[:, half] for b in base]
                        to = z_at * 512 + k * 128
                        out[at, to : to + 128] = jnp.concatenate([one, two], axis=1)

        lax.fori_loop(0, rows // part, one, None)


def gather_rows(parts):
    rows, width = parts[0].shape
    return pl.pallas_call(
        rows_kernel,
        out_shape=jax.ShapeDtypeStruct((4 * rows, width), parts[0].dtype),
        in_specs=[VMEM] * 4,
        out_specs=VMEM,
        compiler_params=params(16),
        cost_estimate=cost(0, 16 * rows * width),
        name="rows",
    )(*parts)


def project_kernel(states_ref, w_ref, out_ref):
    for i in range(out_ref.shape[0]):
        out_ref[i] = jnp.dot(
            states_ref[i], w_ref[0], preferred_element_type=jnp.float32
        ).astype(jnp.bfloat16)


def project(states, w, which, half):
    spans, keys, depth = states.shape
    columns = w.shape[2] // 2
    whole = lambda i: (0, 0, 0)
    return pl.pallas_call(
        project_kernel,
        grid=(1,),
        out_shape=jax.ShapeDtypeStruct((spans, keys, columns), jnp.bfloat16),
        in_specs=[
            pl.BlockSpec(states.shape, whole, pipeline_mode=pl.Buffered(1)),
            pl.BlockSpec((1, depth, columns), lambda i: (which, 0, half), pipeline_mode=pl.Buffered(1)),
        ],
        out_specs=pl.BlockSpec((spans, keys, columns), whole, pipeline_mode=pl.Buffered(1)),
        compiler_params=params(16),
        cost_estimate=cost(2 * spans * keys * depth * columns, 6 * MIB),
        name="project",
    )(states, w)


def project_prev_kernel(mine_ref, other_ref, w_ref, out_ref):
    core, rows = lax.axis_index("core"), mine_ref.shape[0]
    for which in range(2):
        for slot, ref in ((core, mine_ref), (1 - core, other_ref)):
            out_ref[which, pl.ds(pl.multiple_of(slot * rows, rows), rows), :] = jnp.dot(
                ref[...], w_ref[which], preferred_element_type=jnp.float32
            ).astype(jnp.bfloat16)


def project_prev(mine, other, w):
    rows, depth = mine.shape
    columns = w.shape[2]
    return pl.pallas_call(
        project_prev_kernel,
        out_shape=jax.ShapeDtypeStruct((2, 2 * rows, columns), jnp.bfloat16),
        in_specs=[VMEM] * 3,
        out_specs=VMEM,
        compiler_params=params(12),
        cost_estimate=cost(8 * rows * depth * columns, 6 * MIB),
        name="project_prev",
    )(mine, other, w)


def products(n_ref, refs, places):
    total = None
    for ref, place in zip(refs, places, strict=True):
        lanes = pl.ds(pl.multiple_of(place, 128), ref.shape[0])
        term = jnp.dot(n_ref[:, lanes], ref[...], preferred_element_type=jnp.float32)
        total = term if total is None else total + term
    return total


def partial_product(n, terms, before=None):
    pieces = [piece for _, _, some in terms for piece in some]
    rows, columns = n.shape[0], pieces[0].shape[1]
    depth = sum(p.shape[0] for p in pieces)
    extra = [] if before is None else [before]

    def body(n_ref, *refs):
        places = [slot * 512 + start for start, which, _ in terms for slot in outer_slots(which)]
        total = products(n_ref, refs[: len(pieces)], places)
        if extra:
            total = total + refs[len(pieces)][...]
        refs[-1][...] = total

    return pl.pallas_call(
        body,
        out_shape=jax.ShapeDtypeStruct((rows, columns), jnp.float32),
        in_specs=[VMEM] * (1 + len(pieces) + len(extra)),
        out_specs=VMEM,
        compiler_params=params(20),
        cost_estimate=cost(2 * rows * depth * columns, 2 * depth * (rows + columns)),
        name="partial",
    )(n, *pieces, *extra)


def attend(lens, segments, total, n, pieces, prev, keys, values):
    rows, columns = total.shape
    blocks = keys[0].shape[0] + 1
    heads = columns // HEAD_DIM // 2
    half = columns // 2

    def body(lens_ref, seg_ref, total_ref, n_ref, *refs):
        piece_refs, prev_ref, k_refs, v_refs = refs[:4], refs[4], refs[5:7], refs[7:9]
        out_ref, q_scr, c_scr, s_scr, w_scr = refs[9:]
        seq = (lax.axis_index("y") * 2 + lax.axis_index("xl")) * 8 + lax.axis_index("z")
        (slot,) = outer_slots([7])
        places = [slot * 512 + i * 128 for i in range(4)]
        acc = total_ref[...] + products(n_ref, piece_refs, places)
        acc = acc * HEAD_DIM ** (-0.5)
        acc = jnp.concatenate([acc, jnp.zeros((SPAN, columns), jnp.float32)], axis=0)
        q_scr[...] = pltpu.roll(acc, 1, 0).astype(jnp.bfloat16)
        lane = lax.broadcasted_iota(jnp.int32, (1, 128), 1)
        wide = lax.broadcasted_iota(jnp.int32, (1, 2 * NBR_LEN), 1)
        row = lax.broadcasted_iota(jnp.int32, (SPAN, HEAD_DIM), 0)
        usable, live = [], []
        for b in range(blocks):
            span = jnp.maximum(seq * (blocks - 1) + b - 1, 0)
            usable.append(
                wide < jnp.where(wide < NBR_LEN, lens_ref[0, span], lens_ref[1, span] + NBR_LEN)
            )
            line = seg_ref[pl.ds(span // 2, 1), :]
            if b % 2:
                same = (line == line[:, 63:64]) & (lane >= 63) & (lane < 127)
                count = jnp.sum(same.astype(jnp.int32), axis=1, keepdims=True)
            else:
                after = seg_ref[pl.ds(jnp.minimum(span // 2 + 1, seg_ref.shape[0] - 1), 1), :]
                same = (after == line[:, 127:128]) & (lane < 63)
                count = jnp.sum(same.astype(jnp.int32), axis=1, keepdims=True) + 1
            if b == 0:
                count = jnp.where(seq == 0, 0, count)
            live.append(row < count)
        for part in range(2):
            for h in range(heads):
                at = slice(h * HEAD_DIM, (h + 1) * HEAD_DIM)
                to = slice(part * half + h * HEAD_DIM, part * half + (h + 1) * HEAD_DIM)
                for b in range(blocks):
                    scores = lax.dot_general(
                        q_scr[b * SPAN : (b + 1) * SPAN, to],
                        k_refs[part][b - 1, :, at] if b else prev_ref[0, :, to],
                        (((1,), (1,)), ((), ())),
                        preferred_element_type=jnp.float32,
                    )
                    s_scr[h, b * SPAN : (b + 1) * SPAN, :] = jnp.where(usable[b], scores, jnp.float32(-1e30))
            for h in range(heads):
                for c in range(blocks // 3):
                    r = slice(c * 3 * SPAN, (c + 1) * 3 * SPAN)
                    scores = s_scr[h, r, :]
                    weights = jnp.exp(scores - jnp.max(scores, axis=-1, keepdims=True))
                    scale = 1.0 / jnp.sum(weights, axis=-1, keepdims=True)
                    w_scr[h, r, :] = (weights * scale).astype(jnp.bfloat16)
            for h in range(heads):
                at = slice(h * HEAD_DIM, (h + 1) * HEAD_DIM)
                to = slice(part * half + h * HEAD_DIM, part * half + (h + 1) * HEAD_DIM)
                for b in range(blocks):
                    mixed = jnp.dot(
                        w_scr[h, b * SPAN : (b + 1) * SPAN, :],
                        v_refs[part][b - 1, :, at] if b else prev_ref[1, :, to],
                        preferred_element_type=jnp.float32,
                    )
                    c_scr[b * SPAN : (b + 1) * SPAN, to] = jnp.where(live[b], mixed, 0.0)
        moved = pltpu.roll(c_scr[...], blocks * SPAN - 1, 0)
        out_ref[...] = moved[:rows].astype(jnp.bfloat16)

    return pl.pallas_call(
        body,
        out_shape=jax.ShapeDtypeStruct((rows, columns), jnp.bfloat16),
        in_specs=[SMEM] + [VMEM] * 12,
        out_specs=VMEM,
        scratch_shapes=[
            pltpu.VMEM((blocks * SPAN, columns), jnp.bfloat16),
            pltpu.VMEM((blocks * SPAN, columns), jnp.float32),
            pltpu.VMEM((heads, blocks * SPAN, 2 * NBR_LEN), jnp.float32),
            pltpu.VMEM((heads, blocks * SPAN, 2 * NBR_LEN), jnp.bfloat16),
        ],
        compiler_params=params(28),
        cost_estimate=cost(6 * MIB * 1000, 16 * MIB),
        name="attend",
    )(lens, segments, total, n, *pieces, prev, *keys, *values)


def after(value, *others):
    return lax.optimization_barrier((value, *others))[0]


def local(hidden, norm_gain, w_query, w_keyval, nbr_states, nbr_lens, segment_ids):
    core = lax.axis_index("core")

    def pick(zero, one):
        return jnp.where(core == 0, zero, one)

    def outer_first(column):
        return [send(column, (1, 0), (1, "z")), send(column, (-1, 0), (-1, "z"))]

    def outer_second(column, one, two, *first):
        one, two = after(one, *first), after(two, *first)
        return [send(pick(column, one), (0, 1), (1, "z")), send(two, (-1, 0), (-1, "z"))]

    def outer_third(three, four, *first):
        three, four = after(three, *first), after(four, *first)
        return [send(three, (1, 0), (1, "z")), send(pick(three, four), (-1, 0), (-1, "z"))]

    def outer_last(five, six, *first):
        r = five.shape[0] // 2
        five, six = after(five, *first), after(six, *first)
        return [send(five[:r], (1, 0), (1, "z")), send(six[r:], (-1, 0), (-1, "z"))]

    def projected(which, part, *first):
        return project(after(nbr_states, *first), w_keyval, which, part)

    round_one = [
        send(w_query, (1, "z"), (0, 1)),
        send(w_query, (-1, "z"), (1, 0)),
        send(w_query, (2, "z"), (-1, 0)),
        send(w_query, (-2, "z"), (2, 0)),
    ]
    normed = normalize(hidden, norm_gain[None])
    near = hop(normed, "core")
    far = hop(normed, "xh")
    column_a = stacked([w_query, *round_one], ((3, 1, 0, 2), (0, 3, 4, 2)))
    head = after(pick(round_one[3], round_one[0]), normed)
    round_two = [
        send(head, (-1, "z"), (-1, 0)),
        send(head, (-2, "z"), (2, 0)),
        send(pick(round_one[2], round_one[0]), (1, "z"), (1, 0)),
    ]
    column_b = stacked([head, *round_two], ((0, 1, 2, 3), (0, 1, 2, 3)))

    a = [column_a, *outer_first(column_a)]
    half = nbr_states.shape[1] // 2
    prev = lax.dynamic_slice_in_dim(nbr_states[-1], core * half, half, 0)
    prev = lax.ppermute(after(prev, column_a), ("y", "xl", "z"), [(i, i + 1) for i in range(63)])
    keys_a = projected(0, 0, column_a)
    b = [column_b, *outer_first(column_b)]
    a += outer_second(*a, keys_a)
    values_a = projected(1, 0, *a[1:3])
    b += outer_second(*b, values_a, prev)
    prev_near = hop(prev, "core")
    keys_b = projected(0, 1, *b[1:3])
    far_near = hop(after(far, keys_b), "core")
    a += outer_third(*a[3:5], keys_b)
    values_b = projected(1, 1, *a[3:5])
    prev = project_prev(after(prev, values_b), prev_near, w_keyval)
    whole = gather_rows([after(normed, prev), near, far, far_near])
    b += outer_third(*b[3:5], whole)
    total = partial_product(after(whole, *b[3:5]), [(0, [0, 1, 2], a[:3])])
    a += outer_last(*a[5:7], total)
    total = partial_product(
        after(whole, *a[5:7]), [(256, [0, 1, 2], b[:3]), (0, [3, 4], a[3:5])], total
    )
    b += outer_last(*b[5:7], total)
    total = partial_product(
        after(whole, *b[5:7]),
        [(256, [3, 4], b[3:5]), (0, [5, 6], a[5:7]), (256, [5, 6], b[5:7])],
        total,
    )
    return attend(
        nbr_lens.T,
        segment_ids.reshape(-1, 128),
        total,
        whole,
        [*a[7:], *b[7:]],
        prev,
        [keys_a, keys_b],
        [values_a, values_b],
    )


def solution(mesh):
    fine = Mesh(mesh.devices.reshape(tuple(SIZES.values())), tuple(SIZES))
    section, seq = ("xh", "core"), ("y", "xl", "z")
    in_specs = (
        P(seq + section, None),
        P(),
        P(seq, section),
        P(None, None, section),
        P(seq, None, None),
        P(),
        P(),
    )
    out_specs = P(seq, section)
    return jax.shard_map(local, mesh=fine, in_specs=in_specs, out_specs=out_specs, check_vma=False)
```

```python
import functools

import jax
import jax.numpy as jnp
from jax import lax
from jax.experimental import pallas as pl
from jax.experimental.pallas import tpu as pltpu
from jax.sharding import Mesh, PartitionSpec as P

HEAD_DIM = 128
SPAN = 64
NBR_LEN = 128
SIZES = {"xh": 2, "core": 2, "y": 4, "xl": 2, "z": 8}
PLANE = ("core", "y", "xl", "z")
VMEM = pl.BlockSpec(memory_space=pltpu.VMEM)
SMEM = pl.BlockSpec(memory_space=pltpu.SMEM)
MIB = 1 << 20


def params(mib):
    return pltpu.CompilerParams(vmem_limit_bytes=mib * MIB)


def cost(flops, moved, exps=0):
    return pl.CostEstimate(flops=flops, bytes_accessed=moved, transcendentals=exps)


def moved(move, y, xl, z):
    by, how = move
    if how == "z":
        return y, xl, (z + by) % 8
    return (y + by) % 4, xl ^ how, z


def send(x, first, second):
    pairs = []
    for core, move in enumerate((first, second)):
        for y in range(4):
            for xl in range(2):
                for z in range(8):
                    y2, xl2, z2 = moved(move, y, xl, z)
                    pairs.append(
                        (((core * 4 + y) * 2 + xl) * 8 + z, ((core * 4 + y2) * 2 + xl2) * 8 + z2)
                    )
    return lax.ppermute(x, PLANE, pairs)


def hop(x, axis):
    return lax.ppermute(x, axis, [(0, 1), (1, 0)])


OUTER_Z = (0, -1, 1, -2, 2, -3, 3, -4)
OUTER_W = ((0, 0), (-1, 0), (1, 0), (0, 1), (2, 0), (-1, 1), (1, 1), (2, 1))


def outer_slots(which):
    y, xl, z = lax.axis_index("y"), lax.axis_index("xl"), lax.axis_index("z")
    out = []
    for i in which:
        dz, (dy, flip) = OUTER_Z[i], OUTER_W[i]
        other = jnp.where(xl == flip, 0, 1)
        along_w = lax.rem(y + dy + 4, 4) * 2 + other
        out.append(jnp.where(lax.axis_index("core") == 1, lax.rem(z + dz + 8, 8), along_w))
    return out


def stack_kernel(orders, *refs):
    out, rows = refs[-1], refs[0].shape[0]
    for core, order in enumerate(orders):

        @pl.when(lax.axis_index("core") == core)
        def _(order=order):
            for i, which in enumerate(order):
                out[i * rows : (i + 1) * rows, :] = refs[which][...]


def stacked(parts, orders):
    rows, columns = parts[0].shape
    return pl.pallas_call(
        functools.partial(stack_kernel, orders),
        out_shape=jax.ShapeDtypeStruct((4 * rows, columns), parts[0].dtype),
        in_specs=[VMEM] * len(parts),
        out_specs=VMEM,
        compiler_params=params(8),
        cost_estimate=cost(0, 16 * rows * columns),
        name="stack",
    )(*parts)


def norm_kernel(hidden_ref, gain_ref, out_ref):
    values = hidden_ref[...].astype(jnp.float32)
    factor = lax.rsqrt(jnp.mean(values * values, axis=-1, keepdims=True) + 1e-06)
    out_ref[...] = (values * factor * gain_ref[...]).astype(jnp.bfloat16)


def normalize(hidden, gain):
    rows, width = hidden.shape
    return pl.pallas_call(
        norm_kernel,
        out_shape=jax.ShapeDtypeStruct((rows, width), jnp.bfloat16),
        in_specs=[VMEM, VMEM],
        out_specs=VMEM,
        compiler_params=params(8),
        cost_estimate=cost(6 * rows * width, 4 * rows * width),
        name="norm",
    )(hidden, gain)


def rows_kernel(own_ref, near_ref, far_ref, far_near_ref, out):
    xh, core = lax.axis_index("xh"), lax.axis_index("core")
    y, xl, z = lax.axis_index("y"), lax.axis_index("xl"), lax.axis_index("z")
    slots = [xh * 2 + core, xh * 2 + 1 - core, 2 - 2 * xh + core, 3 - 2 * xh - core]
    refs = [own_ref, near_ref, far_ref, far_near_ref]
    rows = own_ref.shape[0]
    part = 32
    start = lax.rem(z + 6, 8) // 2

    for slot, ref in zip(slots, refs, strict=True):

        def one(i, _, slot=slot, ref=ref):
            here = pl.ds(pl.multiple_of(i * part, part), part)
            at = pl.ds(pl.multiple_of(slot * rows + i * part, part), part)

            def tile(lane):
                return ref[here, pl.ds(pl.multiple_of(lane, 128), 128)]

            @pl.when((core == 0) & (lax.rem(z, 2) == 0))
            def _():
                for w in range(8):
                    for k in range(4):
                        to = w * 512 + k * 128
                        out[at, to : to + 128] = tile(w * 512 + lax.rem(start + k, 4) * 128)

            @pl.when((core == 0) & (lax.rem(z, 2) == 1))
            def _():
                for w in range(8):
                    for k in range(4):
                        one = tile(w * 512 + lax.rem(start + k, 4) * 128)[:, 64:]
                        two = tile(w * 512 + lax.rem(start + k + 1, 4) * 128)[:, :64]
                        to = w * 512 + k * 128
                        out[at, to : to + 128] = jnp.concatenate([one, two], axis=1)

            @pl.when(core == 1)
            def _():
                for k in range(4):
                    side = xl if k < 2 else 1 - xl
                    base = [(lax.rem(y + 2 * (k % 2) + j, 4) * 2 + side) * 512 for j in range(2)]
                    for z_at in range(8):
                        half = slice(64 * (z_at % 2), 64 * (z_at % 2) + 64)
                        one, two = [tile(b + z_at // 2 * 128)[:, half] for b in base]
                        to = z_at * 512 + k * 128
                        out[at, to : to + 128] = jnp.concatenate([one, two], axis=1)

        lax.fori_loop(0, rows // part, one, None)


def gather_rows(parts):
    rows, width = parts[0].shape
    return pl.pallas_call(
        rows_kernel,
        out_shape=jax.ShapeDtypeStruct((4 * rows, width), parts[0].dtype),
        in_specs=[VMEM] * 4,
        out_specs=VMEM,
        compiler_params=params(16),
        cost_estimate=cost(0, 16 * rows * width),
        name="rows",
    )(*parts)


def project_kernel(states_ref, w_ref, out_ref):
    for i in range(out_ref.shape[0]):
        out_ref[i] = jnp.dot(
            states_ref[i], w_ref[0], preferred_element_type=jnp.float32
        ).astype(jnp.bfloat16)


def project(states, w, which, half):
    spans, keys, depth = states.shape
    columns = w.shape[2] // 2
    whole = lambda i: (0, 0, 0)
    return pl.pallas_call(
        project_kernel,
        grid=(1,),
        out_shape=jax.ShapeDtypeStruct((spans, keys, columns), jnp.bfloat16),
        in_specs=[
            pl.BlockSpec(states.shape, whole, pipeline_mode=pl.Buffered(1)),
            pl.BlockSpec((1, depth, columns), lambda i: (which, 0, half), pipeline_mode=pl.Buffered(1)),
        ],
        out_specs=pl.BlockSpec((spans, keys, columns), whole, pipeline_mode=pl.Buffered(1)),
        compiler_params=params(16),
        cost_estimate=cost(2 * spans * keys * depth * columns, 6 * MIB),
        name="project",
    )(states, w)


def project_prev_kernel(mine_ref, other_ref, w_ref, out_ref):
    core, rows = lax.axis_index("core"), mine_ref.shape[0]
    for which in range(2):
        for slot, ref in ((core, mine_ref), (1 - core, other_ref)):
            out_ref[which, pl.ds(pl.multiple_of(slot * rows, rows), rows), :] = jnp.dot(
                ref[...], w_ref[which], preferred_element_type=jnp.float32
            ).astype(jnp.bfloat16)


def project_prev(mine, other, w):
    rows, depth = mine.shape
    columns = w.shape[2]
    return pl.pallas_call(
        project_prev_kernel,
        out_shape=jax.ShapeDtypeStruct((2, 2 * rows, columns), jnp.bfloat16),
        in_specs=[VMEM] * 3,
        out_specs=VMEM,
        compiler_params=params(12),
        cost_estimate=cost(8 * rows * depth * columns, 6 * MIB),
        name="project_prev",
    )(mine, other, w)


def products(n_ref, refs, places):
    total = None
    for ref, place in zip(refs, places, strict=True):
        lanes = pl.ds(pl.multiple_of(place, 128), ref.shape[0])
        term = jnp.dot(n_ref[:, lanes], ref[...], preferred_element_type=jnp.float32)
        total = term if total is None else total + term
    return total


def partial_product(n, terms, before=None):
    pieces = [piece for _, _, some in terms for piece in some]
    rows, columns = n.shape[0], pieces[0].shape[1]
    depth = sum(p.shape[0] for p in pieces)
    extra = [] if before is None else [before]

    def body(n_ref, *refs):
        places = [slot * 512 + start for start, which, _ in terms for slot in outer_slots(which)]
        total = products(n_ref, refs[: len(pieces)], places)
        if extra:
            total = total + refs[len(pieces)][...]
        refs[-1][...] = total

    return pl.pallas_call(
        body,
        out_shape=jax.ShapeDtypeStruct((rows, columns), jnp.float32),
        in_specs=[VMEM] * (1 + len(pieces) + len(extra)),
        out_specs=VMEM,
        compiler_params=params(20),
        cost_estimate=cost(2 * rows * depth * columns, 2 * depth * (rows + columns)),
        name="partial",
    )(n, *pieces, *extra)


def attend(lens, segments, total, n, pieces, prev, keys, values):
    rows, columns = total.shape
    blocks = keys[0].shape[0] + 1
    heads = columns // HEAD_DIM // 2
    half = columns // 2

    def body(lens_ref, seg_ref, total_ref, n_ref, *refs):
        piece_refs, prev_ref, k_refs, v_refs = refs[:4], refs[4], refs[5:7], refs[7:9]
        out_ref, q_scr, c_scr, s_scr, w_scr = refs[9:]
        seq = (lax.axis_index("y") * 2 + lax.axis_index("xl")) * 8 + lax.axis_index("z")
        (slot,) = outer_slots([7])
        places = [slot * 512 + i * 128 for i in range(4)]
        acc = total_ref[...] + products(n_ref, piece_refs, places)
        acc = acc * HEAD_DIM ** (-0.5)
        acc = jnp.concatenate([acc, jnp.zeros((SPAN, columns), jnp.float32)], axis=0)
        q_scr[...] = pltpu.roll(acc, 1, 0).astype(jnp.bfloat16)
        lane = lax.broadcasted_iota(jnp.int32, (1, 128), 1)
        wide = lax.broadcasted_iota(jnp.int32, (1, 2 * NBR_LEN), 1)
        row = lax.broadcasted_iota(jnp.int32, (SPAN, HEAD_DIM), 0)
        usable, live = [], []
        for b in range(blocks):
            span = jnp.maximum(seq * (blocks - 1) + b - 1, 0)
            usable.append(
                wide < jnp.where(wide < NBR_LEN, lens_ref[0, span], lens_ref[1, span] + NBR_LEN)
            )
            line = seg_ref[pl.ds(span // 2, 1), :]
            if b % 2:
                same = (line == line[:, 63:64]) & (lane >= 63) & (lane < 127)
                count = jnp.sum(same.astype(jnp.int32), axis=1, keepdims=True)
            else:
                after = seg_ref[pl.ds(jnp.minimum(span // 2 + 1, seg_ref.shape[0] - 1), 1), :]
                same = (after == line[:, 127:128]) & (lane < 63)
                count = jnp.sum(same.astype(jnp.int32), axis=1, keepdims=True) + 1
            if b == 0:
                count = jnp.where(seq == 0, 0, count)
            live.append(row < count)
        for part in range(2):
            for h in range(heads):
                at = slice(h * HEAD_DIM, (h + 1) * HEAD_DIM)
                to = slice(part * half + h * HEAD_DIM, part * half + (h + 1) * HEAD_DIM)
                for b in range(blocks):
                    scores = lax.dot_general(
                        q_scr[b * SPAN : (b + 1) * SPAN, to],
                        k_refs[part][b - 1, :, at] if b else prev_ref[0, :, to],
                        (((1,), (1,)), ((), ())),
                        preferred_element_type=jnp.float32,
                    )
                    s_scr[h, b * SPAN : (b + 1) * SPAN, :] = jnp.where(usable[b], scores, jnp.float32(-1e30))
            for h in range(heads):
                for c in range(blocks // 3):
                    r = slice(c * 3 * SPAN, (c + 1) * 3 * SPAN)
                    scores = s_scr[h, r, :]
                    weights = jnp.exp(scores - jnp.max(scores, axis=-1, keepdims=True))
                    scale = 1.0 / jnp.sum(weights, axis=-1, keepdims=True)
                    w_scr[h, r, :] = (weights * scale).astype(jnp.bfloat16)
            for h in range(heads):
                at = slice(h * HEAD_DIM, (h + 1) * HEAD_DIM)
                to = slice(part * half + h * HEAD_DIM, part * half + (h + 1) * HEAD_DIM)
                for b in range(blocks):
                    mixed = jnp.dot(
                        w_scr[h, b * SPAN : (b + 1) * SPAN, :],
                        v_refs[part][b - 1, :, at] if b else prev_ref[1, :, to],
                        preferred_element_type=jnp.float32,
                    )
                    c_scr[b * SPAN : (b + 1) * SPAN, to] = jnp.where(live[b], mixed, 0.0)
        moved = pltpu.roll(c_scr[...], blocks * SPAN - 1, 0)
        out_ref[...] = moved[:rows].astype(jnp.bfloat16)

    return pl.pallas_call(
        body,
        out_shape=jax.ShapeDtypeStruct((rows, columns), jnp.bfloat16),
        in_specs=[SMEM] + [VMEM] * 12,
        out_specs=VMEM,
        scratch_shapes=[
            pltpu.VMEM((blocks * SPAN, columns), jnp.bfloat16),
            pltpu.VMEM((blocks * SPAN, columns), jnp.float32),
            pltpu.VMEM((heads, blocks * SPAN, 2 * NBR_LEN), jnp.float32),
            pltpu.VMEM((heads, blocks * SPAN, 2 * NBR_LEN), jnp.bfloat16),
        ],
        compiler_params=params(28),
        cost_estimate=cost(6 * MIB * 1000, 16 * MIB),
        name="attend",
    )(lens, segments, total, n, *pieces, prev, *keys, *values)


def after(value, *others):
    return lax.optimization_barrier((value, *others))[0]


def local(hidden, norm_gain, w_query, w_keyval, nbr_states, nbr_lens, segment_ids):
    core = lax.axis_index("core")

    def pick(zero, one):
        return jnp.where(core == 0, zero, one)

    def outer_first(column):
        return [send(column, (1, 0), (1, "z")), send(column, (-1, 0), (-1, "z"))]

    def outer_second(column, one, two, *first):
        one, two = after(one, *first), after(two, *first)
        return [send(pick(column, one), (0, 1), (1, "z")), send(two, (-1, 0), (-1, "z"))]

    def outer_third(three, four, *first):
        three, four = after(three, *first), after(four, *first)
        return [send(three, (1, 0), (1, "z")), send(pick(three, four), (-1, 0), (-1, "z"))]

    def outer_last(five, six, *first):
        r = five.shape[0] // 2
        five, six = after(five, *first), after(six, *first)
        return [send(five[:r], (1, 0), (1, "z")), send(six[r:], (-1, 0), (-1, "z"))]

    def projected(which, part, *first):
        return project(after(nbr_states, *first), w_keyval, which, part)

    round_one = [
        send(w_query, (1, "z"), (0, 1)),
        send(w_query, (-1, "z"), (1, 0)),
        send(w_query, (2, "z"), (-1, 0)),
        send(w_query, (-2, "z"), (2, 0)),
    ]
    normed = normalize(hidden, norm_gain[None])
    near = hop(after(normed, *round_one), "core")
    far = hop(normed, "xh")
    column_a = stacked([w_query, *round_one], ((3, 1, 0, 2), (0, 3, 4, 2)))
    head = after(pick(round_one[3], round_one[0]), normed)
    round_two = [
        send(head, (-1, "z"), (-1, 0)),
        send(head, (-2, "z"), (2, 0)),
        send(pick(round_one[2], round_one[0]), (1, "z"), (1, 0)),
    ]
    column_b = stacked([head, *round_two], ((0, 1, 2, 3), (0, 1, 2, 3)))

    a = [column_a, *outer_first(column_a)]
    half = nbr_states.shape[1] // 2
    prev = lax.dynamic_slice_in_dim(nbr_states[-1], core * half, half, 0)
    prev = lax.ppermute(after(prev, column_b), ("y", "xl", "z"), [(i, i + 1) for i in range(63)])
    keys_a = projected(0, 0, column_b, *a[1:3])
    b = [column_b, *outer_first(after(column_b, near))]
    a += outer_second(*a)
    values_a = projected(1, 0, keys_a, *a[1:3])
    b += outer_second(*b, values_a)
    keys_b = projected(0, 1, *b[1:3])
    far_near = hop(after(far, keys_b), "core")
    a += outer_third(*a[3:5], keys_b)
    values_b = projected(1, 1, *a[3:5])
    whole = gather_rows([after(normed, values_b), near, far, far_near])
    b += outer_third(*b[3:5], whole)
    total = partial_product(after(whole, *b[3:5]), [(0, [0, 1, 2], a[:3])])
    a += outer_last(*a[5:7], total)
    total = partial_product(
        after(whole, *a[5:7]), [(256, [0, 1, 2], b[:3]), (0, [3, 4], a[3:5])], total
    )
    prev_near = hop(after(prev, total), "core")
    prev = project_prev(prev, prev_near, w_keyval)
    b += outer_last(*b[5:7], total)
    total = partial_product(
        after(whole, *b[5:7]),
        [(256, [3, 4], b[3:5]), (0, [5, 6], a[5:7]), (256, [5, 6], b[5:7])],
        total,
    )
    return attend(
        nbr_lens.T,
        segment_ids.reshape(-1, 128),
        total,
        whole,
        [*a[7:], *b[7:]],
        prev,
        [keys_a, keys_b],
        [values_a, values_b],
    )


def solution(mesh):
    fine = Mesh(mesh.devices.reshape(tuple(SIZES.values())), tuple(SIZES))
    section, seq = ("xh", "core"), ("y", "xl", "z")
    in_specs = (
        P(seq + section, None),
        P(),
        P(seq, section),
        P(None, None, section),
        P(seq, None, None),
        P(),
        P(),
    )
    out_specs = P(seq, section)
    return jax.shard_map(local, mesh=fine, in_specs=in_specs, out_specs=out_specs, check_vma=False)
```

```python
import functools

import jax
import jax.numpy as jnp
from jax import lax
from jax.experimental import pallas as pl
from jax.experimental.pallas import tpu as pltpu
from jax.sharding import Mesh, PartitionSpec as P

HEAD_DIM = 128
SPAN = 64
NBR_LEN = 128
SIZES = {"xh": 2, "core": 2, "y": 4, "xl": 2, "z": 8}
PLANE = ("core", "y", "xl", "z")
VMEM = pl.BlockSpec(memory_space=pltpu.VMEM)
SMEM = pl.BlockSpec(memory_space=pltpu.SMEM)
MIB = 1 << 20


def params(mib):
    return pltpu.CompilerParams(vmem_limit_bytes=mib * MIB)


def cost(flops, moved, exps=0):
    return pl.CostEstimate(flops=flops, bytes_accessed=moved, transcendentals=exps)


def moved(move, y, xl, z):
    by, how = move
    if how == "z":
        return y, xl, (z + by) % 8
    return (y + by) % 4, xl ^ how, z


def send(x, first, second):
    pairs = []
    for core, move in enumerate((first, second)):
        for y in range(4):
            for xl in range(2):
                for z in range(8):
                    y2, xl2, z2 = moved(move, y, xl, z)
                    pairs.append(
                        (((core * 4 + y) * 2 + xl) * 8 + z, ((core * 4 + y2) * 2 + xl2) * 8 + z2)
                    )
    return lax.ppermute(x, PLANE, pairs)


def hop(x, axis):
    return lax.ppermute(x, axis, [(0, 1), (1, 0)])


OUTER_Z = (0, -1, 1, -2, 2, -3, 3, -4)
OUTER_W = ((0, 0), (-1, 0), (1, 0), (0, 1), (2, 0), (-1, 1), (1, 1), (2, 1))


def outer_slots(which):
    y, xl, z = lax.axis_index("y"), lax.axis_index("xl"), lax.axis_index("z")
    out = []
    for i in which:
        dz, (dy, flip) = OUTER_Z[i], OUTER_W[i]
        other = jnp.where(xl == flip, 0, 1)
        along_w = lax.rem(y + dy + 4, 4) * 2 + other
        out.append(jnp.where(lax.axis_index("core") == 1, lax.rem(z + dz + 8, 8), along_w))
    return out


def stack_kernel(orders, *refs):
    out, rows = refs[-1], refs[0].shape[0]
    for core, order in enumerate(orders):

        @pl.when(lax.axis_index("core") == core)
        def _(order=order):
            for i, which in enumerate(order):
                out[i * rows : (i + 1) * rows, :] = refs[which][...]


def stacked(parts, orders):
    rows, columns = parts[0].shape
    return pl.pallas_call(
        functools.partial(stack_kernel, orders),
        out_shape=jax.ShapeDtypeStruct((4 * rows, columns), parts[0].dtype),
        in_specs=[VMEM] * len(parts),
        out_specs=VMEM,
        compiler_params=params(8),
        cost_estimate=cost(0, 16 * rows * columns),
        name="stack",
    )(*parts)


def norm_kernel(hidden_ref, gain_ref, out_ref):
    values = hidden_ref[...].astype(jnp.float32)
    factor = lax.rsqrt(jnp.mean(values * values, axis=-1, keepdims=True) + 1e-06)
    out_ref[...] = (values * factor * gain_ref[...]).astype(jnp.bfloat16)


def normalize(hidden, gain):
    rows, width = hidden.shape
    return pl.pallas_call(
        norm_kernel,
        out_shape=jax.ShapeDtypeStruct((rows, width), jnp.bfloat16),
        in_specs=[VMEM, VMEM],
        out_specs=VMEM,
        compiler_params=params(8),
        cost_estimate=cost(6 * rows * width, 4 * rows * width),
        name="norm",
    )(hidden, gain)


def rows_kernel(own_ref, near_ref, far_ref, far_near_ref, out):
    xh, core = lax.axis_index("xh"), lax.axis_index("core")
    y, xl, z = lax.axis_index("y"), lax.axis_index("xl"), lax.axis_index("z")
    slots = [xh * 2 + core, xh * 2 + 1 - core, 2 - 2 * xh + core, 3 - 2 * xh - core]
    refs = [own_ref, near_ref, far_ref, far_near_ref]
    rows = own_ref.shape[0]
    part = 32
    start = lax.rem(z + 6, 8) // 2

    for slot, ref in zip(slots, refs, strict=True):

        def one(i, _, slot=slot, ref=ref):
            here = pl.ds(pl.multiple_of(i * part, part), part)
            at = pl.ds(pl.multiple_of(slot * rows + i * part, part), part)

            def tile(lane):
                return ref[here, pl.ds(pl.multiple_of(lane, 128), 128)]

            @pl.when((core == 0) & (lax.rem(z, 2) == 0))
            def _():
                for w in range(8):
                    for k in range(4):
                        to = w * 512 + k * 128
                        out[at, to : to + 128] = tile(w * 512 + lax.rem(start + k, 4) * 128)

            @pl.when((core == 0) & (lax.rem(z, 2) == 1))
            def _():
                for w in range(8):
                    for k in range(4):
                        one = tile(w * 512 + lax.rem(start + k, 4) * 128)[:, 64:]
                        two = tile(w * 512 + lax.rem(start + k + 1, 4) * 128)[:, :64]
                        to = w * 512 + k * 128
                        out[at, to : to + 128] = jnp.concatenate([one, two], axis=1)

            @pl.when(core == 1)
            def _():
                for k in range(4):
                    side = xl if k < 2 else 1 - xl
                    base = [(lax.rem(y + 2 * (k % 2) + j, 4) * 2 + side) * 512 for j in range(2)]
                    for z_at in range(8):
                        half = slice(64 * (z_at % 2), 64 * (z_at % 2) + 64)
                        one, two = [tile(b + z_at // 2 * 128)[:, half] for b in base]
                        to = z_at * 512 + k * 128
                        out[at, to : to + 128] = jnp.concatenate([one, two], axis=1)

        lax.fori_loop(0, rows // part, one, None)


def gather_rows(parts):
    rows, width = parts[0].shape
    return pl.pallas_call(
        rows_kernel,
        out_shape=jax.ShapeDtypeStruct((4 * rows, width), parts[0].dtype),
        in_specs=[VMEM] * 4,
        out_specs=VMEM,
        compiler_params=params(16),
        cost_estimate=cost(0, 16 * rows * width),
        name="rows",
    )(*parts)


def project_kernel(states_ref, w_ref, out_ref):
    for i in range(out_ref.shape[0]):
        out_ref[i] = jnp.dot(
            states_ref[i], w_ref[0], preferred_element_type=jnp.float32
        ).astype(jnp.bfloat16)


def project(states, w, which, half):
    spans, keys, depth = states.shape
    columns = w.shape[2] // 2
    whole = lambda i: (0, 0, 0)
    return pl.pallas_call(
        project_kernel,
        grid=(1,),
        out_shape=jax.ShapeDtypeStruct((spans, keys, columns), jnp.bfloat16),
        in_specs=[
            pl.BlockSpec(states.shape, whole, pipeline_mode=pl.Buffered(1)),
            pl.BlockSpec((1, depth, columns), lambda i: (which, 0, half), pipeline_mode=pl.Buffered(1)),
        ],
        out_specs=pl.BlockSpec((spans, keys, columns), whole, pipeline_mode=pl.Buffered(1)),
        compiler_params=params(16),
        cost_estimate=cost(2 * spans * keys * depth * columns, 6 * MIB),
        name="project",
    )(states, w)


def project_prev_kernel(mine_ref, other_ref, w_ref, out_ref):
    core, rows = lax.axis_index("core"), mine_ref.shape[0]
    for which in range(2):
        for slot, ref in ((core, mine_ref), (1 - core, other_ref)):
            out_ref[which, pl.ds(pl.multiple_of(slot * rows, rows), rows), :] = jnp.dot(
                ref[...], w_ref[which], preferred_element_type=jnp.float32
            ).astype(jnp.bfloat16)


def project_prev(mine, other, w):
    rows, depth = mine.shape
    columns = w.shape[2]
    return pl.pallas_call(
        project_prev_kernel,
        out_shape=jax.ShapeDtypeStruct((2, 2 * rows, columns), jnp.bfloat16),
        in_specs=[VMEM] * 3,
        out_specs=VMEM,
        compiler_params=params(12),
        cost_estimate=cost(8 * rows * depth * columns, 6 * MIB),
        name="project_prev",
    )(mine, other, w)


def products(n_ref, refs, places):
    total = None
    for ref, place in zip(refs, places, strict=True):
        lanes = pl.ds(pl.multiple_of(place, 128), ref.shape[0])
        term = jnp.dot(n_ref[:, lanes], ref[...], preferred_element_type=jnp.float32)
        total = term if total is None else total + term
    return total


def partial_product(n, terms, before=None):
    pieces = [piece for _, _, some in terms for piece in some]
    rows, columns = n.shape[0], pieces[0].shape[1]
    depth = sum(p.shape[0] for p in pieces)
    extra = [] if before is None else [before]

    def body(n_ref, *refs):
        places = [slot * 512 + start for start, which, _ in terms for slot in outer_slots(which)]
        total = products(n_ref, refs[: len(pieces)], places)
        if extra:
            total = total + refs[len(pieces)][...]
        refs[-1][...] = total

    return pl.pallas_call(
        body,
        out_shape=jax.ShapeDtypeStruct((rows, columns), jnp.float32),
        in_specs=[VMEM] * (1 + len(pieces) + len(extra)),
        out_specs=VMEM,
        compiler_params=params(20),
        cost_estimate=cost(2 * rows * depth * columns, 2 * depth * (rows + columns)),
        name="partial",
    )(n, *pieces, *extra)


def attend(lens, segments, total, n, pieces, prev, keys, values):
    rows, columns = total.shape
    blocks = keys[0].shape[0] + 1
    heads = columns // HEAD_DIM // 2
    half = columns // 2

    def body(lens_ref, seg_ref, total_ref, n_ref, *refs):
        piece_refs, prev_ref, k_refs, v_refs = refs[:3], refs[3], refs[4:6], refs[6:8]
        out_ref, q_scr, c_scr, s_scr, w_scr = refs[8:]
        seq = (lax.axis_index("y") * 2 + lax.axis_index("xl")) * 8 + lax.axis_index("z")
        (slot,) = outer_slots([7])
        places = [slot * 512 + i for i in (0, 256, 384)]
        acc = total_ref[...] + products(n_ref, piece_refs, places)
        acc = acc * HEAD_DIM ** (-0.5)
        acc = jnp.concatenate([acc, jnp.zeros((SPAN, columns), jnp.float32)], axis=0)
        q_scr[...] = pltpu.roll(acc, 1, 0).astype(jnp.bfloat16)
        lane = lax.broadcasted_iota(jnp.int32, (1, 128), 1)
        wide = lax.broadcasted_iota(jnp.int32, (1, 2 * NBR_LEN), 1)
        row = lax.broadcasted_iota(jnp.int32, (SPAN, HEAD_DIM), 0)
        usable, live = [], []
        for b in range(blocks):
            span = jnp.maximum(seq * (blocks - 1) + b - 1, 0)
            usable.append(
                wide < jnp.where(wide < NBR_LEN, lens_ref[0, span], lens_ref[1, span] + NBR_LEN)
            )
            line = seg_ref[pl.ds(span // 2, 1), :]
            if b % 2:
                same = (line == line[:, 63:64]) & (lane >= 63) & (lane < 127)
                count = jnp.sum(same.astype(jnp.int32), axis=1, keepdims=True)
            else:
                after = seg_ref[pl.ds(jnp.minimum(span // 2 + 1, seg_ref.shape[0] - 1), 1), :]
                same = (after == line[:, 127:128]) & (lane < 63)
                count = jnp.sum(same.astype(jnp.int32), axis=1, keepdims=True) + 1
            if b == 0:
                count = jnp.where(seq == 0, 0, count)
            live.append(row < count)
        for part in range(2):
            for h in range(heads):
                at = slice(h * HEAD_DIM, (h + 1) * HEAD_DIM)
                to = slice(part * half + h * HEAD_DIM, part * half + (h + 1) * HEAD_DIM)
                for b in range(blocks):
                    scores = lax.dot_general(
                        q_scr[b * SPAN : (b + 1) * SPAN, to],
                        k_refs[part][b - 1, :, at] if b else prev_ref[0, :, to],
                        (((1,), (1,)), ((), ())),
                        preferred_element_type=jnp.float32,
                    )
                    s_scr[h, b * SPAN : (b + 1) * SPAN, :] = jnp.where(usable[b], scores, jnp.float32(-1e30))
            for h in range(heads):
                for c in range(blocks // 3):
                    r = slice(c * 3 * SPAN, (c + 1) * 3 * SPAN)
                    scores = s_scr[h, r, :]
                    weights = jnp.exp(scores - jnp.max(scores, axis=-1, keepdims=True))
                    scale = 1.0 / jnp.sum(weights, axis=-1, keepdims=True)
                    w_scr[h, r, :] = (weights * scale).astype(jnp.bfloat16)
            for h in range(heads):
                at = slice(h * HEAD_DIM, (h + 1) * HEAD_DIM)
                to = slice(part * half + h * HEAD_DIM, part * half + (h + 1) * HEAD_DIM)
                for b in range(blocks):
                    mixed = jnp.dot(
                        w_scr[h, b * SPAN : (b + 1) * SPAN, :],
                        v_refs[part][b - 1, :, at] if b else prev_ref[1, :, to],
                        preferred_element_type=jnp.float32,
                    )
                    c_scr[b * SPAN : (b + 1) * SPAN, to] = jnp.where(live[b], mixed, 0.0)
        moved = pltpu.roll(c_scr[...], blocks * SPAN - 1, 0)
        out_ref[...] = moved[:rows].astype(jnp.bfloat16)

    return pl.pallas_call(
        body,
        out_shape=jax.ShapeDtypeStruct((rows, columns), jnp.bfloat16),
        in_specs=[SMEM] + [VMEM] * 11,
        out_specs=VMEM,
        scratch_shapes=[
            pltpu.VMEM((blocks * SPAN, columns), jnp.bfloat16),
            pltpu.VMEM((blocks * SPAN, columns), jnp.float32),
            pltpu.VMEM((heads, blocks * SPAN, 2 * NBR_LEN), jnp.float32),
            pltpu.VMEM((heads, blocks * SPAN, 2 * NBR_LEN), jnp.bfloat16),
        ],
        compiler_params=params(28),
        cost_estimate=cost(6 * MIB * 1000, 16 * MIB),
        name="attend",
    )(lens, segments, total, n, *pieces, prev, *keys, *values)


def after(value, *others):
    return lax.optimization_barrier((value, *others))[0]


def local(hidden, norm_gain, w_query, w_keyval, nbr_states, nbr_lens, segment_ids):
    core = lax.axis_index("core")

    def pick(zero, one):
        return jnp.where(core == 0, zero, one)

    def outer_first(column):
        return [send(column, (1, 0), (1, "z")), send(column, (-1, 0), (-1, "z"))]

    def outer_second(column, one, two, *first):
        one, two = after(one, *first), after(two, *first)
        return [send(pick(column, one), (0, 1), (1, "z")), send(two, (-1, 0), (-1, "z"))]

    def outer_third(three, four, *first):
        three, four = after(three, *first), after(four, *first)
        return [send(three, (1, 0), (1, "z")), send(pick(three, four), (-1, 0), (-1, "z"))]

    def outer_last(five, six, *first):
        r = five.shape[0] // 2
        five, six = after(five, *first), after(six, *first)
        return [send(five[:r], (1, 0), (1, "z")), send(six[r:], (-1, 0), (-1, "z"))]

    def projected(which, part, *first):
        return project(after(nbr_states, *first), w_keyval, which, part)

    round_one = [
        send(w_query, (1, "z"), (0, 1)),
        send(w_query, (-1, "z"), (1, 0)),
        send(w_query, (2, "z"), (-1, 0)),
        send(w_query, (-2, "z"), (2, 0)),
    ]
    normed = normalize(hidden, norm_gain[None])
    near = hop(normed, "core")
    far = hop(normed, "xh")
    column_a = stacked([w_query, *round_one], ((3, 1, 0, 2), (0, 3, 4, 2)))
    head = after(pick(round_one[3], round_one[0]), normed)
    round_two = [
        send(head, (-1, "z"), (-1, 0)),
        send(head, (-2, "z"), (2, 0)),
        send(pick(round_one[2], round_one[0]), (1, "z"), (1, 0)),
    ]
    column_b = stacked([head, *round_two], ((0, 1, 2, 3), (0, 1, 2, 3)))

    a = [column_a, *outer_first(column_a)]
    half = nbr_states.shape[1] // 2
    prev = lax.dynamic_slice_in_dim(nbr_states[-1], core * half, half, 0)
    prev = lax.ppermute(after(prev, column_a), ("y", "xl", "z"), [(i, i + 1) for i in range(63)])
    keys_a = projected(0, 0, column_a)
    b = [column_b, *outer_first(column_b)]
    a += outer_second(*a, keys_a)
    values_a = projected(1, 0, *a[1:3])
    b += outer_second(*b, values_a, prev)
    prev_near = hop(prev, "core")
    keys_b = projected(0, 1, *b[1:3])
    far_near = hop(after(far, keys_b), "core")
    a += outer_third(*a[3:5], keys_b)
    values_b = projected(1, 1, *a[3:5])
    prev = project_prev(after(prev, values_b), prev_near, w_keyval)
    whole = gather_rows([after(normed, prev), near, far, far_near])
    b += outer_third(*b[3:5], whole)
    total = partial_product(after(whole, *b[3:5]), [(0, [0, 1, 2], a[:3])])
    a.append(send(after(a[5], total), (1, 0), (1, "z")))
    total = partial_product(
        after(whole, *a[5:7]), [(256, [0, 1, 2], b[:3]), (0, [3, 4], a[3:5])], total
    )
    b += outer_last(*b[5:7], total)
    total = partial_product(
        after(whole, *b[5:7]),
        [(256, [3, 4], b[3:5]), (0, [5, 6], a[5:7]), (256, [5, 6], b[5:7])],
        total,
    )
    return attend(
        nbr_lens.T,
        segment_ids.reshape(-1, 128),
        total,
        whole,
        [*a[7:], *b[7:]],
        prev,
        [keys_a, keys_b],
        [values_a, values_b],
    )


def solution(mesh):
    fine = Mesh(mesh.devices.reshape(tuple(SIZES.values())), tuple(SIZES))
    section, seq = ("xh", "core"), ("y", "xl", "z")
    in_specs = (
        P(seq + section, None),
        P(),
        P(seq, section),
        P(None, None, section),
        P(seq, None, None),
        P(),
        P(),
    )
    out_specs = P(seq, section)
    return jax.shard_map(local, mesh=fine, in_specs=in_specs, out_specs=out_specs, check_vma=False)
```

```python
import functools

import jax
import jax.numpy as jnp
from jax import lax
from jax.experimental import pallas as pl
from jax.experimental.pallas import tpu as pltpu
from jax.sharding import Mesh, PartitionSpec as P

HEAD_DIM = 128
SPAN = 64
NBR_LEN = 128
SIZES = {"xh": 2, "core": 2, "y": 4, "xl": 2, "z": 8}
PLANE = ("core", "y", "xl", "z")
VMEM = pl.BlockSpec(memory_space=pltpu.VMEM)
SMEM = pl.BlockSpec(memory_space=pltpu.SMEM)
MIB = 1 << 20


def params(mib):
    return pltpu.CompilerParams(vmem_limit_bytes=mib * MIB)


def cost(flops, moved, exps=0):
    return pl.CostEstimate(flops=flops, bytes_accessed=moved, transcendentals=exps)


def moved(move, y, xl, z):
    by, how = move
    if how == "z":
        return y, xl, (z + by) % 8
    return (y + by) % 4, xl ^ how, z


def send(x, first, second):
    pairs = []
    for core, move in enumerate((first, second)):
        for y in range(4):
            for xl in range(2):
                for z in range(8):
                    y2, xl2, z2 = moved(move, y, xl, z)
                    pairs.append(
                        (((core * 4 + y) * 2 + xl) * 8 + z, ((core * 4 + y2) * 2 + xl2) * 8 + z2)
                    )
    return lax.ppermute(x, PLANE, pairs)


def hop(x, axis):
    return lax.ppermute(x, axis, [(0, 1), (1, 0)])


OUTER_Z = (0, -1, 1, -2, 2, -3, 3, -4)
OUTER_W = ((0, 0), (-1, 0), (1, 0), (0, 1), (2, 0), (-1, 1), (1, 1), (2, 1))


def outer_slots(which):
    y, xl, z = lax.axis_index("y"), lax.axis_index("xl"), lax.axis_index("z")
    out = []
    for i in which:
        dz, (dy, flip) = OUTER_Z[i], OUTER_W[i]
        other = jnp.where(xl == flip, 0, 1)
        along_w = lax.rem(y + dy + 4, 4) * 2 + other
        out.append(jnp.where(lax.axis_index("core") == 1, lax.rem(z + dz + 8, 8), along_w))
    return out


def stack_kernel(orders, *refs):
    out, rows = refs[-1], refs[0].shape[0]
    for core, order in enumerate(orders):

        @pl.when(lax.axis_index("core") == core)
        def _(order=order):
            for i, which in enumerate(order):
                out[i * rows : (i + 1) * rows, :] = refs[which][...]


def stacked(parts, orders):
    rows, columns = parts[0].shape
    return pl.pallas_call(
        functools.partial(stack_kernel, orders),
        out_shape=jax.ShapeDtypeStruct((4 * rows, columns), parts[0].dtype),
        in_specs=[VMEM] * len(parts),
        out_specs=VMEM,
        compiler_params=params(8),
        cost_estimate=cost(0, 16 * rows * columns),
        name="stack",
    )(*parts)


def norm_kernel(hidden_ref, gain_ref, out_ref):
    values = hidden_ref[...].astype(jnp.float32)
    factor = lax.rsqrt(jnp.mean(values * values, axis=-1, keepdims=True) + 1e-06)
    out_ref[...] = (values * factor * gain_ref[...]).astype(jnp.bfloat16)


def normalize(hidden, gain):
    rows, width = hidden.shape
    return pl.pallas_call(
        norm_kernel,
        out_shape=jax.ShapeDtypeStruct((rows, width), jnp.bfloat16),
        in_specs=[VMEM, VMEM],
        out_specs=VMEM,
        compiler_params=params(8),
        cost_estimate=cost(6 * rows * width, 4 * rows * width),
        name="norm",
    )(hidden, gain)


def rows_kernel(own_ref, near_ref, far_ref, far_near_ref, out):
    xh, core = lax.axis_index("xh"), lax.axis_index("core")
    y, xl, z = lax.axis_index("y"), lax.axis_index("xl"), lax.axis_index("z")
    slots = [xh * 2 + core, xh * 2 + 1 - core, 2 - 2 * xh + core, 3 - 2 * xh - core]
    refs = [own_ref, near_ref, far_ref, far_near_ref]
    rows = own_ref.shape[0]
    part = 32
    start = lax.rem(z + 6, 8) // 2

    for slot, ref in zip(slots, refs, strict=True):

        def one(i, _, slot=slot, ref=ref):
            here = pl.ds(pl.multiple_of(i * part, part), part)
            at = pl.ds(pl.multiple_of(slot * rows + i * part, part), part)

            def tile(lane):
                return ref[here, pl.ds(pl.multiple_of(lane, 128), 128)]

            @pl.when((core == 0) & (lax.rem(z, 2) == 0))
            def _():
                for w in range(8):
                    for k in range(4):
                        to = w * 512 + k * 128
                        out[at, to : to + 128] = tile(w * 512 + lax.rem(start + k, 4) * 128)

            @pl.when((core == 0) & (lax.rem(z, 2) == 1))
            def _():
                for w in range(8):
                    for k in range(4):
                        one = tile(w * 512 + lax.rem(start + k, 4) * 128)[:, 64:]
                        two = tile(w * 512 + lax.rem(start + k + 1, 4) * 128)[:, :64]
                        to = w * 512 + k * 128
                        out[at, to : to + 128] = jnp.concatenate([one, two], axis=1)

            @pl.when(core == 1)
            def _():
                for k in range(4):
                    side = xl if k < 2 else 1 - xl
                    base = [(lax.rem(y + 2 * (k % 2) + j, 4) * 2 + side) * 512 for j in range(2)]
                    for z_at in range(8):
                        half = slice(64 * (z_at % 2), 64 * (z_at % 2) + 64)
                        one, two = [tile(b + z_at // 2 * 128)[:, half] for b in base]
                        to = z_at * 512 + k * 128
                        out[at, to : to + 128] = jnp.concatenate([one, two], axis=1)

        lax.fori_loop(0, rows // part, one, None)


def gather_rows(parts):
    rows, width = parts[0].shape
    return pl.pallas_call(
        rows_kernel,
        out_shape=jax.ShapeDtypeStruct((4 * rows, width), parts[0].dtype),
        in_specs=[VMEM] * 4,
        out_specs=VMEM,
        compiler_params=params(16),
        cost_estimate=cost(0, 16 * rows * width),
        name="rows",
    )(*parts)


def project_kernel(states_ref, w_ref, out_ref):
    for i in range(out_ref.shape[0]):
        out_ref[i] = jnp.dot(
            states_ref[i], w_ref[0], preferred_element_type=jnp.float32
        ).astype(jnp.bfloat16)


def project(states, w, which, half):
    spans, keys, depth = states.shape
    columns = w.shape[2] // 2
    whole = lambda i: (0, 0, 0)
    return pl.pallas_call(
        project_kernel,
        grid=(1,),
        out_shape=jax.ShapeDtypeStruct((spans, keys, columns), jnp.bfloat16),
        in_specs=[
            pl.BlockSpec(states.shape, whole, pipeline_mode=pl.Buffered(1)),
            pl.BlockSpec((1, depth, columns), lambda i: (which, 0, half), pipeline_mode=pl.Buffered(1)),
        ],
        out_specs=pl.BlockSpec((spans, keys, columns), whole, pipeline_mode=pl.Buffered(1)),
        compiler_params=params(16),
        cost_estimate=cost(2 * spans * keys * depth * columns, 6 * MIB),
        name="project",
    )(states, w)


def project_prev_kernel(mine_ref, other_ref, w_ref, out_ref):
    core, rows = lax.axis_index("core"), mine_ref.shape[0]
    for which in range(2):
        for slot, ref in ((core, mine_ref), (1 - core, other_ref)):
            out_ref[which, pl.ds(pl.multiple_of(slot * rows, rows), rows), :] = jnp.dot(
                ref[...], w_ref[which], preferred_element_type=jnp.float32
            ).astype(jnp.bfloat16)


def project_prev(mine, other, w):
    rows, depth = mine.shape
    columns = w.shape[2]
    return pl.pallas_call(
        project_prev_kernel,
        out_shape=jax.ShapeDtypeStruct((2, 2 * rows, columns), jnp.bfloat16),
        in_specs=[VMEM] * 3,
        out_specs=VMEM,
        compiler_params=params(12),
        cost_estimate=cost(8 * rows * depth * columns, 6 * MIB),
        name="project_prev",
    )(mine, other, w)


def products(n_ref, refs, places):
    total = None
    for ref, place in zip(refs, places, strict=True):
        lanes = pl.ds(pl.multiple_of(place, 128), ref.shape[0])
        term = jnp.dot(n_ref[:, lanes], ref[...], preferred_element_type=jnp.float32)
        total = term if total is None else total + term
    return total


def partial_product(n, terms, before=None):
    pieces = [piece for _, _, some in terms for piece in some]
    rows, columns = n.shape[0], pieces[0].shape[1]
    depth = sum(p.shape[0] for p in pieces)
    extra = [] if before is None else [before]

    def body(n_ref, *refs):
        places = [slot * 512 + start for start, which, _ in terms for slot in outer_slots(which)]
        total = products(n_ref, refs[: len(pieces)], places)
        if extra:
            total = total + refs[len(pieces)][...]
        refs[-1][...] = total

    return pl.pallas_call(
        body,
        out_shape=jax.ShapeDtypeStruct((rows, columns), jnp.float32),
        in_specs=[VMEM] * (1 + len(pieces) + len(extra)),
        out_specs=VMEM,
        compiler_params=params(20),
        cost_estimate=cost(2 * rows * depth * columns, 2 * depth * (rows + columns)),
        name="partial",
    )(n, *pieces, *extra)


def attend(lens, segments, total, n, pieces, prev, keys, values):
    rows, columns = total.shape
    blocks = keys[0].shape[0] + 1
    heads = columns // HEAD_DIM // 2
    half = columns // 2

    def body(lens_ref, seg_ref, total_ref, n_ref, *refs):
        piece_refs, prev_ref, k_refs, v_refs = refs[:3], refs[3], refs[4:6], refs[6:8]
        out_ref, q_scr, c_scr, s_scr, w_scr = refs[8:]
        seq = (lax.axis_index("y") * 2 + lax.axis_index("xl")) * 8 + lax.axis_index("z")
        (slot,) = outer_slots([7])
        places = [slot * 512 + i for i in (0, 256, 384)]
        acc = total_ref[...] + products(n_ref, piece_refs, places)
        acc = acc * HEAD_DIM ** (-0.5)
        acc = jnp.concatenate([acc, jnp.zeros((SPAN, columns), jnp.float32)], axis=0)
        q_scr[...] = pltpu.roll(acc, 1, 0).astype(jnp.bfloat16)
        lane = lax.broadcasted_iota(jnp.int32, (1, 128), 1)
        wide = lax.broadcasted_iota(jnp.int32, (1, 2 * NBR_LEN), 1)
        row = lax.broadcasted_iota(jnp.int32, (SPAN, HEAD_DIM), 0)
        usable, live = [], []
        for b in range(blocks):
            span = jnp.maximum(seq * (blocks - 1) + b - 1, 0)
            usable.append(
                wide < jnp.where(wide < NBR_LEN, lens_ref[0, span], lens_ref[1, span] + NBR_LEN)
            )
            line = seg_ref[pl.ds(span // 2, 1), :]
            if b % 2:
                same = (line == line[:, 63:64]) & (lane >= 63) & (lane < 127)
                count = jnp.sum(same.astype(jnp.int32), axis=1, keepdims=True)
            else:
                after = seg_ref[pl.ds(jnp.minimum(span // 2 + 1, seg_ref.shape[0] - 1), 1), :]
                same = (after == line[:, 127:128]) & (lane < 63)
                count = jnp.sum(same.astype(jnp.int32), axis=1, keepdims=True) + 1
            if b == 0:
                count = jnp.where(seq == 0, 0, count)
            live.append(row < count)
        for part in range(2):
            for h in range(heads):
                at = slice(h * HEAD_DIM, (h + 1) * HEAD_DIM)
                to = slice(part * half + h * HEAD_DIM, part * half + (h + 1) * HEAD_DIM)
                for b in range(blocks):
                    scores = lax.dot_general(
                        q_scr[b * SPAN : (b + 1) * SPAN, to],
                        k_refs[part][b - 1, :, at] if b else prev_ref[0, :, to],
                        (((1,), (1,)), ((), ())),
                        preferred_element_type=jnp.float32,
                    )
                    s_scr[h, b * SPAN : (b + 1) * SPAN, :] = jnp.where(usable[b], scores, jnp.float32(-1e30))
            for h in range(heads):
                for c in range(blocks // 3):
                    r = slice(c * 3 * SPAN, (c + 1) * 3 * SPAN)
                    scores = s_scr[h, r, :]
                    weights = jnp.exp(scores - jnp.max(scores, axis=-1, keepdims=True))
                    scale = 1.0 / jnp.sum(weights, axis=-1, keepdims=True)
                    w_scr[h, r, :] = (weights * scale).astype(jnp.bfloat16)
            for h in range(heads):
                at = slice(h * HEAD_DIM, (h + 1) * HEAD_DIM)
                to = slice(part * half + h * HEAD_DIM, part * half + (h + 1) * HEAD_DIM)
                for b in range(blocks):
                    mixed = jnp.dot(
                        w_scr[h, b * SPAN : (b + 1) * SPAN, :],
                        v_refs[part][b - 1, :, at] if b else prev_ref[1, :, to],
                        preferred_element_type=jnp.float32,
                    )
                    c_scr[b * SPAN : (b + 1) * SPAN, to] = jnp.where(live[b], mixed, 0.0)
        moved = pltpu.roll(c_scr[...], blocks * SPAN - 1, 0)
        out_ref[...] = moved[:rows].astype(jnp.bfloat16)

    return pl.pallas_call(
        body,
        out_shape=jax.ShapeDtypeStruct((rows, columns), jnp.bfloat16),
        in_specs=[SMEM] + [VMEM] * 11,
        out_specs=VMEM,
        scratch_shapes=[
            pltpu.VMEM((blocks * SPAN, columns), jnp.bfloat16),
            pltpu.VMEM((blocks * SPAN, columns), jnp.float32),
            pltpu.VMEM((heads, blocks * SPAN, 2 * NBR_LEN), jnp.float32),
            pltpu.VMEM((heads, blocks * SPAN, 2 * NBR_LEN), jnp.bfloat16),
        ],
        compiler_params=params(28),
        cost_estimate=cost(6 * MIB * 1000, 16 * MIB),
        name="attend",
    )(lens, segments, total, n, *pieces, prev, *keys, *values)


def after(value, *others):
    return lax.optimization_barrier((value, *others))[0]


def local(hidden, norm_gain, w_query, w_keyval, nbr_states, nbr_lens, segment_ids):
    core = lax.axis_index("core")

    def pick(zero, one):
        return jnp.where(core == 0, zero, one)

    def outer_first(column):
        return [send(column, (1, 0), (1, "z")), send(column, (-1, 0), (-1, "z"))]

    def outer_second(column, one, two, *first):
        one, two = after(one, *first), after(two, *first)
        return [send(pick(column, one), (0, 1), (1, "z")), send(two, (-1, 0), (-1, "z"))]

    def outer_third(three, four, *first):
        three, four = after(three, *first), after(four, *first)
        return [send(three, (1, 0), (1, "z")), send(pick(three, four), (-1, 0), (-1, "z"))]

    def outer_last(five, six, *first):
        r = five.shape[0] // 2
        five, six = after(five, *first), after(six, *first)
        return [send(five[:r], (1, 0), (1, "z")), send(six[r:], (-1, 0), (-1, "z"))]

    def projected(which, part, *first):
        return project(after(nbr_states, *first), w_keyval, which, part)

    round_one = [
        send(w_query, (1, "z"), (0, 1)),
        send(w_query, (-1, "z"), (1, 0)),
        send(w_query, (2, "z"), (-1, 0)),
        send(w_query, (-2, "z"), (2, 0)),
    ]
    normed = normalize(hidden, norm_gain[None])
    near = hop(normed, "core")
    far = hop(normed, "xh")
    column_a = stacked([w_query, *round_one], ((3, 1, 0, 2), (0, 3, 4, 2)))
    head = after(pick(round_one[3], round_one[0]), normed)
    round_two = [
        send(head, (-1, "z"), (-1, 0)),
        send(head, (-2, "z"), (2, 0)),
        send(pick(round_one[2], round_one[0]), (1, "z"), (1, 0)),
    ]
    column_b = stacked([head, *round_two], ((0, 1, 2, 3), (0, 1, 2, 3)))

    a = [column_a, *outer_first(column_a)]
    half = nbr_states.shape[1] // 2
    prev = lax.dynamic_slice_in_dim(nbr_states[-1], core * half, half, 0)
    prev = lax.ppermute(after(prev, column_a), ("y", "xl", "z"), [(i, i + 1) for i in range(63)])
    keys_a = projected(0, 0, column_a)
    b = [column_b, *outer_first(column_b)]
    a += outer_second(*a, keys_a)
    values_a = projected(1, 0, *a[1:3])
    b += outer_second(*b, values_a, prev)
    prev_near = hop(prev, "core")
    keys_b = projected(0, 1, *b[1:3])
    far_near = hop(after(far, keys_b), "core")
    a += outer_third(*a[3:5], keys_b)
    values_b = projected(1, 1, *a[3:5])
    prev = project_prev(after(prev, values_b), prev_near, w_keyval)
    whole = gather_rows([after(normed, prev), near, far, far_near])
    b += outer_third(*b[3:5], prev)
    total = partial_product(after(whole, *b[3:5]), [(0, [0, 1, 2], a[:3])])
    a.append(send(after(a[5], total), (1, 0), (1, "z")))
    total = partial_product(
        after(whole, *a[5:7]), [(256, [0, 1, 2], b[:3]), (0, [3, 4], a[3:5])], total
    )
    b += outer_last(*b[5:7], total)
    total = partial_product(
        after(whole, *b[5:7]),
        [(256, [3, 4], b[3:5]), (0, [5, 6], a[5:7]), (256, [5, 6], b[5:7])],
        total,
    )
    return attend(
        nbr_lens.T,
        segment_ids.reshape(-1, 128),
        total,
        whole,
        [*a[7:], *b[7:]],
        prev,
        [keys_a, keys_b],
        [values_a, values_b],
    )


def solution(mesh):
    fine = Mesh(mesh.devices.reshape(tuple(SIZES.values())), tuple(SIZES))
    section, seq = ("xh", "core"), ("y", "xl", "z")
    in_specs = (
        P(seq + section, None),
        P(),
        P(seq, section),
        P(None, None, section),
        P(seq, None, None),
        P(),
        P(),
    )
    out_specs = P(seq, section)
    return jax.shard_map(local, mesh=fine, in_specs=in_specs, out_specs=out_specs, check_vma=False)
```
